32 devices in a mesh: seq: 8 (over z, y), head: 4 (over x, core).
Axes of the slice: x: 2, y: 2, z: 4, core: 2. Of those that a mesh axis runs over, the one named last changes fastest.
Arguments:
- queries: bfloat16 [2048, 8192], P('seq', 'head'), may hold values from -6 to 6
- keys: bfloat16 [2048, 8192], P('seq', 'head'), may hold values from -6 to 6
- values: bfloat16 [2048, 8192], P('seq', 'head'), may hold values from -20 to 20
- out_grad: bfloat16 [2048, 8192], P('seq', 'head'), may hold values from -6 to 6
- norm_gain: bfloat16 [8192], P('head'), may hold values from 0.099609375 to 1.8984375
Outputs:
- query_grad: bfloat16 [2048, 8192], P('seq', 'head')
- key_grad: bfloat16 [2048, 8192], P('seq', 'head')
- value_grad: bfloat16 [2048, 8192], P('seq', 'head')
The draws below stay inside these ranges and needn't reach their ends.
All inputs are finite; a program needn't handle non-finite values.
Results may differ from the reference program's by a relative error of at most 0.0058.
Values sent between devices are 32-bit elements; how exact they have to be, the bound alone decides.
No kernel may reach another device: no remote copies, remote signals or barrier semaphores. Data moves between devices by JAX's collectives and lax.ppermute only.
A program may use at most 192 MiB of HBM per device.

```python
import jax
import jax.numpy as jnp
from jax import lax

HEADS = 64
DH = 128
GROUP = 256
SEQ = 2048


def draw_values(key, part):
    width = HEADS * DH
    head_of = jnp.arange(width) // DH
    rising = 3.0 ** (0.5 * head_of.astype(jnp.float32) / (HEADS - 1))
    sample = jnp.clip(jax.random.normal(jax.random.fold_in(key, 4), (SEQ, width), jnp.float32), -4.0, 4.0)
    result = sample * rising[None, :]
    return result.astype(jnp.bfloat16)


def levels(key, dims, cuts, smallest, largest):
    loudness = 1.0
    for position, blocks in cuts:
        steps = jax.random.uniform(jax.random.fold_in(jax.random.fold_in(key, 6), position), (blocks,), jnp.float32, smallest / len(cuts), largest / len(cuts))
        loudness = loudness * jnp.repeat(jnp.exp(steps), dims[position] // blocks).reshape((-1,) + (1,) * (len(dims) - 1 - position))
    return loudness


def normal_values(key, shape, scale, reach, shards=(), held_as=jnp.bfloat16):
    values = jax.random.normal(key, shape, jnp.float32) * scale
    if len(shards) > 0:
        values = levels(key, shape, shards, -0.22, 0.18) * values
    return jnp.clip(values, min=-reach, max=reach).astype(held_as)


def setup_inputs(seed: int = 0) -> dict:
    streams_of = jax.random.split(jax.random.key(seed), 6)
    return {
        "queries": normal_values(streams_of[0], (SEQ, HEADS * DH), 1.0, 6.0, ((0, 8), (1, 4))),
        "keys": normal_values(streams_of[1], (SEQ, HEADS * DH), 1.0, 6.0, ((0, 8), (1, 4))),
        "values": draw_values(jax.random.fold_in(streams_of[5], 71), 0),
        "out_grad": normal_values(streams_of[3], (SEQ, HEADS * DH), 1.0, 6.0, ((0, 8), (1, 4))),
        "norm_gain": jnp.clip(1.0 + 0.18 * jax.random.normal(streams_of[4], (HEADS * DH,), jnp.float32), 0.099609375, 1.8984375).astype(jnp.bfloat16),
    }


def round_bf(array):
    return lax.optimization_barrier(array.astype(jnp.bfloat16)).astype(jnp.float32)

def causal_mask(count):
    rows = lax.broadcasted_iota(jnp.int32, (count, count), 0)
    cols = lax.broadcasted_iota(jnp.int32, (count, count), 1)
    return (rows >= cols).astype(jnp.float32)

def reference(queries, keys, values, out_grad, norm_gain):
    blocks = SEQ // GROUP
    features = HEADS * DH
    highest = lax.Precision.HIGHEST
    masking = causal_mask(GROUP)
    gain = norm_gain.astype(jnp.float32)

    def split(array):
        return array.reshape(blocks, GROUP, HEADS, DH)
    query_b, key_b, value_b = (split(queries), split(keys), split(values))
    grad_rows = out_grad.reshape(blocks, GROUP, features)

    def forward(state, inputs):
        query_c, key_c, value_c, grad_c = inputs
        query_f = query_c.astype(jnp.float32)
        key_f = key_c.astype(jnp.float32)
        value_f = value_c.astype(jnp.float32)
        state_b = round_bf(state)
        scores = jnp.einsum('chd,khd->hck', query_f, key_f, precision=highest)
        masked = round_bf(scores * masking[None])
        attn = jnp.einsum('hck,khd->chd', masked, value_f, precision=highest)
        attn = attn + jnp.einsum('chd,hde->che', query_f, state_b, precision=highest)
        attn = attn.reshape(GROUP, features)
        scaled = gain[None, :] * grad_c.astype(jnp.float32)
        inverse = lax.rsqrt(lax.optimization_barrier(jnp.sum(attn * attn, axis=1, keepdims=True)) / features + 1e-05)
        cross = lax.optimization_barrier(jnp.sum(scaled * attn, axis=1, keepdims=True)) / features
        delta = (inverse * scaled - attn * inverse * inverse * inverse * cross).astype(jnp.bfloat16)
        delta_f = delta.astype(jnp.float32).reshape(GROUP, HEADS, DH)
        dscore = round_bf(jnp.einsum('che,khe->hck', delta_f, value_f, precision=highest) * masking[None])
        query_grad = jnp.einsum('hck,khd->chd', dscore, key_f, precision=highest)
        query_grad = query_grad + jnp.einsum('che,hde->chd', delta_f, state_b, precision=highest)
        new_state = state + jnp.einsum('chd,che->hde', key_f, value_f, precision=highest)
        return (new_state, (query_grad.astype(jnp.bfloat16), delta.reshape(GROUP, HEADS, DH)))
    start = jnp.zeros((HEADS, DH, DH), jnp.float32)
    unused, (query_grad, deltas) = lax.scan(forward, start, (query_b, key_b, value_b, grad_rows))

    def backward(later, inputs):
        query_c, key_c, value_c, delta_c = inputs
        query_f = query_c.astype(jnp.float32)
        key_f = key_c.astype(jnp.float32)
        value_f = value_c.astype(jnp.float32)
        delta_f = delta_c.astype(jnp.float32)
        later_b = round_bf(later)
        scores = jnp.einsum('chd,khd->hck', query_f, key_f, precision=highest)
        masked = round_bf(scores * masking[None])
        dscore = round_bf(jnp.einsum('che,khe->hck', delta_f, value_f, precision=highest) * masking[None])
        key_grad = jnp.einsum('hck,chd->khd', dscore, query_f, precision=highest)
        key_grad = key_grad + jnp.einsum('che,hde->chd', value_f, later_b, precision=highest)
        value_grad = jnp.einsum('hck,che->khe', masked, delta_f, precision=highest)
        value_grad = value_grad + jnp.einsum('chd,hde->che', key_f, later_b, precision=highest)
        new_later = later + jnp.einsum('chd,che->hde', query_f, delta_f, precision=highest)
        return (new_later, (key_grad.astype(jnp.bfloat16), value_grad.astype(jnp.bfloat16)))
    unused_two, (key_grad, value_grad) = lax.scan(backward, start, (query_b, key_b, value_b, deltas), reverse=True)
    return (query_grad.reshape(SEQ, features), key_grad.reshape(SEQ, features), value_grad.reshape(SEQ, features))
```

```python
import functools

import jax
import jax.numpy as jnp
from jax import lax
from jax.experimental import pallas as pl
from jax.experimental.pallas import tpu as pltpu
from jax.sharding import PartitionSpec as P

DH = 128
GROUP = 256
CHUNKS = 4
EPS = 1e-05
F32 = jnp.float32
BF16 = jnp.bfloat16


def dot(a, b, ca, cb):
    return lax.dot_general(a, b, (((ca,), (cb,)), ((), ())), preferred_element_type=F32)


def head(ref, j):
    return ref[:, j * DH:(j + 1) * DH]


def causal():
    rows = lax.broadcasted_iota(jnp.int32, (GROUP, GROUP), 0)
    cols = lax.broadcasted_iota(jnp.int32, (GROUP, GROUP), 1)
    return rows >= cols


def masked(scores, mask):
    return jnp.where(mask, scores, 0.0).astype(BF16)


def call(body, place, ins, outs, grid=(1,), aliases=None, flops=0):
    size = sum(a.size * a.dtype.itemsize // 2 for a, _, _ in ins)
    return pl.pallas_call(
        body,
        grid_spec=pltpu.PrefetchScalarGridSpec(
            num_scalar_prefetch=1,
            grid=grid,
            in_specs=[pl.BlockSpec(b, m) for _, b, m in ins],
            out_specs=[pl.BlockSpec(b, m) for _, _, b, m in outs],
        ),
        out_shape=[jax.ShapeDtypeStruct(s, d) for s, d, _, _ in outs],
        input_output_aliases=aliases or {},
        compiler_params=pltpu.CompilerParams(vmem_limit_bytes=24 * 1024 * 1024),
        cost_estimate=pl.CostEstimate(flops=flops, bytes_accessed=size, transcendentals=0),
    )(place, *[a for a, _, _ in ins])


def states_body(per, place, a, b, *outs):
    for c, out in enumerate(outs):
        for j in range(per):
            h = c * per + j
            out[j] = dot(head(a, h), head(b, h), 0, 0)


def local_body(heads, place, q, k, v, scores, attn):
    mask = causal()
    for j in range(heads):
        s = masked(dot(head(q, j), head(k, j), 1, 1), mask)
        scores[j] = s
        attn[:, j * DH:(j + 1) * DH] = dot(s, head(v, j), 1, 0)


def attn_body(per, first, last, place, al_k, al_o, q_k, q_o, g_k, g_o, n_k, n_o, e, r, other, *refs):
    if not first:
        sq_in, cr_in, *refs = refs
    at_k, at_o, sb_k, sb_o, *stats = refs
    second = place[0] == 1
    square = jnp.zeros((GROUP, DH), F32) if first else sq_in[...]
    cross = jnp.zeros((GROUP, DH), F32) if first else cr_in[...]
    for j in range(per):
        kept = jnp.where(second, e[j] + r[j], e[j]).astype(BF16)
        sb_k[j] = kept
        sb_o[j] = other[j].astype(BF16)
        for al, q, g, n, sb, at in (
            (al_k, q_k, g_k, n_k, sb_k, at_k),
            (al_o, q_o, g_o, n_o, sb_o, at_o),
        ):
            x = head(al, j) + dot(head(q, j), sb[j], 1, 0)
            at[:, j * DH:(j + 1) * DH] = x
            scaled = head(n, j).astype(F32) * head(g, j).astype(F32)
            square = square + x * x
            cross = cross + scaled * x
    if last:
        stats[0][0:1] = jnp.sum(square.T, axis=0, keepdims=True)
        stats[0][1:2] = jnp.sum(cross.T, axis=0, keepdims=True)
    else:
        stats[0][...] = square
        stats[1][...] = cross


def delta_body(per, chunks, parts, features, place, *refs):
    stats = refs[:parts]
    attn = refs[parts:parts + chunks]
    q, g, n, d = refs[parts + chunks:parts + chunks + 4]
    outs = refs[parts + chunks + 4:]
    total = stats[0][...]
    for s in stats[1:]:
        total = total + s[...]
    inverse = lax.rsqrt(total[0:1] / features + EPS)
    slope = inverse * inverse * inverse * (total[1:2] / features)
    inverse = jnp.broadcast_to(inverse, (DH, GROUP)).T
    slope = jnp.broadcast_to(slope, (DH, GROUP)).T
    for c in range(chunks):
        for j in range(per):
            h = c * per + j
            scaled = head(n, h).astype(F32) * head(g, h).astype(F32)
            x = (inverse * scaled - head(attn[c], j) * slope).astype(BF16)
            d[:, h * DH:(h + 1) * DH] = x
            outs[c][j] = dot(head(q, h), x, 0, 0)


def grads_body(per, aliased, place, *refs):
    (q_k, q_o, k_k, k_o, v_k, v_o, s_k, s_o, d_k, d_o, sb_k, sb_o) = refs[:12]
    qg_k, qg_o, kg_k, kg_o, vg_k, vg_o = refs[12:]
    mask = causal()
    for j in range(per):
        at = slice(j * DH, (j + 1) * DH)
        for q, k, v, s, d, sb, qg, kg, vg in (
            (q_k, k_k, v_k, s_k, d_k, sb_k, qg_k, kg_k, vg_k),
            (q_o, k_o, v_o, s_o, d_o, sb_o, qg_o, kg_o, vg_o),
        ):
            do = head(d, j)
            ds = masked(dot(do, head(v, j), 1, 1), mask)
            qg[:, at] = (dot(ds, head(k, j), 1, 0) + dot(do, sb[j], 1, 1)).astype(BF16)
            kg[:, at] = dot(ds, head(q, j), 0, 0)
            vg[:, at] = dot(s[j], do, 0, 0)


def solution(mesh):
    count = mesh.shape["seq"]
    parts = mesh.shape["head"]
    long = count // 2
    swap = [(i, i ^ 1) for i in range(count)]

    def hop(array, near, far, reverse):
        pairs = []
        for z in range(long):
            to = z + far
            if to < long and near(z):
                for y in range(2):
                    pairs.append((2 * z + y, 2 * to + y))
        if reverse:
            pairs = [(count - 1 - a, count - 1 - b) for a, b in pairs]
        return lax.ppermute(array, "seq", pairs)

    def along(part, reverse):
        if long <= 4:
            carry, send = None, part
            for z in range(long - 1):
                got = hop(send, lambda at: at == z, 1, reverse)
                carry = got if carry is None else carry + got
                send = carry + part
            return jnp.zeros_like(part) if carry is None else carry
        carry = hop(part, lambda at: True, 1, reverse)
        far = 1
        while far < long:
            carry = carry + hop(carry, lambda at: True, far, reverse)
            far *= 2
        return carry

    def scan(kept, sent, leads, reverse):
        out = []
        for a, b in zip(kept, sent):
            r = lax.ppermute(b, "seq", swap)
            e = along(a + r, reverse)
            other = lax.ppermute(jnp.where(leads, e + a, e), "seq", swap)
            out.append((e, r, other))
        return out

    def shards(queries, keys, values, out_grad, norm_gain):
        tokens, width = queries.shape
        heads = width // DH
        half = heads // 2
        per = half // CHUNKS
        wide = half * DH
        narrow = per * DH
        y = lax.axis_index("seq") % 2
        place = y.astype(jnp.int32).reshape(1)
        turned = 1 - place
        gain = norm_gain.reshape(1, width)
        mac = 2 * GROUP * DH

        kept_half = lambda i, s: (0, s[0])
        sent_half = lambda i, s: (0, 1 - s[0])
        whole2 = lambda i, s: (0, 0)
        whole3 = lambda i, s: (0, 0, 0)

        def at_k(c):
            return lambda i, s: (0, s[0] * CHUNKS + c)

        def at_o(c):
            return lambda i, s: (0, (1 - s[0]) * CHUNKS + c)

        def at_k3(c):
            return lambda i, s: (s[0] * CHUNKS + c, 0, 0)

        def at_o3(c):
            return lambda i, s: ((1 - s[0]) * CHUNKS + c, 0, 0)

        def states(a, b, index):
            return call(
                functools.partial(states_body, per), place,
                [(a, (tokens, wide), index), (b, (tokens, wide), index)],
                [((per, DH, DH), F32, (per, DH, DH), whole3)] * CHUNKS,
                flops=half * mac * DH,
            )

        sent = states(keys, values, sent_half)
        kept = states(keys, values, kept_half)

        group = 4
        scores, attn_local = call(
            functools.partial(local_body, group), place,
            [(a, (tokens, group * DH), lambda i, s: (0, i)) for a in (queries, keys, values)],
            [
                ((heads, GROUP, GROUP), BF16, (group, GROUP, GROUP), lambda i, s: (i, 0, 0)),
                ((tokens, width), F32, (tokens, group * DH), lambda i, s: (0, i)),
            ],
            grid=(heads // group,), flops=2 * heads * mac * GROUP,
        )

        before = scan(kept, sent, y == 0, False)

        block = (tokens, narrow)
        square = cross = None
        attns, priors = [], []
        for c in range(CHUNKS):
            e, r, other = before[c]
            first, last = c == 0, c == CHUNKS - 1
            ins = []
            for a in (attn_local, queries, out_grad):
                ins += [(a, block, at_k(c)), (a, block, at_o(c))]
            ins += [(gain, (1, narrow), at_k(c)), (gain, (1, narrow), at_o(c))]
            ins += [(a, (per, DH, DH), whole3) for a in (e, r, other)]
            if not first:
                ins += [(a, (GROUP, DH), whole2) for a in (square, cross)]
            outs = [(block, F32, block, whole2)] * 2 + [((per, DH, DH), BF16, (per, DH, DH), whole3)] * 2
            if last:
                outs += [((2, GROUP), F32, (2, GROUP), whole2)]
            else:
                outs += [((GROUP, DH), F32, (GROUP, DH), whole2)] * 2
            a_k, a_o, s_k, s_o, *stats = call(
                functools.partial(attn_body, per, first, last), place, ins, outs, flops=2 * per * mac * DH)
            attns.append((a_k, a_o))
            priors.append((s_k, s_o))
            if last:
                mine = stats[0]
            else:
                square, cross = stats

        sums = [mine]
        for step in range(1, parts):
            sums.append(lax.ppermute(mine, "head", [(i, (i + step) % parts) for i in range(parts)]))

        def delta(which, index):
            ins = [(a, (2, GROUP), whole2) for a in sums]
            ins += [(attns[c][which], block, whole2) for c in range(CHUNKS)]
            ins += [(queries, (tokens, wide), index), (out_grad, (tokens, wide), index), (gain, (1, wide), index)]
            outs = [((tokens, wide), BF16, (tokens, wide), whole2)]
            outs += [((per, DH, DH), F32, (per, DH, DH), whole3)] * CHUNKS
            d, *g = call(
                functools.partial(delta_body, per, CHUNKS, parts, float(parts * width)), place, ins, outs,
                flops=half * mac * DH)
            return d, g

        d_o, sent = delta(1, sent_half)
        d_k, kept = delta(0, kept_half)
        after = scan(kept, sent, y == 1, True)

        grads = []
        for c in range(CHUNKS):
            ins = []
            for a in (queries, keys, values):
                ins += [(a, block, at_k(c)), (a, block, at_o(c))]
            ins += [(scores, (per, GROUP, GROUP), at_k3(c)), (scores, (per, GROUP, GROUP), at_o3(c))]
            here = lambda i, s, c=c: (0, c)
            ins += [(d_k, block, here), (d_o, block, here)]
            ins += [(a, (per, DH, DH), whole3) for a in priors[c]]
            outs = [(block, BF16, block, whole2)] * 2 + [(block, F32, block, whole2)] * 4
            grads.append(call(
                functools.partial(grads_body, per, c > 0), place, ins, outs,
                flops=2 * per * mac * (4 * GROUP + DH)))

        kg = vg = qg = None
        for c in range(CHUNKS):
            e, r, other = after[c]
            kg, vg, qg = finish(c, per, narrow, tokens, width, place, keys, values, grads[c], e, r, other, kg, vg, qg)
        return qg, kg, vg

    def finish(c, per, narrow, tokens, width, place, keys, values, grads, e, r, other, *done):
        qg_k, qg_o, kl_k, kl_o, vl_k, vl_o = grads
        block = (tokens, narrow)
        mine = lambda i, s: (0, jnp.where(i == 0, s[0], 1 - s[0]) * CHUNKS + c)
        whole2 = lambda i, s: (0, 0)
        whole3 = lambda i, s: (0, 0, 0)
        ins = [(a, block, whole2) for a in (qg_k, qg_o, kl_k, kl_o, vl_k, vl_o)]
        ins += [(a, block, mine) for a in (keys, values)]
        ins += [(a, (per, DH, DH), whole3) for a in (e, r, other)]
        aliases = {}
        if done[0] is not None:
            for n, a in enumerate(done):
                aliases[len(ins) + 1] = n
                ins.append((a, (8, 128), whole2))
        outs = [((tokens, width), BF16, block, mine)] * 3

        def body(place, qk, qo, kk, ko, vk, vo, k, v, e, r, other, *refs):
            kg, vg, qg = refs[-3:]
            mine = pl.program_id(0) == 0

            def one(q_in, k_in, v_in, state):
                qg[...] = q_in[...]
                for j in range(per):
                    at = slice(j * DH, (j + 1) * DH)
                    later = state(j).astype(BF16)
                    kg[:, at] = (k_in[:, at] + dot(v[:, at], later, 1, 1)).astype(BF16)
                    vg[:, at] = (v_in[:, at] + dot(k[:, at], later, 1, 0)).astype(BF16)

            @pl.when(mine)
            def _():
                one(qk, kk, vk, lambda j: jnp.where(place[0] == 0, e[j] + r[j], e[j]))

            @pl.when(jnp.logical_not(mine))
            def _():
                one(qo, ko, vo, lambda j: other[j])

        return call(body, place, ins, outs, grid=(2,), aliases=aliases, flops=4 * per * 2 * GROUP * DH * DH)

    return jax.shard_map(
        shards,
        mesh=mesh,
        in_specs=(
            P("seq", "head"),
            P("seq", "head"),
            P("seq", "head"),
            P("seq", "head"),
            P("head"),
        ),
        out_specs=(P("seq", "head"), P("seq", "head"), P("seq", "head")),
        check_vma=False,
    )
```

```python
import functools

import jax
import jax.numpy as jnp
from jax import lax
from jax.experimental import pallas as pl
from jax.experimental.pallas import tpu as pltpu
from jax.sharding import PartitionSpec as P

DH = 128
GROUP = 256
CHUNKS = 4
EPS = 1e-05
F32 = jnp.float32
BF16 = jnp.bfloat16


def dot(a, b, ca, cb):
    return lax.dot_general(a, b, (((ca,), (cb,)), ((), ())), preferred_element_type=F32)


def head(ref, j):
    return ref[:, j * DH:(j + 1) * DH]


def causal():
    rows = lax.broadcasted_iota(jnp.int32, (GROUP, GROUP), 0)
    cols = lax.broadcasted_iota(jnp.int32, (GROUP, GROUP), 1)
    return rows >= cols


def masked(scores, mask):
    return jnp.where(mask, scores, 0.0).astype(BF16)


def call(body, place, ins, outs, grid=(1,), aliases=None, flops=0, grant=12):
    size = sum(a.size * a.dtype.itemsize // 2 for a, _, _ in ins)
    return pl.pallas_call(
        body,
        grid_spec=pltpu.PrefetchScalarGridSpec(
            num_scalar_prefetch=1,
            grid=grid,
            in_specs=[pl.BlockSpec(b, m) if b else pl.BlockSpec(memory_space=pl.ANY) for _, b, m in ins],
            out_specs=[pl.BlockSpec(b, m) for _, _, b, m in outs],
        ),
        out_shape=[jax.ShapeDtypeStruct(s, d) for s, d, _, _ in outs],
        input_output_aliases=aliases or {},
        compiler_params=pltpu.CompilerParams(vmem_limit_bytes=grant * 1024 * 1024),
        cost_estimate=pl.CostEstimate(flops=flops, bytes_accessed=size, transcendentals=0),
    )(place, *[a for a, _, _ in ins])


def states_body(per, skip, place, a, b, *outs):
    for c, out in enumerate(outs):
        for j in range(per):
            h = (skip + c) * per + j
            out[j] = dot(head(a, h), head(b, h), 0, 0)


def local_body(per, chunks, heads, place, q, k, v, *refs):
    outs, scores, attn = refs[:chunks], refs[chunks], refs[chunks + 1]
    for turn in range(2):
        @pl.when(pl.program_id(0) == turn)
        def _():
            for j in range(heads):
                h = turn * heads + j
                outs[h // per][h % per] = dot(head(k, j), head(v, j), 0, 0)
    mask = causal()
    for j in range(heads):
        s = masked(dot(head(q, j), head(k, j), 1, 1), mask)
        scores[j] = s
        attn[:, j * DH:(j + 1) * DH] = dot(s, head(v, j), 1, 0)


def step_body(ready, sends, back, older, lately, ties, place, *refs):
    refs = list(refs)
    y, z = place[0], place[1]
    if ready:
        mine = refs.pop(0)[...] + refs.pop(0)[...]
    if sends:
        items = [refs.pop(0)[...] if there else mine for there in older]
        send = items[0]
        for at in range(1, len(items)):
            send = jnp.where(z == at, items[at], send)
    recent = [refs.pop(0)[...] for _ in range(lately)]
    if sends and recent:
        send = send + recent[-1]
    if back:
        kept = refs.pop(0)[...]
        e = recent[0]
        for at in range(1, len(recent)):
            e = jnp.where(z == at + 1, recent[at], e)
    del refs[:ties]
    if ready:
        refs.pop(0)[...] = mine
    if sends:
        refs.pop(0)[...] = send
    if back:
        refs.pop(0)[...] = e
        refs.pop(0)[...] = jnp.where(y == 0, e + kept, e)


def attn_body(per, first, last, place, al_k, al_o, q_k, q_o, g_k, g_o, n_k, n_o, e, r, other, *refs):
    if not first:
        sq_in, cr_in, *refs = refs
    at_k, at_o, sb_k, sb_o, *stats = refs
    second = place[0] == 1
    square = jnp.zeros((GROUP, DH), F32) if first else sq_in[...]
    cross = jnp.zeros((GROUP, DH), F32) if first else cr_in[...]
    for j in range(per):
        kept = jnp.where(second, e[j] + r[j], e[j]).astype(BF16)
        sb_k[j] = kept
        sb_o[j] = other[j].astype(BF16)
        for al, q, g, n, sb, at in (
            (al_k, q_k, g_k, n_k, sb_k, at_k),
            (al_o, q_o, g_o, n_o, sb_o, at_o),
        ):
            x = head(al, j) + dot(head(q, j), sb[j], 1, 0)
            at[:, j * DH:(j + 1) * DH] = x
            scaled = head(n, j).astype(F32) * head(g, j).astype(F32)
            square = square + x * x
            cross = cross + scaled * x
    if last:
        stats[0][0:1] = jnp.sum(square.T, axis=0, keepdims=True)
        stats[0][1:2] = jnp.sum(cross.T, axis=0, keepdims=True)
    else:
        stats[0][...] = square
        stats[1][...] = cross


def delta_body(per, skip, chunks, parts, features, place, *refs):
    stats = refs[:parts]
    attn = refs[parts:parts + chunks]
    q, g, n = refs[parts + chunks:parts + chunks + 3]
    outs = refs[parts + chunks + 3:]
    total = stats[0][...]
    for s in stats[1:]:
        total = total + s[...]
    inverse = lax.rsqrt(total[0:1] / features + EPS)
    slope = inverse * inverse * inverse * (total[1:2] / features)
    inverse = jnp.broadcast_to(inverse, (DH, GROUP)).T
    slope = jnp.broadcast_to(slope, (DH, GROUP)).T
    for c in range(chunks):
        for j in range(per):
            h = (skip + c) * per + j
            scaled = head(n, h).astype(F32) * head(g, h).astype(F32)
            x = (inverse * scaled - head(attn[c], j) * slope).astype(BF16)
            outs[c][:, j * DH:(j + 1) * DH] = x
            outs[chunks + c][j] = dot(head(q, h), x, 0, 0)


def grads_body(per, ties, place, *refs):
    (q_k, q_o, k_k, k_o, v_k, v_o, s_k, s_o, d_k, d_o, sb_k, sb_o) = refs[:12]
    qg_k, qg_o, kg_k, kg_o, vg_k, vg_o = refs[12 + ties:]
    mask = causal()
    for j in range(per):
        at = slice(j * DH, (j + 1) * DH)
        for q, k, v, s, d, sb, qg, kg, vg in (
            (q_k, k_k, v_k, s_k, d_k, sb_k, qg_k, kg_k, vg_k),
            (q_o, k_o, v_o, s_o, d_o, sb_o, qg_o, kg_o, vg_o),
        ):
            do = head(d, j)
            ds = masked(dot(do, head(v, j), 1, 1), mask)
            qg[:, at] = (dot(ds, head(k, j), 1, 0) + dot(do, sb[j], 1, 1)).astype(BF16)
            kg[:, at] = dot(ds, head(q, j), 0, 0)
            vg[:, at] = dot(s[j], do, 0, 0)


def solution(mesh):
    count = mesh.shape["seq"]
    parts = mesh.shape["head"]
    long = count // 2
    swap = [(i, i ^ 1) for i in range(count)]

    def hop(array, near, far, reverse):
        pairs = []
        for z in range(long):
            to = z + far
            if to < long and near(z):
                for y in range(2):
                    pairs.append((2 * z + y, 2 * to + y))
        if reverse:
            pairs = [(count - 1 - a, count - 1 - b) for a, b in pairs]
        return lax.ppermute(array, "seq", pairs)

    def shift(array, far, reverse):
        return hop(array, lambda at: True, far, reverse)

    def doubling(parts, reverse):
        out = []
        for part in parts:
            carry = shift(part, 1, reverse)
            far = 1
            while far < long:
                carry = carry + shift(carry, far, reverse)
                far *= 2
            out.append(carry)
        return out

    def scan(kept, sent, y, z, reverse, beside):
        swapped = [lax.ppermute(b, "seq", swap) for b in sent]
        if long > 4 or long < 2:
            sums = [a + r for a, r in zip(kept, swapped)]
            sums = doubling(sums, reverse) if long > 1 else [jnp.zeros_like(a) for a in sums]
            others = [
                lax.ppermute(jnp.where(y == 0, e + a, e), "seq", swap) for a, e in zip(kept, sums)
            ]
            return list(zip(sums, swapped, others)), [work(None) for work in beside]
        chunks = len(kept)
        shape = kept[0].shape
        where = jnp.stack([y, z]).astype(jnp.int32)
        whole = lambda i, s: (0, 0, 0)
        parts, got, out, done, ties = [], [], [], [], []
        for t in range(chunks + long - 1):
            ready, sends, back = t < chunks, t < chunks + long - 2, t - (long - 1)
            ins, outs = [], 0
            if ready:
                ins += [kept[t], swapped[t]]
                outs += 1
            older = []
            if sends:
                older = [parts[min(max(t - at, 0), chunks - 1)] if (t - at != t or not ready) and parts else None
                         for at in range(long - 1)]
                ins += [a for a in older if a is not None]
                outs += 1
            lately = got[max(back, 0):] if back >= 0 else got[-1:]
            ins += lately
            if back >= 0:
                ins += [kept[back]]
                outs += 2
            here = functools.partial(step_body, ready, sends, back >= 0, tuple(a is not None for a in older), len(lately), len(ties))
            result = list(call(
                here, where, [(a, shape, whole) for a in ins] + [(a, None, None) for a in ties],
                [(shape, F32, shape, whole)] * outs, flops=kept[0].size))
            ties = []
            if ready:
                parts.append(result.pop(0))
            if sends:
                send = result.pop(0)
                got.append(shift(send, 1, reverse))
                if t > 0 and len(done) < len(beside):
                    done.append(beside[len(done)](send))
                    ties.append(done[-1][0])
            if back >= 0:
                e, turned = result
                out.append((e, swapped[back], lax.ppermute(turned, "seq", swap)))
                ties.append(out[-1][2])
        while len(done) < len(beside):
            done.append(beside[len(done)](None))
        return out, done

    def shards(queries, keys, values, out_grad, norm_gain):
        tokens, width = queries.shape
        heads = width // DH
        half = heads // 2
        per = half // CHUNKS
        wide = half * DH
        narrow = per * DH
        at_seq = lax.axis_index("seq")
        y, z = at_seq % 2, at_seq // 2
        place = y.astype(jnp.int32).reshape(1)
        turned = 1 - place
        gain = norm_gain.reshape(1, width)
        mac = 2 * GROUP * DH

        kept_half = lambda i, s: (0, s[0])
        sent_half = lambda i, s: (0, 1 - s[0])
        whole2 = lambda i, s: (0, 0)
        whole3 = lambda i, s: (0, 0, 0)

        def at_k(c):
            return lambda i, s: (0, s[0] * CHUNKS + c)

        def at_o(c):
            return lambda i, s: (0, (1 - s[0]) * CHUNKS + c)

        def at_k3(c):
            return lambda i, s: (s[0] * CHUNKS + c, 0, 0)

        def at_o3(c):
            return lambda i, s: ((1 - s[0]) * CHUNKS + c, 0, 0)

        def states(skip, width, index):
            count = width // narrow - skip
            return call(
                functools.partial(states_body, per, skip), place,
                [(a, (tokens, width), index) for a in (keys, values)],
                [((per, DH, DH), F32, (per, DH, DH), whole3)] * count,
                flops=count * per * mac * DH, grant=61,
            )

        sent = states(0, narrow, at_o(0)) + states(1, wide, sent_half)

        group = half // 2
        strip = lambda i, s: (0, (2 * s[0] + i) % 4)
        *kept, scores, attn_local = call(
            functools.partial(local_body, per, CHUNKS, group), place,
            [(a, (tokens, group * DH), strip) for a in (queries, keys, values)],
            [((per, DH, DH), F32, (per, DH, DH), whole3)] * CHUNKS + [
                ((heads, GROUP, GROUP), BF16, (group, GROUP, GROUP), lambda i, s: ((2 * s[0] + i) % 4, 0, 0)),
                ((tokens, width), F32, (tokens, group * DH), strip),
            ],
            grid=(4,), flops=heads * mac * (2 * GROUP + DH // 2),
        )

        before, _ = scan(kept, sent, y, z, False, [])

        block = (tokens, narrow)
        square = cross = None
        attns, priors = [], []
        for c in range(CHUNKS):
            e, r, other = before[c]
            first, last = c == 0, c == CHUNKS - 1
            ins = []
            for a in (attn_local, queries, out_grad):
                ins += [(a, block, at_k(c)), (a, block, at_o(c))]
            ins += [(gain, (1, narrow), at_k(c)), (gain, (1, narrow), at_o(c))]
            ins += [(a, (per, DH, DH), whole3) for a in (e, r, other)]
            if not first:
                ins += [(a, (GROUP, DH), whole2) for a in (square, cross)]
            outs = [(block, F32, block, whole2)] * 2 + [((per, DH, DH), BF16, (per, DH, DH), whole3)] * 2
            if last:
                outs += [((2, GROUP), F32, (2, GROUP), whole2)]
            else:
                outs += [((GROUP, DH), F32, (GROUP, DH), whole2)] * 2
            a_k, a_o, s_k, s_o, *stats = call(
                functools.partial(attn_body, per, first, last), place, ins, outs, flops=2 * per * mac * DH)
            attns.append((a_k, a_o))
            priors.append((s_k, s_o))
            if last:
                mine = stats[0]
            else:
                square, cross = stats

        sums = [mine]
        for step in range(1, parts):
            sums.append(lax.ppermute(mine, "head", [(i, (i + step) % parts) for i in range(parts)]))

        def delta(which, skip, width, index):
            count = width // narrow - skip
            ins = [(a, (2, GROUP), whole2) for a in sums]
            ins += [(attns[skip + c][which], block, whole2) for c in range(count)]
            ins += [(queries, (tokens, width), index), (out_grad, (tokens, width), index), (gain, (1, width), index)]
            outs = [(block, BF16, block, whole2)] * count
            outs += [((per, DH, DH), F32, (per, DH, DH), whole3)] * count
            result = call(
                functools.partial(delta_body, per, skip, count, parts, float(parts * heads * DH)), place, ins, outs,
                flops=count * per * mac * DH)
            return result[:count], result[count:]

        d_first, first_sent = delta(1, 0, narrow, at_o(0))
        d_rest, rest_sent = delta(1, 1, wide, sent_half)
        d_o, sent = d_first + d_rest, first_sent + rest_sent
        d_k, kept = delta(0, 0, wide, kept_half)

        def grads(c, tie):
            ins = []
            for a in (queries, keys, values):
                ins += [(a, block, at_k(c)), (a, block, at_o(c))]
            ins += [(scores, (per, GROUP, GROUP), at_k3(c)), (scores, (per, GROUP, GROUP), at_o3(c))]
            ins += [(d_k[c], block, whole2), (d_o[c], block, whole2)]
            ins += [(a, (per, DH, DH), whole3) for a in priors[c]]
            ties = 0 if tie is None else 1
            if ties:
                ins += [(tie, None, None)]
            outs = [(block, BF16, block, whole2)] * 2 + [(block, F32, block, whole2)] * 4
            return call(
                functools.partial(grads_body, per, ties), place, ins, outs,
                flops=2 * per * mac * (4 * GROUP + DH))

        after, grads = scan(
            kept, sent, 1 - y, long - 1 - z, True, [functools.partial(grads, c) for c in range(CHUNKS)])

        kg = vg = qg = None
        for c in range(CHUNKS):
            e, r, other = after[c]
            kg, vg, qg = finish(c, per, narrow, tokens, width, place, keys, values, grads[c], e, r, other, kg, vg, qg)
        return qg, kg, vg

    def finish(c, per, narrow, tokens, width, place, keys, values, grads, e, r, other, *done):
        qg_k, qg_o, kl_k, kl_o, vl_k, vl_o = grads
        block = (tokens, narrow)
        mine = lambda i, s: (0, jnp.where(i == 0, s[0], 1 - s[0]) * CHUNKS + c)
        whole2 = lambda i, s: (0, 0)
        whole3 = lambda i, s: (0, 0, 0)
        ins = [(a, block, whole2) for a in (qg_k, qg_o, kl_k, kl_o, vl_k, vl_o)]
        ins += [(a, block, mine) for a in (keys, values)]
        ins += [(a, (per, DH, DH), whole3) for a in (e, r, other)]
        aliases = {}
        if done[0] is not None:
            for n, a in enumerate(done):
                aliases[len(ins) + 1] = n
                ins.append((a, None, None))
        outs = [((tokens, width), BF16, block, mine)] * 3

        def body(place, qk, qo, kk, ko, vk, vo, k, v, e, r, other, *refs):
            kg, vg, qg = refs[-3:]
            mine = pl.program_id(0) == 0

            def one(q_in, k_in, v_in, state):
                qg[...] = q_in[...]
                for j in range(per):
                    at = slice(j * DH, (j + 1) * DH)
                    later = state(j).astype(BF16)
                    kg[:, at] = (k_in[:, at] + dot(v[:, at], later, 1, 1)).astype(BF16)
                    vg[:, at] = (v_in[:, at] + dot(k[:, at], later, 1, 0)).astype(BF16)

            @pl.when(mine)
            def _():
                one(qk, kk, vk, lambda j: jnp.where(place[0] == 0, e[j] + r[j], e[j]))

            @pl.when(jnp.logical_not(mine))
            def _():
                one(qo, ko, vo, lambda j: other[j])

        return call(body, place, ins, outs, grid=(2,), aliases=aliases, flops=4 * per * 2 * GROUP * DH * DH)

    return jax.shard_map(
        shards,
        mesh=mesh,
        in_specs=(
            P("seq", "head"),
            P("seq", "head"),
            P("seq", "head"),
            P("seq", "head"),
            P("head"),
        ),
        out_specs=(P("seq", "head"), P("seq", "head"), P("seq", "head")),
        check_vma=False,
    )
```

```python
import functools

import jax
import jax.numpy as jnp
from jax import lax
from jax.experimental import pallas as pl
from jax.experimental.pallas import tpu as pltpu
from jax.sharding import PartitionSpec as P

DH = 128
GROUP = 256
CHUNKS = 4
EPS = 1e-05
F32 = jnp.float32
BF16 = jnp.bfloat16


def dot(a, b, ca, cb):
    return lax.dot_general(a, b, (((ca,), (cb,)), ((), ())), preferred_element_type=F32)


def head(ref, j):
    return ref[:, j * DH:(j + 1) * DH]


def causal():
    rows = lax.broadcasted_iota(jnp.int32, (GROUP, GROUP), 0)
    cols = lax.broadcasted_iota(jnp.int32, (GROUP, GROUP), 1)
    return rows >= cols


def masked(scores, mask):
    return jnp.where(mask, scores, 0.0).astype(BF16)


def call(body, place, ins, outs, grid=(1,), aliases=None, flops=0, grant=6):
    size = sum(a.size * a.dtype.itemsize // 2 for a, _, _ in ins)
    return pl.pallas_call(
        body,
        grid_spec=pltpu.PrefetchScalarGridSpec(
            num_scalar_prefetch=1,
            grid=grid,
            in_specs=[pl.BlockSpec(b, m) if b else pl.BlockSpec(memory_space=pl.ANY) for _, b, m in ins],
            out_specs=[pl.BlockSpec(b, m) for _, _, b, m in outs],
        ),
        out_shape=[jax.ShapeDtypeStruct(s, d) for s, d, _, _ in outs],
        input_output_aliases=aliases or {},
        compiler_params=pltpu.CompilerParams(vmem_limit_bytes=grant * 1024 * 1024),
        cost_estimate=pl.CostEstimate(flops=flops, bytes_accessed=size, transcendentals=0),
    )(place, *[a for a, _, _ in ins])


def states_body(per, place, a, b, *outs):
    for c, out in enumerate(outs):
        for j in range(per):
            h = c * per + j
            out[j] = dot(head(a, h), head(b, h), 0, 0)


def local_body(per, chunks, heads, place, q, k, v, *refs):
    outs, scores, attn = refs[:chunks], refs[chunks], refs[chunks + 1]
    for turn in range(2):
        @pl.when(pl.program_id(0) == turn)
        def _():
            for j in range(heads):
                h = turn * heads + j
                outs[h // per][h % per] = dot(head(k, j), head(v, j), 0, 0)
    mask = causal()
    for j in range(heads):
        s = masked(dot(head(q, j), head(k, j), 1, 1), mask)
        scores[j] = s
        attn[:, j * DH:(j + 1) * DH] = dot(s, head(v, j), 1, 0)


def attn_body(per, first, last, place, al_k, al_o, q_k, q_o, g_k, g_o, n_k, n_o, e, r, other, *refs):
    if not first:
        sq_in, cr_in, *refs = refs
    at_k, at_o, sb_k, sb_o, *stats = refs
    second = place[0] == 1
    square = jnp.zeros((GROUP, DH), F32) if first else sq_in[...]
    cross = jnp.zeros((GROUP, DH), F32) if first else cr_in[...]
    for j in range(per):
        kept = jnp.where(second, e[j] + r[j], e[j]).astype(BF16)
        sb_k[j] = kept
        sb_o[j] = other[j].astype(BF16)
        for al, q, g, n, sb, at in (
            (al_k, q_k, g_k, n_k, sb_k, at_k),
            (al_o, q_o, g_o, n_o, sb_o, at_o),
        ):
            x = head(al, j) + dot(head(q, j), sb[j], 1, 0)
            at[:, j * DH:(j + 1) * DH] = x
            scaled = head(n, j).astype(F32) * head(g, j).astype(F32)
            square = square + x * x
            cross = cross + scaled * x
    if last:
        stats[0][0:1] = jnp.sum(square.T, axis=0, keepdims=True)
        stats[0][1:2] = jnp.sum(cross.T, axis=0, keepdims=True)
    else:
        stats[0][...] = square
        stats[1][...] = cross


def delta_body(per, chunks, parts, features, place, *refs):
    stats = refs[:parts]
    attn = refs[parts:parts + chunks]
    q, g, n = refs[parts + chunks:parts + chunks + 3]
    outs = refs[parts + chunks + 3:]
    total = stats[0][...]
    for s in stats[1:]:
        total = total + s[...]
    inverse = lax.rsqrt(total[0:1] / features + EPS)
    slope = inverse * inverse * inverse * (total[1:2] / features)
    inverse = jnp.broadcast_to(inverse, (DH, GROUP)).T
    slope = jnp.broadcast_to(slope, (DH, GROUP)).T
    for c in range(chunks):
        for j in range(per):
            h = c * per + j
            scaled = head(n, h).astype(F32) * head(g, h).astype(F32)
            x = (inverse * scaled - head(attn[c], j) * slope).astype(BF16)
            outs[c][:, j * DH:(j + 1) * DH] = x
            outs[chunks + c][j] = dot(head(q, h), x, 0, 0)


def grads_body(per, place, *refs):
    (q_k, q_o, k_k, k_o, v_k, v_o, s_k, s_o, d_k, d_o, sb_k, sb_o) = refs[:12]
    qg_k, qg_o, kg_k, kg_o, vg_k, vg_o = refs[12:]
    mask = causal()
    for j in range(per):
        at = slice(j * DH, (j + 1) * DH)
        for q, k, v, s, d, sb, qg, kg, vg in (
            (q_k, k_k, v_k, s_k, d_k, sb_k, qg_k, kg_k, vg_k),
            (q_o, k_o, v_o, s_o, d_o, sb_o, qg_o, kg_o, vg_o),
        ):
            do = head(d, j)
            ds = masked(dot(do, head(v, j), 1, 1), mask)
            qg[:, at] = (dot(ds, head(k, j), 1, 0) + dot(do, sb[j], 1, 1)).astype(BF16)
            kg[:, at] = dot(ds, head(q, j), 0, 0)
            vg[:, at] = dot(s[j], do, 0, 0)


def solution(mesh):
    count = mesh.shape["seq"]
    parts = mesh.shape["head"]
    long = count // 2
    swap = [(i, i ^ 1) for i in range(count)]

    def hop(array, near, far, reverse):
        pairs = []
        for z in range(long):
            to = z + far
            if to < long and near(z):
                for y in range(2):
                    pairs.append((2 * z + y, 2 * to + y))
        if reverse:
            pairs = [(count - 1 - a, count - 1 - b) for a, b in pairs]
        return lax.ppermute(array, "seq", pairs)

    def shift(array, far, reverse):
        return hop(array, lambda at: True, far, reverse)

    def doubling(parts, reverse):
        out = []
        for part in parts:
            carry = shift(part, 1, reverse)
            far = 1
            while far < long:
                carry = carry + shift(carry, far, reverse)
                far *= 2
            out.append(carry)
        return out

    def scan(kept, sent, y, reverse, beside):
        swapped = [lax.ppermute(b, "seq", swap) for b in sent]
        if long > 4 or long < 2:
            sums = [a + r for a, r in zip(kept, swapped)]
            sums = doubling(sums, reverse) if long > 1 else [jnp.zeros_like(a) for a in sums]
            others = [
                lax.ppermute(jnp.where(y == 0, e + a, e), "seq", swap) for a, e in zip(kept, sums)
            ]
            return list(zip(sums, swapped, others)), [work() for work in beside]
        chunks = len(kept)
        order = sorted((2 * stage + c, -stage, c, stage) for stage in range(long) for c in range(chunks))
        part, flight, carry, out, done = {}, dict(enumerate(swapped)), {}, {}, []
        last = []
        for turn, (_, _, c, stage) in enumerate(order):
            if turn in (0, 3) and len(done) < len(beside):
                done.append(beside[len(done)]())
                last.append(done[-1][0])
            got = flight[c]
            if last:
                got, *_ = lax.optimization_barrier((got, *last))
            if stage == 0:
                swapped[c] = got
                part[c] = send = kept[c] + got
            else:
                carry[c] = got if stage == 1 else carry[c] + got
                send = carry[c] + part[c]
            if stage < long - 1:
                flight[c] = hop(send, lambda at: at == stage, 1, reverse)
                last = [send]
            else:
                send = jnp.where(y == 0, carry[c] + kept[c], carry[c])
                out[c] = (carry[c], swapped[c], lax.ppermute(send, "seq", swap))
                last = [send]
        return [out[c] for c in range(chunks)], done + [work() for work in beside[len(done):]]

    def shards(queries, keys, values, out_grad, norm_gain):
        tokens, width = queries.shape
        heads = width // DH
        half = heads // 2
        per = half // CHUNKS
        wide = half * DH
        narrow = per * DH
        at_seq = lax.axis_index("seq")
        y = at_seq % 2
        place = y.astype(jnp.int32).reshape(1)
        turned = 1 - place
        gain = norm_gain.reshape(1, width)
        mac = 2 * GROUP * DH

        kept_half = lambda i, s: (0, s[0])
        sent_half = lambda i, s: (0, 1 - s[0])
        whole2 = lambda i, s: (0, 0)
        whole3 = lambda i, s: (0, 0, 0)

        def at_k(c):
            return lambda i, s: (0, s[0] * CHUNKS + c)

        def at_o(c):
            return lambda i, s: (0, (1 - s[0]) * CHUNKS + c)

        def at_k3(c):
            return lambda i, s: (s[0] * CHUNKS + c, 0, 0)

        def at_o3(c):
            return lambda i, s: ((1 - s[0]) * CHUNKS + c, 0, 0)

        sent = call(
            functools.partial(states_body, per), place,
            [(a, (tokens, wide), sent_half) for a in (keys, values)],
            [((per, DH, DH), F32, (per, DH, DH), whole3)] * CHUNKS,
            flops=half * mac * DH,
        )

        group = half // 2
        strip = lambda i, s: (0, (2 * s[0] + i) % 4)
        *kept, scores, attn_local = call(
            functools.partial(local_body, per, CHUNKS, group), place,
            [(a, (tokens, group * DH), strip) for a in (queries, keys, values)],
            [((per, DH, DH), F32, (per, DH, DH), whole3)] * CHUNKS + [
                ((heads, GROUP, GROUP), BF16, (group, GROUP, GROUP), lambda i, s: ((2 * s[0] + i) % 4, 0, 0)),
                ((tokens, width), F32, (tokens, group * DH), strip),
            ],
            grid=(4,), flops=heads * mac * (2 * GROUP + DH // 2),
        )

        before, _ = scan(kept, sent, y, False, [])

        block = (tokens, narrow)
        square = cross = None
        attns, priors = [], []
        for c in range(CHUNKS):
            e, r, other = before[c]
            first, last = c == 0, c == CHUNKS - 1
            ins = []
            for a in (attn_local, queries, out_grad):
                ins += [(a, block, at_k(c)), (a, block, at_o(c))]
            ins += [(gain, (1, narrow), at_k(c)), (gain, (1, narrow), at_o(c))]
            ins += [(a, (per, DH, DH), whole3) for a in (e, r, other)]
            if not first:
                ins += [(a, (GROUP, DH), whole2) for a in (square, cross)]
            outs = [(block, F32, block, whole2)] * 2 + [((per, DH, DH), BF16, (per, DH, DH), whole3)] * 2
            if last:
                outs += [((2, GROUP), F32, (2, GROUP), whole2)]
            else:
                outs += [((GROUP, DH), F32, (GROUP, DH), whole2)] * 2
            a_k, a_o, s_k, s_o, *stats = call(
                functools.partial(attn_body, per, first, last), place, ins, outs, flops=2 * per * mac * DH)
            attns.append((a_k, a_o))
            priors.append((s_k, s_o))
            if last:
                mine = stats[0]
            else:
                square, cross = stats

        sums = [mine]
        paired = parts & (parts - 1) == 0
        for step in range(1, parts):
            sums.append(lax.ppermute(
                mine, "head", [(i, i ^ step if paired else (i + step) % parts) for i in range(parts)]))

        def delta(which, index):
            ins = [(a, (2, GROUP), whole2) for a in sums]
            ins += [(attns[c][which], block, whole2) for c in range(CHUNKS)]
            ins += [(queries, (tokens, wide), index), (out_grad, (tokens, wide), index), (gain, (1, wide), index)]
            outs = [(block, BF16, block, whole2)] * CHUNKS
            outs += [((per, DH, DH), F32, (per, DH, DH), whole3)] * CHUNKS
            result = call(
                functools.partial(delta_body, per, CHUNKS, parts, float(parts * heads * DH)), place, ins, outs,
                flops=half * mac * DH)
            return result[:CHUNKS], result[CHUNKS:]

        d_o, sent = delta(1, sent_half)
        d_k, kept = delta(0, kept_half)

        def grads(c):
            ins = []
            for a in (queries, keys, values):
                ins += [(a, block, at_k(c)), (a, block, at_o(c))]
            ins += [(scores, (per, GROUP, GROUP), at_k3(c)), (scores, (per, GROUP, GROUP), at_o3(c))]
            ins += [(d_k[c], block, whole2), (d_o[c], block, whole2)]
            ins += [(a, (per, DH, DH), whole3) for a in priors[c]]
            outs = [(block, BF16, block, whole2)] * 2 + [(block, F32, block, whole2)] * 4
            return call(
                functools.partial(grads_body, per), place, ins, outs,
                flops=2 * per * mac * (4 * GROUP + DH))

        after, grads = scan(
            kept, sent, 1 - y, True, [functools.partial(grads, c) for c in range(CHUNKS)])

        kg = vg = qg = None
        for c in range(CHUNKS):
            e, r, other = after[c]
            kg, vg, qg = finish(c, per, narrow, tokens, width, place, keys, values, grads[c], e, r, other, kg, vg, qg)
        return qg, kg, vg

    def finish(c, per, narrow, tokens, width, place, keys, values, grads, e, r, other, *done):
        qg_k, qg_o, kl_k, kl_o, vl_k, vl_o = grads
        block = (tokens, narrow)
        mine = lambda i, s: (0, jnp.where(i == 0, s[0], 1 - s[0]) * CHUNKS + c)
        whole2 = lambda i, s: (0, 0)
        whole3 = lambda i, s: (0, 0, 0)
        ins = [(a, block, whole2) for a in (qg_k, qg_o, kl_k, kl_o, vl_k, vl_o)]
        ins += [(a, block, mine) for a in (keys, values)]
        ins += [(a, (per, DH, DH), whole3) for a in (e, r, other)]
        aliases = {}
        if done[0] is not None:
            for n, a in enumerate(done):
                aliases[len(ins) + 1] = n
                ins.append((a, None, None))
        outs = [((tokens, width), BF16, block, mine)] * 3

        def body(place, qk, qo, kk, ko, vk, vo, k, v, e, r, other, *refs):
            kg, vg, qg = refs[-3:]
            mine = pl.program_id(0) == 0

            def one(q_in, k_in, v_in, state):
                qg[...] = q_in[...]
                for j in range(per):
                    at = slice(j * DH, (j + 1) * DH)
                    later = state(j).astype(BF16)
                    kg[:, at] = (k_in[:, at] + dot(v[:, at], later, 1, 1)).astype(BF16)
                    vg[:, at] = (v_in[:, at] + dot(k[:, at], later, 1, 0)).astype(BF16)

            @pl.when(mine)
            def _():
                one(qk, kk, vk, lambda j: jnp.where(place[0] == 0, e[j] + r[j], e[j]))

            @pl.when(jnp.logical_not(mine))
            def _():
                one(qo, ko, vo, lambda j: other[j])

        return call(body, place, ins, outs, grid=(2,), aliases=aliases, flops=4 * per * 2 * GROUP * DH * DH)

    return jax.shard_map(
        shards,
        mesh=mesh,
        in_specs=(
            P("seq", "head"),
            P("seq", "head"),
            P("seq", "head"),
            P("seq", "head"),
            P("head"),
        ),
        out_specs=(P("seq", "head"), P("seq", "head"), P("seq", "head")),
        check_vma=False,
    )
```

```python
import functools

import jax
import jax.numpy as jnp
from jax import lax
from jax.experimental import pallas as pl
from jax.experimental.pallas import tpu as pltpu
from jax.sharding import PartitionSpec as P

DH = 128
GROUP = 256
CHUNKS = 4
EPS = 1e-05
F32 = jnp.float32
BF16 = jnp.bfloat16


def dot(a, b, ca, cb):
    return lax.dot_general(a, b, (((ca,), (cb,)), ((), ())), preferred_element_type=F32)


def head(ref, j):
    return ref[:, j * DH:(j + 1) * DH]


def causal():
    rows = lax.broadcasted_iota(jnp.int32, (GROUP, GROUP), 0)
    cols = lax.broadcasted_iota(jnp.int32, (GROUP, GROUP), 1)
    return rows >= cols


def masked(scores, mask):
    return jnp.where(mask, scores, 0.0).astype(BF16)


HBM, VMEM = pltpu.HBM, pltpu.VMEM


def call(body, place, ins, outs, grid=(1,), aliases=None, flops=0, grant=6):
    ins = [(*item, None)[:4] for item in ins]
    outs = [(*item, None)[:5] for item in outs]
    arrays = [pltpu.with_memory_space_constraint(a, m) if m else a for a, _, _, m in ins]
    size = sum(a.size * a.dtype.itemsize // 2 for a in arrays)
    return pl.pallas_call(
        body,
        grid_spec=pltpu.PrefetchScalarGridSpec(
            num_scalar_prefetch=1,
            grid=grid,
            in_specs=[pl.BlockSpec(b, m) if b else pl.BlockSpec(memory_space=pl.ANY) for _, b, m, _ in ins],
            out_specs=[pl.BlockSpec(b, m) for _, _, b, m, _ in outs],
        ),
        out_shape=[(m or jax.ShapeDtypeStruct)(s, d) for s, d, _, _, m in outs],
        input_output_aliases=aliases or {},
        compiler_params=pltpu.CompilerParams(vmem_limit_bytes=grant * 1024 * 1024),
        cost_estimate=pl.CostEstimate(flops=flops, bytes_accessed=size, transcendentals=0),
    )(place, *arrays)


def states_body(per, place, a, b, *outs):
    for c, out in enumerate(outs):
        for j in range(per):
            h = c * per + j
            out[j] = dot(head(a, h), head(b, h), 0, 0)


def local_body(per, chunks, heads, place, q, k, v, *refs):
    outs, scores, attn = refs[:chunks], refs[chunks], refs[chunks + 1]
    for turn in range(2):
        @pl.when(pl.program_id(0) == turn)
        def _():
            for j in range(heads):
                h = turn * heads + j
                outs[h // per][h % per] = dot(head(k, j), head(v, j), 0, 0)
    mask = causal()
    for j in range(heads):
        s = masked(dot(head(q, j), head(k, j), 1, 1), mask)
        scores[j] = s
        attn[:, j * DH:(j + 1) * DH] = dot(s, head(v, j), 1, 0)


def attn_body(per, first, last, place, al_k, al_o, q_k, q_o, g_k, g_o, n_k, n_o, e, r, other, *refs):
    if not first:
        sq_in, cr_in, *refs = refs
    at_k, at_o, sb_k, sb_o, *stats = refs
    second = place[0] == 1
    square = jnp.zeros((GROUP, DH), F32) if first else sq_in[...]
    cross = jnp.zeros((GROUP, DH), F32) if first else cr_in[...]
    for j in range(per):
        kept = jnp.where(second, e[j] + r[j], e[j]).astype(BF16)
        sb_k[j] = kept
        sb_o[j] = other[j].astype(BF16)
        for al, q, g, n, sb, at in (
            (al_k, q_k, g_k, n_k, sb_k, at_k),
            (al_o, q_o, g_o, n_o, sb_o, at_o),
        ):
            x = head(al, j) + dot(head(q, j), sb[j], 1, 0)
            at[:, j * DH:(j + 1) * DH] = x
            scaled = head(n, j).astype(F32) * head(g, j).astype(F32)
            square = square + x * x
            cross = cross + scaled * x
    if last:
        stats[0][0:1] = jnp.sum(square.T, axis=0, keepdims=True)
        stats[0][1:2] = jnp.sum(cross.T, axis=0, keepdims=True)
    else:
        stats[0][...] = square
        stats[1][...] = cross


def delta_body(per, chunks, parts, features, place, *refs):
    stats = refs[:parts]
    attn = refs[parts:parts + chunks]
    q, g, n = refs[parts + chunks:parts + chunks + 3]
    outs = refs[parts + chunks + 3:]
    total = stats[0][...]
    for s in stats[1:]:
        total = total + s[...]
    inverse = lax.rsqrt(total[0:1] / features + EPS)
    slope = inverse * inverse * inverse * (total[1:2] / features)
    inverse = jnp.broadcast_to(inverse, (DH, GROUP)).T
    slope = jnp.broadcast_to(slope, (DH, GROUP)).T
    for c in range(chunks):
        for j in range(per):
            h = c * per + j
            scaled = head(n, h).astype(F32) * head(g, h).astype(F32)
            x = (inverse * scaled - head(attn[c], j) * slope).astype(BF16)
            outs[c][:, j * DH:(j + 1) * DH] = x
            outs[chunks + c][j] = dot(head(q, h), x, 0, 0)


def grads_body(per, place, *refs):
    (q_k, q_o, k_k, k_o, v_k, v_o, s_k, s_o, d_k, d_o, sb_k, sb_o) = refs[:12]
    qg_k, qg_o, kg_k, kg_o, vg_k, vg_o = refs[12:]
    mask = causal()
    for j in range(per):
        at = slice(j * DH, (j + 1) * DH)
        for q, k, v, s, d, sb, qg, kg, vg in (
            (q_k, k_k, v_k, s_k, d_k, sb_k, qg_k, kg_k, vg_k),
            (q_o, k_o, v_o, s_o, d_o, sb_o, qg_o, kg_o, vg_o),
        ):
            do = head(d, j)
            ds = masked(dot(do, head(v, j), 1, 1), mask)
            qg[:, at] = (dot(ds, head(k, j), 1, 0) + dot(do, sb[j], 1, 1)).astype(BF16)
            kg[:, at] = dot(ds, head(q, j), 0, 0)
            vg[:, at] = dot(s[j], do, 0, 0)


def solution(mesh):
    count = mesh.shape["seq"]
    parts = mesh.shape["head"]
    long = count // 2
    swap = [(i, i ^ 1) for i in range(count)]

    def hop(array, near, far, reverse):
        pairs = []
        for z in range(long):
            to = z + far
            if to < long and near(z):
                for y in range(2):
                    pairs.append((2 * z + y, 2 * to + y))
        if reverse:
            pairs = [(count - 1 - a, count - 1 - b) for a, b in pairs]
        return lax.ppermute(array, "seq", pairs)

    def shift(array, far, reverse):
        return hop(array, lambda at: True, far, reverse)

    def doubling(parts, reverse):
        out = []
        for part in parts:
            carry = shift(part, 1, reverse)
            far = 1
            while far < long:
                carry = carry + shift(carry, far, reverse)
                far *= 2
            out.append(carry)
        return out

    def scan(kept, sent, y, reverse, beside):
        swapped = [lax.ppermute(b, "seq", swap) for b in sent]
        if long > 4 or long < 2:
            sums = [a + r for a, r in zip(kept, swapped)]
            sums = doubling(sums, reverse) if long > 1 else [jnp.zeros_like(a) for a in sums]
            others = [
                lax.ppermute(jnp.where(y == 0, e + a, e), "seq", swap) for a, e in zip(kept, sums)
            ]
            return list(zip(sums, swapped, others)), [work() for work in beside]
        chunks = len(kept)
        order = sorted((2 * stage + c, -stage, c, stage) for stage in range(long) for c in range(chunks))
        part, flight, carry, out, done = {}, dict(enumerate(swapped)), {}, {}, []
        last = []
        for turn, (_, _, c, stage) in enumerate(order):
            if turn in (0, 3) and len(done) < len(beside):
                done.append(beside[len(done)]())
                last.append(done[-1][0])
            got = flight[c]
            if last:
                got, *_ = lax.optimization_barrier((got, *last))
            if stage == 0:
                swapped[c] = got
                part[c] = send = kept[c] + got
            else:
                carry[c] = got if stage == 1 else carry[c] + got
                send = carry[c] + part[c]
            if stage < long - 1:
                flight[c] = hop(send, lambda at: at == stage, 1, reverse)
                last = [send]
            else:
                send = jnp.where(y == 0, carry[c] + kept[c], carry[c])
                out[c] = (carry[c], swapped[c], lax.ppermute(send, "seq", swap))
                last = [send]
        return [out[c] for c in range(chunks)], done + [work() for work in beside[len(done):]]

    def shards(queries, keys, values, out_grad, norm_gain):
        tokens, width = queries.shape
        heads = width // DH
        half = heads // 2
        per = half // CHUNKS
        wide = half * DH
        narrow = per * DH
        at_seq = lax.axis_index("seq")
        y = at_seq % 2
        place = y.astype(jnp.int32).reshape(1)
        turned = 1 - place
        gain = norm_gain.reshape(1, width)
        mac = 2 * GROUP * DH

        kept_half = lambda i, s: (0, s[0])
        sent_half = lambda i, s: (0, 1 - s[0])
        whole2 = lambda i, s: (0, 0)
        whole3 = lambda i, s: (0, 0, 0)

        def at_k(c):
            return lambda i, s: (0, s[0] * CHUNKS + c)

        def at_o(c):
            return lambda i, s: (0, (1 - s[0]) * CHUNKS + c)

        def at_k3(c):
            return lambda i, s: (s[0] * CHUNKS + c, 0, 0)

        def at_o3(c):
            return lambda i, s: ((1 - s[0]) * CHUNKS + c, 0, 0)

        sent = call(
            functools.partial(states_body, per), place,
            [(a, (tokens, wide), sent_half, HBM) for a in (keys, values)],
            [((per, DH, DH), F32, (per, DH, DH), whole3, VMEM)] * CHUNKS,
            flops=half * mac * DH,
        )

        group = half // 2
        strip = lambda i, s: (0, (2 * s[0] + i) % 4)
        *kept, scores, attn_local = call(
            functools.partial(local_body, per, CHUNKS, group), place,
            [(a, (tokens, group * DH), strip, HBM) for a in (queries, keys, values)],
            [((per, DH, DH), F32, (per, DH, DH), whole3, VMEM)] * CHUNKS + [
                ((heads, GROUP, GROUP), BF16, (group, GROUP, GROUP), lambda i, s: ((2 * s[0] + i) % 4, 0, 0), HBM),
                ((tokens, width), F32, (tokens, group * DH), strip, HBM),
            ],
            grid=(4,), flops=heads * mac * (2 * GROUP + DH // 2),
        )

        before, _ = scan(kept, sent, y, False, [])

        block = (tokens, narrow)
        square = cross = None
        attns, priors = [], []
        for c in range(CHUNKS):
            e, r, other = before[c]
            first, last = c == 0, c == CHUNKS - 1
            ins = []
            for a in (attn_local, queries, out_grad):
                ins += [(a, block, at_k(c)), (a, block, at_o(c))]
            ins += [(gain, (1, narrow), at_k(c)), (gain, (1, narrow), at_o(c))]
            ins += [(a, (per, DH, DH), whole3) for a in (e, r, other)]
            if not first:
                ins += [(a, (GROUP, DH), whole2) for a in (square, cross)]
            outs = [(block, F32, block, whole2, VMEM)] * 2 + [((per, DH, DH), BF16, (per, DH, DH), whole3, VMEM)] * 2
            if last:
                outs += [((2, GROUP), F32, (2, GROUP), whole2)]
            else:
                outs += [((GROUP, DH), F32, (GROUP, DH), whole2)] * 2
            a_k, a_o, s_k, s_o, *stats = call(
                functools.partial(attn_body, per, first, last), place, ins, outs, flops=2 * per * mac * DH)
            attns.append((a_k, a_o))
            priors.append((s_k, s_o))
            if last:
                mine = stats[0]
            else:
                square, cross = stats

        sums = [mine]
        paired = parts & (parts - 1) == 0
        for step in range(1, parts):
            sums.append(lax.ppermute(
                mine, "head", [(i, i ^ step if paired else (i + step) % parts) for i in range(parts)]))

        def delta(which, index):
            ins = [(a, (2, GROUP), whole2) for a in sums]
            ins += [(attns[c][which], block, whole2) for c in range(CHUNKS)]
            ins += [(queries, (tokens, wide), index), (out_grad, (tokens, wide), index), (gain, (1, wide), index)]
            outs = [(block, BF16, block, whole2, VMEM)] * CHUNKS
            outs += [((per, DH, DH), F32, (per, DH, DH), whole3, VMEM)] * CHUNKS
            result = call(
                functools.partial(delta_body, per, CHUNKS, parts, float(parts * heads * DH)), place, ins, outs,
                flops=half * mac * DH)
            return result[:CHUNKS], result[CHUNKS:]

        d_o, sent = delta(1, sent_half)
        d_k, kept = delta(0, kept_half)

        def grads(c):
            ins = []
            for a, m in ((queries, None), (keys, HBM), (values, HBM)):
                ins += [(a, block, at_k(c), m), (a, block, at_o(c), m)]
            ins += [(scores, (per, GROUP, GROUP), at(c), HBM) for at in (at_k3, at_o3)]
            ins += [(d_k[c], block, whole2), (d_o[c], block, whole2)]
            ins += [(a, (per, DH, DH), whole3) for a in priors[c]]
            outs = [(block, BF16, block, whole2, HBM)] * 2 + [(block, F32, block, whole2, HBM)] * 4
            return call(
                functools.partial(grads_body, per), place, ins, outs,
                flops=2 * per * mac * (4 * GROUP + DH))

        after, grads = scan(
            kept, sent, 1 - y, True, [functools.partial(grads, c) for c in range(CHUNKS)])

        kg = vg = qg = None
        for c in range(CHUNKS):
            e, r, other = after[c]
            kg, vg, qg = finish(c, per, narrow, tokens, width, place, keys, values, grads[c], e, r, other, kg, vg, qg)
        return qg, kg, vg

    def finish(c, per, narrow, tokens, width, place, keys, values, grads, e, r, other, *done):
        qg_k, qg_o, kl_k, kl_o, vl_k, vl_o = grads
        block = (tokens, narrow)
        mine = lambda i, s: (0, jnp.where(i == 0, s[0], 1 - s[0]) * CHUNKS + c)
        whole2 = lambda i, s: (0, 0)
        whole3 = lambda i, s: (0, 0, 0)
        ins = [(a, block, whole2, HBM) for a in (qg_k, qg_o, kl_k, kl_o, vl_k, vl_o)]
        ins += [(a, block, mine, HBM) for a in (keys, values)]
        ins += [(a, (per, DH, DH), whole3) for a in (e, r, other)]
        aliases = {}
        if done[0] is not None:
            for n, a in enumerate(done):
                aliases[len(ins) + 1] = n
                ins.append((a, None, None, HBM))
        outs = [((tokens, width), BF16, block, mine, HBM)] * 3

        def body(place, qk, qo, kk, ko, vk, vo, k, v, e, r, other, *refs):
            kg, vg, qg = refs[-3:]
            mine = pl.program_id(0) == 0

            def one(q_in, k_in, v_in, state):
                qg[...] = q_in[...]
                for j in range(per):
                    at = slice(j * DH, (j + 1) * DH)
                    later = state(j).astype(BF16)
                    kg[:, at] = (k_in[:, at] + dot(v[:, at], later, 1, 1)).astype(BF16)
                    vg[:, at] = (v_in[:, at] + dot(k[:, at], later, 1, 0)).astype(BF16)

            @pl.when(mine)
            def _():
                one(qk, kk, vk, lambda j: jnp.where(place[0] == 0, e[j] + r[j], e[j]))

            @pl.when(jnp.logical_not(mine))
            def _():
                one(qo, ko, vo, lambda j: other[j])

        return call(body, place, ins, outs, grid=(2,), aliases=aliases, flops=4 * per * 2 * GROUP * DH * DH)

    return jax.shard_map(
        shards,
        mesh=mesh,
        in_specs=(
            P("seq", "head"),
            P("seq", "head"),
            P("seq", "head"),
            P("seq", "head"),
            P("head"),
        ),
        out_specs=(P("seq", "head"), P("seq", "head"), P("seq", "head")),
        check_vma=False,
    )
```

```python
import functools

import jax
import jax.numpy as jnp
from jax import lax
from jax.experimental import pallas as pl
from jax.experimental.pallas import tpu as pltpu
from jax.sharding import PartitionSpec as P

DH = 128
GROUP = 256
CHUNKS = 4
EPS = 1e-05
F32 = jnp.float32
BF16 = jnp.bfloat16


def dot(a, b, ca, cb):
    return lax.dot_general(a, b, (((ca,), (cb,)), ((), ())), preferred_element_type=F32)


def head(ref, j):
    return ref[:, j * DH:(j + 1) * DH]


def causal(turned=False):
    rows = lax.broadcasted_iota(jnp.int32, (GROUP, GROUP), 0)
    cols = lax.broadcasted_iota(jnp.int32, (GROUP, GROUP), 1)
    return cols >= rows if turned else rows >= cols


def masked(scores, mask):
    return jnp.where(mask, scores, 0.0).astype(BF16)


HBM, VMEM = pltpu.HBM, pltpu.VMEM


def call(body, place, ins, outs, grid=(1,), aliases=None, flops=0, grant=6):
    ins = [(*item, None)[:4] for item in ins]
    outs = [(*item, None)[:5] for item in outs]
    arrays = [pltpu.with_memory_space_constraint(a, m) if m else a for a, _, _, m in ins]
    size = sum(a.size * a.dtype.itemsize // 2 for a in arrays)
    return pl.pallas_call(
        body,
        grid_spec=pltpu.PrefetchScalarGridSpec(
            num_scalar_prefetch=1,
            grid=grid,
            in_specs=[pl.BlockSpec(b, m) if b else pl.BlockSpec(memory_space=pl.ANY) for _, b, m, _ in ins],
            out_specs=[pl.BlockSpec(b, m) for _, _, b, m, _ in outs],
        ),
        out_shape=[(m or jax.ShapeDtypeStruct)(s, d) for s, d, _, _, m in outs],
        input_output_aliases=aliases or {},
        compiler_params=pltpu.CompilerParams(vmem_limit_bytes=grant * 1024 * 1024),
        cost_estimate=pl.CostEstimate(flops=flops, bytes_accessed=size, transcendentals=0),
    )(place, *arrays)


def states_body(per, place, a, b, *outs):
    for c, out in enumerate(outs):
        for j in range(per):
            h = c * per + j
            out[j] = dot(head(a, h), head(b, h), 0, 0)


def local_body(per, chunks, heads, place, q, k, v, *refs):
    outs, attn = refs[:chunks], refs[chunks]
    for turn in range(2):
        @pl.when(pl.program_id(0) == turn)
        def _():
            for j in range(heads):
                h = turn * heads + j
                outs[h // per][h % per] = dot(head(k, j), head(v, j), 0, 0)
    mask = causal()
    for j in range(heads):
        s = masked(dot(head(q, j), head(k, j), 1, 1), mask)
        attn[:, j * DH:(j + 1) * DH] = dot(s, head(v, j), 1, 0)


def attn_body(per, first, last, place, al_k, al_o, q_k, q_o, g_k, g_o, n_k, n_o, e, r, other, *refs):
    if not first:
        sq_in, cr_in, *refs = refs
    at_k, at_o, sb_k, sb_o, *stats = refs
    square = jnp.zeros((GROUP, DH), F32) if first else sq_in[...]
    cross = jnp.zeros((GROUP, DH), F32) if first else cr_in[...]
    for j in range(per):
        kept = (e[j] + r[j]).astype(BF16)
        sb_k[j] = kept
        sb_o[j] = other[j].astype(BF16)
        for al, q, g, n, sb, at in (
            (al_k, q_k, g_k, n_k, sb_k, at_k),
            (al_o, q_o, g_o, n_o, sb_o, at_o),
        ):
            x = head(al, j) + dot(head(q, j), sb[j], 1, 0)
            at[:, j * DH:(j + 1) * DH] = x
            scaled = head(n, j).astype(F32) * head(g, j).astype(F32)
            square = square + x * x
            cross = cross + scaled * x
    if last:
        stats[0][0:1] = jnp.sum(square.T, axis=0, keepdims=True)
        stats[0][1:2] = jnp.sum(cross.T, axis=0, keepdims=True)
    else:
        stats[0][...] = square
        stats[1][...] = cross


def delta_body(per, chunks, parts, features, place, *refs):
    stats = refs[:parts]
    attn = refs[parts:parts + chunks]
    q, g, n = refs[parts + chunks:parts + chunks + 3]
    outs = refs[parts + chunks + 3:]
    total = stats[0][...]
    for s in stats[1:]:
        total = total + s[...]
    inverse = lax.rsqrt(total[0:1] / features + EPS)
    slope = inverse * inverse * inverse * (total[1:2] / features)
    inverse = jnp.broadcast_to(inverse, (DH, GROUP)).T
    slope = jnp.broadcast_to(slope, (DH, GROUP)).T
    for c in range(chunks):
        for j in range(per):
            h = c * per + j
            scaled = head(n, h).astype(F32) * head(g, h).astype(F32)
            x = (inverse * scaled - head(attn[c], j) * slope).astype(BF16)
            outs[c][:, j * DH:(j + 1) * DH] = x
            outs[chunks + c][j] = dot(head(q, h), x, 0, 0)


def query_body(per, place, k, v, d_k, d_o, sb_k, sb_o, *refs):
    qg = refs[-1]
    mask = causal()
    for turn, d, sb in ((0, d_k, sb_k), (1, d_o, sb_o)):
        @pl.when(pl.program_id(0) == turn)
        def _():
            for j in range(per):
                do = head(d, j)
                ds = masked(dot(do, head(v, j), 1, 1), mask)
                qg[:, j * DH:(j + 1) * DH] = (dot(ds, head(k, j), 1, 0) + dot(do, sb[j], 1, 1)).astype(BF16)


def final_body(per, terms, place, q, k, v, d, *refs):
    later_in, kg, vg = refs[:terms], refs[-2], refs[-1]
    mask = causal(turned=True)
    for j in range(per):
        at = slice(j * DH, (j + 1) * DH)
        later = later_in[0][j]
        for term in later_in[1:]:
            later = later + term[j]
        later = later.astype(BF16)
        qj, kj, vj, do = head(q, j), head(k, j), head(v, j), head(d, j)
        ds = masked(dot(vj, do, 1, 1), mask)
        st = masked(dot(kj, qj, 1, 1), mask)
        kg[:, at] = (dot(ds, qj, 1, 0) + dot(vj, later, 1, 1)).astype(BF16)
        vg[:, at] = (dot(st, do, 1, 0) + dot(kj, later, 1, 0)).astype(BF16)


def solution(mesh):
    count = mesh.shape["seq"]
    parts = mesh.shape["head"]
    long = count // 2
    swap = [(i, i ^ 1) for i in range(count)]

    def hop(array, near, far, reverse):
        pairs = []
        for z in range(long):
            to = z + far
            if to < long and near(z):
                for y in range(2):
                    pairs.append((2 * z + y, 2 * to + y))
        if reverse:
            pairs = [(count - 1 - a, count - 1 - b) for a, b in pairs]
        return lax.ppermute(array, "seq", pairs)

    def shift(array, far, reverse):
        return hop(array, lambda at: True, far, reverse)

    def doubling(parts, reverse):
        out = []
        for part in parts:
            carry = shift(part, 1, reverse)
            far = 1
            while far < long:
                carry = carry + shift(carry, far, reverse)
                far *= 2
            out.append(carry)
        return out

    def scan(kept, sent, y, reverse, ready):
        own = [None] * len(kept)
        if long > 4 or long < 2:
            swapped = [lax.ppermute(b, "seq", swap) for b in sent]
            own = [jnp.where(y == 0, 0.0, r) for r in swapped]
            sums = [a + r for a, r in zip(kept, swapped)]
            sums = doubling(sums, reverse) if long > 1 else [jnp.zeros_like(a) for a in sums]
            others = [
                lax.ppermute(jnp.where(y == 0, e + a, e), "seq", swap) for a, e in zip(kept, sums)
            ]
            return list(zip(sums, own, others))
        chunks = len(kept)
        order = sorted((2 * stage + c, -stage, c, stage) for stage in range(long) for c in range(chunks))
        part, flight, carry, out = {}, {}, {}, {}
        last = ready

        def swap_after(c, *things):
            if c < chunks:
                part_sent, *_ = lax.optimization_barrier((sent[c], *things))
                flight[c] = lax.ppermute(part_sent, "seq", swap)

        swap_after(0)
        swap_after(1)
        swap_after(2, *ready)
        for _, _, c, stage in order:
            got, *_ = lax.optimization_barrier((flight[c], *last))
            if stage == 0:
                own[c] = jnp.where(y == 0, 0.0, got)
                part[c] = send = kept[c] + got
                swap_after(c + 3, send)
            else:
                carry[c] = got if stage == 1 else carry[c] + got
                send = carry[c] + part[c]
            if stage < long - 1:
                flight[c] = hop(send, lambda at: at == stage, 1, reverse)
            else:
                send = jnp.where(y == 0, carry[c] + kept[c], carry[c])
                out[c] = (carry[c], own[c], lax.ppermute(send, "seq", swap))
            last = [send]
        return [out[c] for c in range(chunks)]

    def shards(queries, keys, values, out_grad, norm_gain):
        tokens, width = queries.shape
        heads = width // DH
        half = heads // 2
        per = half // CHUNKS
        wide = half * DH
        narrow = per * DH
        at_seq = lax.axis_index("seq")
        y = at_seq % 2
        place = y.astype(jnp.int32).reshape(1)
        turned = 1 - place
        gain = norm_gain.reshape(1, width)
        mac = 2 * GROUP * DH

        kept_half = lambda i, s: (0, s[0])
        sent_half = lambda i, s: (0, 1 - s[0])
        whole2 = lambda i, s: (0, 0)
        whole3 = lambda i, s: (0, 0, 0)

        def at_k(c):
            return lambda i, s: (0, s[0] * CHUNKS + c)

        def at_o(c):
            return lambda i, s: (0, (1 - s[0]) * CHUNKS + c)

        sent = call(
            functools.partial(states_body, per), place,
            [(a, (tokens, wide), sent_half, HBM) for a in (keys, values)],
            [((per, DH, DH), F32, (per, DH, DH), whole3, VMEM)] * CHUNKS,
            flops=half * mac * DH,
        )

        group = half // 2
        strip = lambda i, s: (0, (2 * s[0] + i) % 4)
        *kept, attn_local = call(
            functools.partial(local_body, per, CHUNKS, group), place,
            [(a, (tokens, group * DH), strip, HBM) for a in (queries, keys, values)],
            [((per, DH, DH), F32, (per, DH, DH), whole3, VMEM)] * CHUNKS + [
                ((tokens, width), F32, (tokens, group * DH), strip, VMEM),
            ],
            grid=(4,), flops=heads * mac * (2 * GROUP + DH // 2),
        )

        before = scan(kept, sent, y, False, [attn_local])

        block = (tokens, narrow)
        square = cross = None
        attns, priors = [], []
        for c in range(CHUNKS):
            e, r, other = before[c]
            first, last = c == 0, c == CHUNKS - 1
            ins = []
            for a in (attn_local, queries, out_grad):
                ins += [(a, block, at_k(c)), (a, block, at_o(c))]
            ins += [(gain, (1, narrow), at_k(c)), (gain, (1, narrow), at_o(c))]
            ins += [(a, (per, DH, DH), whole3) for a in (e, r, other)]
            if not first:
                ins += [(a, (GROUP, DH), whole2) for a in (square, cross)]
            outs = [(block, F32, block, whole2, VMEM)] * 2 + [((per, DH, DH), BF16, (per, DH, DH), whole3, VMEM)] * 2
            if last:
                outs += [((2, GROUP), F32, (2, GROUP), whole2)]
            else:
                outs += [((GROUP, DH), F32, (GROUP, DH), whole2)] * 2
            a_k, a_o, s_k, s_o, *stats = call(
                functools.partial(attn_body, per, first, last), place, ins, outs, flops=2 * per * mac * DH)
            attns.append((a_k, a_o))
            priors.append((s_k, s_o))
            if last:
                mine = stats[0]
            else:
                square, cross = stats

        sums = [mine]
        paired = parts & (parts - 1) == 0
        for step in range(1, parts):
            sums.append(lax.ppermute(
                mine, "head", [(i, i ^ step if paired else (i + step) % parts) for i in range(parts)]))

        def delta(which, index):
            ins = [(a, (2, GROUP), whole2) for a in sums]
            ins += [(attns[c][which], block, whole2) for c in range(CHUNKS)]
            ins += [(queries, (tokens, wide), index), (out_grad, (tokens, wide), index), (gain, (1, wide), index)]
            outs = [(block, BF16, block, whole2, VMEM)] * CHUNKS
            outs += [((per, DH, DH), F32, (per, DH, DH), whole3, VMEM)] * CHUNKS
            result = call(
                functools.partial(delta_body, per, CHUNKS, parts, float(parts * heads * DH)), place, ins, outs,
                flops=half * mac * DH)
            return result[:CHUNKS], result[CHUNKS:]

        d_o, sent = delta(1, sent_half)
        d_k, kept = delta(0, kept_half)

        def mine(c):
            return lambda i, s: (0, jnp.where(i == 0, s[0], 1 - s[0]) * CHUNKS + c)

        state3 = (per, DH, DH)
        qg = None
        for c in range(CHUNKS):
            ins = [(a, block, mine(c)) for a in (keys, values)]
            ins += [(a, block, whole2) for a in (d_k[c], d_o[c])]
            ins += [(a, state3, whole3) for a in priors[c]]
            aliases = {}
            if c > 0:
                aliases[len(ins) + 1] = 0
                ins.append((qg, None, None, HBM))
            qg, = call(
                functools.partial(query_body, per), place, ins, [((tokens, width), BF16, block, mine(c), HBM)],
                grid=(2,), aliases=aliases, flops=2 * per * mac * (2 * GROUP + DH))

        after = scan(kept, sent, 1 - y, True, [qg])

        grads = None
        turns = [(c, 0) for c in range(CHUNKS)] + [(c, 1) for c in range(CHUNKS)]
        for c, which in turns:
            index, d = ((at_k(c), d_k[c]), (at_o(c), d_o[c]))[which]
            states = after[c][2:] if which else after[c][:2]
            ins = [(a, block, index) for a in (queries, keys, values)]
            ins += [(d, block, whole2)] + [(a, state3, whole3) for a in states]
            aliases = {}
            if grads is not None:
                aliases = {len(ins) + 1: 0, len(ins) + 2: 1}
                ins += [(a, None, None, HBM) for a in grads]
            grads = call(
                functools.partial(final_body, per, len(states)), place, ins,
                [((tokens, width), BF16, block, index, HBM)] * 2,
                aliases=aliases, flops=per * mac * (4 * GROUP + 2 * DH))
        return qg, grads[0], grads[1]

    return jax.shard_map(
        shards,
        mesh=mesh,
        in_specs=(
            P("seq", "head"),
            P("seq", "head"),
            P("seq", "head"),
            P("seq", "head"),
            P("head"),
        ),
        out_specs=(P("seq", "head"), P("seq", "head"), P("seq", "head")),
        check_vma=False,
    )
```

```python
import functools

import jax
import jax.numpy as jnp
from jax import lax
from jax.experimental import pallas as pl
from jax.experimental.pallas import tpu as pltpu
from jax.sharding import PartitionSpec as P

DH = 128
GROUP = 256
CHUNKS = 4
EPS = 1e-05
F32 = jnp.float32
BF16 = jnp.bfloat16


def dot(a, b, ca, cb):
    return lax.dot_general(a, b, (((ca,), (cb,)), ((), ())), preferred_element_type=F32)


def head(ref, j):
    return ref[:, j * DH:(j + 1) * DH]


def causal(turned=False):
    rows = lax.broadcasted_iota(jnp.int32, (GROUP, GROUP), 0)
    cols = lax.broadcasted_iota(jnp.int32, (GROUP, GROUP), 1)
    return cols >= rows if turned else rows >= cols


def masked(scores, mask):
    return jnp.where(mask, scores, 0.0).astype(BF16)


HBM, VMEM = pltpu.HBM, pltpu.VMEM


def call(body, place, ins, outs, grid=(1,), aliases=None, grant=6):
    ins = [(*item, None)[:4] for item in ins]
    outs = [(*item, None)[:5] for item in outs]
    arrays = [pltpu.with_memory_space_constraint(a, m) if m else a for a, _, _, m in ins]
    return pl.pallas_call(
        body,
        grid_spec=pltpu.PrefetchScalarGridSpec(
            num_scalar_prefetch=1,
            grid=grid,
            in_specs=[pl.BlockSpec(b, m) if b else pl.BlockSpec(memory_space=pl.ANY) for _, b, m, _ in ins],
            out_specs=[pl.BlockSpec(b, m) for _, _, b, m, _ in outs],
        ),
        out_shape=[(m or jax.ShapeDtypeStruct)(s, d) for s, d, _, _, m in outs],
        input_output_aliases=aliases or {},
        compiler_params=pltpu.CompilerParams(vmem_limit_bytes=grant * 1024 * 1024),
        cost_estimate=pl.CostEstimate(flops=1024, bytes_accessed=1024, transcendentals=0),
    )(place, *arrays)


def states_body(per, place, a, b, *outs):
    for c, out in enumerate(outs):
        for j in range(per):
            h = c * per + j
            out[j] = dot(head(a, h), head(b, h), 0, 0)


def local_body(per, chunks, heads, place, q, k, v, *refs):
    outs, attn = refs[:chunks], refs[chunks]
    for turn in range(2):
        @pl.when(pl.program_id(0) == turn)
        def _():
            for j in range(heads):
                h = turn * heads + j
                outs[h // per][h % per] = dot(head(k, j), head(v, j), 0, 0)
    mask = causal()
    for j in range(heads):
        s = masked(dot(head(q, j), head(k, j), 1, 1), mask)
        attn[:, j * DH:(j + 1) * DH] = dot(s, head(v, j), 1, 0)


def attn_body(per, first, last, place, al_k, al_o, q_k, q_o, g_k, g_o, n_k, n_o, e, r, other, *refs):
    if not first:
        sq_in, cr_in, *refs = refs
    at_k, at_o, sb_k, sb_o, *stats = refs
    square = jnp.zeros((GROUP, DH), F32) if first else sq_in[...]
    cross = jnp.zeros((GROUP, DH), F32) if first else cr_in[...]
    for j in range(per):
        kept = (e[j] + r[j]).astype(BF16)
        sb_k[j] = kept
        sb_o[j] = other[j].astype(BF16)
        for al, q, g, n, sb, at in (
            (al_k, q_k, g_k, n_k, sb_k, at_k),
            (al_o, q_o, g_o, n_o, sb_o, at_o),
        ):
            x = head(al, j) + dot(head(q, j), sb[j], 1, 0)
            at[:, j * DH:(j + 1) * DH] = x
            scaled = head(n, j).astype(F32) * head(g, j).astype(F32)
            square = square + x * x
            cross = cross + scaled * x
    if last:
        stats[0][0:1] = jnp.sum(square.T, axis=0, keepdims=True)
        stats[0][1:2] = jnp.sum(cross.T, axis=0, keepdims=True)
    else:
        stats[0][...] = square
        stats[1][...] = cross


def delta_body(per, chunks, parts, features, place, *refs):
    stats = refs[:parts]
    attn = refs[parts:parts + chunks]
    q, g, n = refs[parts + chunks:parts + chunks + 3]
    outs = refs[parts + chunks + 3:]
    total = stats[0][...]
    for s in stats[1:]:
        total = total + s[...]
    inverse = lax.rsqrt(total[0:1] / features + EPS)
    slope = inverse * inverse * inverse * (total[1:2] / features)
    inverse = jnp.broadcast_to(inverse, (DH, GROUP)).T
    slope = jnp.broadcast_to(slope, (DH, GROUP)).T
    for c in range(chunks):
        for j in range(per):
            h = c * per + j
            scaled = head(n, h).astype(F32) * head(g, h).astype(F32)
            x = (inverse * scaled - head(attn[c], j) * slope).astype(BF16)
            outs[c][:, j * DH:(j + 1) * DH] = x
            outs[chunks + c][j] = dot(head(q, h), x, 0, 0)


def query_body(per, chunks, place, k, v, *refs):
    qg = refs[-1]
    mask = causal()
    for turn in range(2 * chunks):
        d, sb = refs[turn], refs[2 * chunks + turn]

        @pl.when(pl.program_id(0) == turn)
        def _():
            for j in range(per):
                do = head(d, j)
                ds = masked(dot(do, head(v, j), 1, 1), mask)
                qg[:, j * DH:(j + 1) * DH] = (dot(ds, head(k, j), 1, 0) + dot(do, sb[j], 1, 1)).astype(BF16)


def final_body(per, terms, place, q, k, v, d, *refs):
    later_in, kg, vg = refs[:terms], refs[-2], refs[-1]
    mask = causal(turned=True)
    for j in range(per):
        at = slice(j * DH, (j + 1) * DH)
        later = later_in[0][j]
        for term in later_in[1:]:
            later = later + term[j]
        later = later.astype(BF16)
        qj, kj, vj, do = head(q, j), head(k, j), head(v, j), head(d, j)
        ds = masked(dot(vj, do, 1, 1), mask)
        st = masked(dot(kj, qj, 1, 1), mask)
        kg[:, at] = (dot(ds, qj, 1, 0) + dot(vj, later, 1, 1)).astype(BF16)
        vg[:, at] = (dot(st, do, 1, 0) + dot(kj, later, 1, 0)).astype(BF16)


def solution(mesh):
    count = mesh.shape["seq"]
    parts = mesh.shape["head"]
    long = count // 2
    swap = [(i, i ^ 1) for i in range(count)]

    def hop(array, near, far, reverse):
        pairs = []
        for z in range(long):
            to = z + far
            if to < long and near(z):
                for y in range(2):
                    pairs.append((2 * z + y, 2 * to + y))
        if reverse:
            pairs = [(count - 1 - a, count - 1 - b) for a, b in pairs]
        return lax.ppermute(array, "seq", pairs)

    def shift(array, far, reverse):
        return hop(array, lambda at: True, far, reverse)

    def doubling(parts, reverse):
        out = []
        for part in parts:
            carry = shift(part, 1, reverse)
            far = 1
            while far < long:
                carry = carry + shift(carry, far, reverse)
                far *= 2
            out.append(carry)
        return out

    def scan(kept, sent, y, reverse, ready, beside):
        own = [None] * len(kept)
        if long > 4 or long < 2:
            swapped = [lax.ppermute(b, "seq", swap) for b in sent]
            own = [jnp.where(y == 0, 0.0, r) for r in swapped]
            sums = [a + r for a, r in zip(kept, swapped)]
            sums = doubling(sums, reverse) if long > 1 else [jnp.zeros_like(a) for a in sums]
            others = [
                lax.ppermute(jnp.where(y == 0, e + a, e), "seq", swap) for a, e in zip(kept, sums)
            ]
            return list(zip(sums, own, others))
        chunks = len(kept)
        order = sorted((2 * stage + c, -stage, c, stage) for stage in range(long) for c in range(chunks))
        part, flight, carry, out = {}, {}, {}, {}
        last = ready

        def swap_after(c, *things):
            if c < chunks:
                part_sent, *_ = lax.optimization_barrier((sent[c], *things))
                flight[c] = lax.ppermute(part_sent, "seq", swap)

        swap_after(0)
        swap_after(1)
        swap_after(2, *ready)
        for _, _, c, stage in order:
            if (stage, c) in beside:
                last = last + [beside[stage, c](out)]
            got, *_ = lax.optimization_barrier((flight[c], *last))
            if stage == 0:
                own[c] = jnp.where(y == 0, 0.0, got)
                part[c] = send = kept[c] + got
                swap_after(c + 3, send)
            else:
                carry[c] = got if stage == 1 else carry[c] + got
                send = carry[c] + part[c]
            if stage < long - 1:
                flight[c] = hop(send, lambda at: at == stage, 1, reverse)
            else:
                send = jnp.where(y == 0, carry[c] + kept[c], carry[c])
                out[c] = (carry[c], own[c], lax.ppermute(send, "seq", swap))
            last = [send]
        return [out[c] for c in range(chunks)]

    def shards(queries, keys, values, out_grad, norm_gain):
        tokens, width = queries.shape
        heads = width // DH
        half = heads // 2
        per = half // CHUNKS
        wide = half * DH
        narrow = per * DH
        at_seq = lax.axis_index("seq")
        y = at_seq % 2
        place = y.astype(jnp.int32).reshape(1)
        turned = 1 - place
        gain = norm_gain.reshape(1, width)

        kept_half = lambda i, s: (0, s[0])
        sent_half = lambda i, s: (0, 1 - s[0])
        whole2 = lambda i, s: (0, 0)
        whole3 = lambda i, s: (0, 0, 0)

        def at_k(c):
            return lambda i, s: (0, s[0] * CHUNKS + c)

        def at_o(c):
            return lambda i, s: (0, (1 - s[0]) * CHUNKS + c)

        sent = call(
            functools.partial(states_body, per), place,
            [(a, (tokens, wide), sent_half, HBM) for a in (keys, values)],
            [((per, DH, DH), F32, (per, DH, DH), whole3, VMEM)] * CHUNKS,
        )

        group = half // 2
        strip = lambda i, s: (0, (2 * s[0] + i) % 4)
        *kept, attn_local = call(
            functools.partial(local_body, per, CHUNKS, group), place,
            [(a, (tokens, group * DH), strip, HBM) for a in (queries, keys, values)],
            [((per, DH, DH), F32, (per, DH, DH), whole3, VMEM)] * CHUNKS + [
                ((tokens, width), F32, (tokens, group * DH), strip, HBM),
            ],
            grid=(4,),
        )

        before = scan(kept, sent, y, False, [attn_local], {})

        block = (tokens, narrow)
        square = cross = None
        attns, priors = [], []
        for c in range(CHUNKS):
            e, r, other = before[c]
            first, last = c == 0, c == CHUNKS - 1
            ins = []
            for a in (attn_local, queries, out_grad):
                ins += [(a, block, at_k(c)), (a, block, at_o(c))]
            ins += [(gain, (1, narrow), at_k(c)), (gain, (1, narrow), at_o(c))]
            ins += [(a, (per, DH, DH), whole3) for a in (e, r, other)]
            if not first:
                ins += [(a, (GROUP, DH), whole2) for a in (square, cross)]
            outs = [(block, F32, block, whole2, VMEM)] * 2 + [((per, DH, DH), BF16, (per, DH, DH), whole3, VMEM)] * 2
            if last:
                outs += [((2, GROUP), F32, (2, GROUP), whole2)]
            else:
                outs += [((GROUP, DH), F32, (GROUP, DH), whole2)] * 2
            a_k, a_o, s_k, s_o, *stats = call(
                functools.partial(attn_body, per, first, last), place, ins, outs)
            attns.append((a_k, a_o))
            priors.append((s_k, s_o))
            if last:
                mine = stats[0]
            else:
                square, cross = stats

        sums = [mine]
        paired = parts & (parts - 1) == 0
        for step in range(1, parts):
            sums.append(lax.ppermute(
                mine, "head", [(i, i ^ step if paired else (i + step) % parts) for i in range(parts)]))

        def delta(which, index):
            ins = [(a, (2, GROUP), whole2) for a in sums]
            ins += [(attns[c][which], block, whole2) for c in range(CHUNKS)]
            ins += [(queries, (tokens, wide), index), (out_grad, (tokens, wide), index), (gain, (1, wide), index)]
            outs = [(block, BF16, block, whole2, VMEM)] * CHUNKS
            outs += [((per, DH, DH), F32, (per, DH, DH), whole3, VMEM)] * CHUNKS
            result = call(
                functools.partial(delta_body, per, CHUNKS, parts, float(parts * heads * DH)), place, ins, outs)
            return result[:CHUNKS], result[CHUNKS:]

        d_o, sent = delta(1, sent_half)
        d_k, kept = delta(0, kept_half)

        def mine(c):
            return lambda i, s: (0, jnp.where(i % 2 == 0, s[0], 1 - s[0]) * CHUNKS + c + i // 2)

        state3 = (per, DH, DH)
        made = {"query": [], "rest": []}

        def query(c, count):
            ins = [(a, block, mine(c), HBM) for a in (keys, values)]
            some = range(c, c + count)
            ins += [(a, block, whole2) for i in some for a in (d_k[i], d_o[i])]
            ins += [(a, state3, whole3) for i in some for a in priors[i]]
            aliases = {}
            if made["query"]:
                aliases[len(ins) + 1] = 0
                ins += [(a, None, None, HBM) for a in made["query"]]
            made["query"] = call(
                functools.partial(query_body, per, count), place, ins,
                [((tokens, width), BF16, block, mine(c), HBM)], grid=(2 * count,), aliases=aliases)
            return made["query"][0]

        def rest(c, which, after):
            index, d = ((at_k(c), d_k[c]), (at_o(c), d_o[c]))[which]
            states = after[c][2:] if which else after[c][:2]
            ins = [(a, block, index, HBM) for a in (queries, keys, values)]
            ins += [(d, block, whole2)] + [(a, state3, whole3) for a in states]
            aliases = {}
            if made["rest"]:
                aliases = {len(ins) + 1: 0, len(ins) + 2: 1}
                ins += [(a, None, None, HBM) for a in made["rest"]]
            made["rest"] = call(
                functools.partial(final_body, per, len(states)), place, ins,
                [((tokens, width), BF16, block, index, HBM)] * 2,
                aliases=aliases)
            return made["rest"][0]

        tail = long - 1
        beside = {
            (1, 0): lambda out: query(2, 1),
            (2, 0): lambda out: query(3, 1),
            (tail, CHUNKS - 2): lambda out: rest(0, 0, out),
            (tail, CHUNKS - 1): lambda out: rest(1, 0, out),
        } if 2 < long <= 4 else {}
        after = scan(kept, sent, 1 - y, True, [query(0, 2)], beside)
        if not beside:
            query(2, 2)
        for c in range(2 if beside else 0, CHUNKS):
            rest(c, 0, after)
        for c in range(CHUNKS):
            rest(c, 1, after)
        return made["query"][0], made["rest"][0], made["rest"][1]

    return jax.shard_map(
        shards,
        mesh=mesh,
        in_specs=(
            P("seq", "head"),
            P("seq", "head"),
            P("seq", "head"),
            P("seq", "head"),
            P("head"),
        ),
        out_specs=(P("seq", "head"), P("seq", "head"), P("seq", "head")),
        check_vma=False,
    )
```

```python
import functools

import jax
import jax.numpy as jnp
from jax import lax
from jax.experimental import pallas as pl
from jax.experimental.pallas import tpu as pltpu
from jax.sharding import PartitionSpec as P

DH = 128
GROUP = 256
CHUNKS = 4
EPS = 1e-05
F32 = jnp.float32
BF16 = jnp.bfloat16


def dot(a, b, ca, cb):
    return lax.dot_general(a, b, (((ca,), (cb,)), ((), ())), preferred_element_type=F32)


def head(ref, j):
    return ref[:, j * DH:(j + 1) * DH]


def causal(turned=False):
    rows = lax.broadcasted_iota(jnp.int32, (GROUP, GROUP), 0)
    cols = lax.broadcasted_iota(jnp.int32, (GROUP, GROUP), 1)
    return cols >= rows if turned else rows >= cols


def masked(scores, mask):
    return jnp.where(mask, scores, 0.0).astype(BF16)


HBM, VMEM = pltpu.HBM, pltpu.VMEM


def call(body, place, ins, outs, grid=(1,), aliases=None, grant=8):
    ins = [(*item, None)[:4] for item in ins]
    outs = [(*item, None)[:5] for item in outs]
    arrays = [pltpu.with_memory_space_constraint(a, m) if m else a for a, _, _, m in ins]
    return pl.pallas_call(
        body,
        grid_spec=pltpu.PrefetchScalarGridSpec(
            num_scalar_prefetch=1,
            grid=grid,
            in_specs=[pl.BlockSpec(b, m) if b else pl.BlockSpec(memory_space=pl.ANY) for _, b, m, _ in ins],
            out_specs=[pl.BlockSpec(b, m) for _, _, b, m, _ in outs],
        ),
        out_shape=[(m or jax.ShapeDtypeStruct)(s, d) for s, d, _, _, m in outs],
        input_output_aliases=aliases or {},
        compiler_params=pltpu.CompilerParams(vmem_limit_bytes=grant * 1024 * 1024),
        cost_estimate=pl.CostEstimate(flops=1024, bytes_accessed=1024, transcendentals=0),
    )(place, *arrays)


def states_body(per, place, a, b, *outs):
    for c, out in enumerate(outs):
        for j in range(per):
            h = c * per + j
            out[j] = dot(head(a, h), head(b, h), 0, 0)


def local_body(per, chunks, heads, place, q, k, v, *refs):
    outs, attn = refs[:chunks], refs[chunks]
    for turn in range(2):
        @pl.when(pl.program_id(0) == turn)
        def _():
            for j in range(heads):
                h = turn * heads + j
                outs[h // per][h % per] = dot(head(k, j), head(v, j), 0, 0)
    mask = causal()
    for j in range(heads):
        s = masked(dot(head(q, j), head(k, j), 1, 1), mask)
        attn[:, j * DH:(j + 1) * DH] = dot(s, head(v, j), 1, 0)


def attn_body(per, first, last, place, al_k, al_o, q_k, q_o, g_k, g_o, n_k, n_o, e, r, other, *refs):
    one, two, *refs = refs
    if not first:
        sq_in, cr_in = one, two
    at_k, at_o, sb_k, sb_o, *stats = refs
    square = jnp.zeros((GROUP, DH), F32) if first else sq_in[...]
    cross = jnp.zeros((GROUP, DH), F32) if first else cr_in[...]
    for j in range(per):
        kept = (e[j] + r[j]).astype(BF16)
        sb_k[j] = kept
        sb_o[j] = other[j].astype(BF16)
        for al, q, g, n, sb, at in (
            (al_k, q_k, g_k, n_k, sb_k, at_k),
            (al_o, q_o, g_o, n_o, sb_o, at_o),
        ):
            x = head(al, j) + dot(head(q, j), sb[j], 1, 0)
            at[:, j * DH:(j + 1) * DH] = x
            scaled = head(n, j).astype(F32) * head(g, j).astype(F32)
            square = square + x * x
            cross = cross + scaled * x
    if last:
        stats[0][0:1] = jnp.sum(square.T, axis=0, keepdims=True)
        stats[0][1:2] = jnp.sum(cross.T, axis=0, keepdims=True)
    else:
        stats[0][...] = square
        stats[1][...] = cross


def delta_body(per, chunks, parts, features, place, *refs):
    stats = refs[:parts]
    attn = refs[parts:parts + chunks]
    q, g, n = refs[parts + chunks:parts + chunks + 3]
    outs = refs[parts + chunks + 3:]
    total = stats[0][...]
    for s in stats[1:]:
        total = total + s[...]
    inverse = lax.rsqrt(total[0:1] / features + EPS)
    slope = inverse * inverse * inverse * (total[1:2] / features)
    inverse = jnp.broadcast_to(inverse, (DH, GROUP)).T
    slope = jnp.broadcast_to(slope, (DH, GROUP)).T
    for c in range(chunks):
        for j in range(per):
            h = c * per + j
            scaled = head(n, h).astype(F32) * head(g, h).astype(F32)
            x = (inverse * scaled - head(attn[c], j) * slope).astype(BF16)
            outs[c][:, j * DH:(j + 1) * DH] = x
            outs[chunks + c][j] = dot(head(q, h), x, 0, 0)


def query_body(per, chunks, place, k, v, *refs):
    qg = refs[-1]
    mask = causal()
    for turn in range(2 * chunks):
        d, sb = refs[turn], refs[2 * chunks + turn]

        @pl.when(pl.program_id(0) == turn)
        def _():
            for j in range(per):
                do = head(d, j)
                ds = masked(dot(do, head(v, j), 1, 1), mask)
                qg[:, j * DH:(j + 1) * DH] = (dot(ds, head(k, j), 1, 0) + dot(do, sb[j], 1, 1)).astype(BF16)


def final_body(per, terms, place, q, k, v, d, *refs):
    later_in, kg, vg = refs[:terms], refs[-2], refs[-1]
    mask = causal(turned=True)
    for j in range(per):
        at = slice(j * DH, (j + 1) * DH)
        later = later_in[0][j]
        for term in later_in[1:]:
            later = later + term[j]
        later = later.astype(BF16)
        qj, kj, vj, do = head(q, j), head(k, j), head(v, j), head(d, j)
        ds = masked(dot(vj, do, 1, 1), mask)
        st = masked(dot(kj, qj, 1, 1), mask)
        kg[:, at] = (dot(ds, qj, 1, 0) + dot(vj, later, 1, 1)).astype(BF16)
        vg[:, at] = (dot(st, do, 1, 0) + dot(kj, later, 1, 0)).astype(BF16)


def solution(mesh):
    count = mesh.shape["seq"]
    parts = mesh.shape["head"]
    long = count // 2
    swap = [(i, i ^ 1) for i in range(count)]

    def hop(array, near, far, reverse):
        pairs = []
        for z in range(long):
            to = z + far
            if to < long and near(z):
                for y in range(2):
                    pairs.append((2 * z + y, 2 * to + y))
        if reverse:
            pairs = [(count - 1 - a, count - 1 - b) for a, b in pairs]
        return lax.ppermute(array, "seq", pairs)

    def shift(array, far, reverse):
        return hop(array, lambda at: True, far, reverse)

    def doubling(parts, reverse):
        out = []
        for part in parts:
            carry = shift(part, 1, reverse)
            far = 1
            while far < long:
                carry = carry + shift(carry, far, reverse)
                far *= 2
            out.append(carry)
        return out

    def scan(kept, sent, leads, reverse, ready, beside):
        own = [None] * len(kept)
        if long > 4 or long < 2:
            swapped = [lax.ppermute(b, "seq", swap) for b in sent]
            own = [jnp.where(leads, 0.0, r) for r in swapped]
            sums = [a + r for a, r in zip(kept, swapped)]
            sums = doubling(sums, reverse) if long > 1 else [jnp.zeros_like(a) for a in sums]
            others = [
                lax.ppermute(jnp.where(leads, e + a, e), "seq", swap) for a, e in zip(kept, sums)
            ]
            return list(zip(sums, own, others))
        chunks = len(kept)
        order = sorted((2 * stage + c, -stage, c, stage) for stage in range(long) for c in range(chunks))
        part, flight, carry, out = {}, {}, {}, {}
        last = ready

        def swap_after(c, *things):
            if c < chunks:
                part_sent, *_ = lax.optimization_barrier((sent[c], *things))
                flight[c] = lax.ppermute(part_sent, "seq", swap)

        swap_after(0)
        swap_after(1)
        swap_after(2, *ready)
        for _, _, c, stage in order:
            if (stage, c) in beside:
                last = last + [beside[stage, c](out)]
            got, *_ = lax.optimization_barrier((flight[c], *last))
            if stage == 0:
                own[c] = jnp.where(leads, 0.0, got)
                part[c] = send = kept[c] + got
                swap_after(c + 3, send)
            else:
                carry[c] = got if stage == 1 else carry[c] + got
                send = carry[c] + part[c]
            if stage < long - 1:
                flight[c] = hop(send, lambda at: at == stage, 1, reverse)
            else:
                send = jnp.where(leads, carry[c] + kept[c], carry[c])
                out[c] = (carry[c], own[c], lax.ppermute(send, "seq", swap))
            last = [send]
        return [out[c] for c in range(chunks)]

    def shards(queries, keys, values, out_grad, norm_gain):
        tokens, width = queries.shape
        heads = width // DH
        half = heads // 2
        per = half // CHUNKS
        wide = half * DH
        narrow = per * DH
        at_seq = lax.axis_index("seq")
        y = at_seq % 2
        place, leads, ends = lax.optimization_barrier((y.astype(jnp.int32).reshape(1), y == 0, y == 1))
        gain = norm_gain.reshape(1, width)

        kept_half = lambda i, s: (0, s[0])
        sent_half = lambda i, s: (0, 1 - s[0])
        whole2 = lambda i, s: (0, 0)
        whole3 = lambda i, s: (0, 0, 0)

        def at_k(c):
            return lambda i, s: (0, s[0] * CHUNKS + c)

        def at_o(c):
            return lambda i, s: (0, (1 - s[0]) * CHUNKS + c)

        sent = call(
            functools.partial(states_body, per), place,
            [(a, (tokens, wide), sent_half, HBM) for a in (keys, values)],
            [((per, DH, DH), F32, (per, DH, DH), whole3, VMEM)] * CHUNKS,
        )

        group = half // 2
        strip = lambda i, s: (0, (2 * s[0] + i) % 4)
        *kept, attn_local = call(
            functools.partial(local_body, per, CHUNKS, group), place,
            [(a, (tokens, group * DH), strip, HBM) for a in (queries, keys, values)],
            [((per, DH, DH), F32, (per, DH, DH), whole3, VMEM)] * CHUNKS + [
                ((tokens, width), F32, (tokens, group * DH), strip, VMEM),
            ],
            grid=(4,),
        )
        tail = long - 1
        spread = 2 < long <= 4
        before = scan(kept, sent, leads, False, [attn_local], {})

        block = (tokens, narrow)
        square = cross = None
        attns, priors = [], []
        for c in range(CHUNKS):
            e, r, other = before[c]
            first, last = c == 0, c == CHUNKS - 1
            ins = []
            for a in (attn_local, queries, out_grad):
                ins += [(a, block, at_k(c)), (a, block, at_o(c))]
            ins += [(gain, (1, narrow), at_k(c)), (gain, (1, narrow), at_o(c))]
            ins += [(a, (per, DH, DH), whole3) for a in (e, r, other)]
            if first:
                ins += [(a, None, None, VMEM) for a in (keys, values)]
            else:
                ins += [(a, (GROUP, DH), whole2) for a in (square, cross)]
            outs = [(block, F32, block, whole2, VMEM)] * 2 + [((per, DH, DH), BF16, (per, DH, DH), whole3, VMEM)] * 2
            if last:
                outs += [((2, GROUP), F32, (2, GROUP), whole2)]
            else:
                outs += [((GROUP, DH), F32, (GROUP, DH), whole2)] * 2
            a_k, a_o, s_k, s_o, *stats = call(
                functools.partial(attn_body, per, first, last), place, ins, outs)
            attns.append((a_k, a_o))
            priors.append((s_k, s_o))
            if last:
                mine = stats[0]
            else:
                square, cross = stats

        sums = [mine]
        paired = parts & (parts - 1) == 0
        for step in range(1, parts):
            sums.append(lax.ppermute(
                mine, "head", [(i, i ^ step if paired else (i + step) % parts) for i in range(parts)]))

        def delta(which, index):
            ins = [(a, (2, GROUP), whole2) for a in sums]
            ins += [(attns[c][which], block, whole2) for c in range(CHUNKS)]
            ins += [(queries, (tokens, wide), index), (out_grad, (tokens, wide), index), (gain, (1, wide), index)]
            outs = [(block, BF16, block, whole2, VMEM)] * CHUNKS
            outs += [((per, DH, DH), F32, (per, DH, DH), whole3, VMEM)] * CHUNKS
            result = call(
                functools.partial(delta_body, per, CHUNKS, parts, float(parts * heads * DH)), place, ins, outs)
            return result[:CHUNKS], result[CHUNKS:]

        d_o, sent = delta(1, sent_half)
        d_k, kept = delta(0, kept_half)

        def mine(c):
            return lambda i, s: (0, jnp.where(i % 2 == 0, s[0], 1 - s[0]) * CHUNKS + c + i // 2)

        state3 = (per, DH, DH)
        made = {"query": [], "rest": []}

        def query(c, count):
            ins = [(a, block, mine(c)) for a in (keys, values)]
            some = range(c, c + count)
            ins += [(a, block, whole2) for i in some for a in (d_k[i], d_o[i])]
            ins += [(a, state3, whole3) for i in some for a in priors[i]]
            aliases = {}
            if made["query"]:
                aliases[len(ins) + 1] = 0
                ins += [(a, None, None, HBM) for a in made["query"]]
            made["query"] = call(
                functools.partial(query_body, per, count), place, ins,
                [((tokens, width), BF16, block, mine(c), HBM)], grid=(2 * count,), aliases=aliases)
            return made["query"][0]

        def rest(c, which, after):
            index, d = ((at_k(c), d_k[c]), (at_o(c), d_o[c]))[which]
            states = after[c][2:] if which else after[c][:2]
            ins = [(a, block, index) for a in (queries, keys, values)]
            ins += [(d, block, whole2)] + [(a, state3, whole3) for a in states]
            aliases = {}
            if made["rest"]:
                aliases = {len(ins) + 1: 0, len(ins) + 2: 1}
                ins += [(a, None, None, HBM) for a in made["rest"]]
            made["rest"] = call(
                functools.partial(final_body, per, len(states)), place, ins,
                [((tokens, width), BF16, block, index, HBM)] * 2,
                aliases=aliases)
            return made["rest"][0]

        beside = {
            (1, 0): lambda out: query(2, 1),
            (2, 0): lambda out: query(3, 1),
            (tail, CHUNKS - 2): lambda out: rest(0, 0, out),
            (tail, CHUNKS - 1): lambda out: rest(1, 0, out),
        } if spread else {}
        after = scan(kept, sent, ends, True, [query(0, 2)], beside)
        if not beside:
            query(2, 2)
        for c in range(2 if beside else 0, CHUNKS):
            rest(c, 0, after)
        for c in range(CHUNKS):
            rest(c, 1, after)
        return made["query"][0], made["rest"][0], made["rest"][1]

    return jax.shard_map(
        shards,
        mesh=mesh,
        in_specs=(
            P("seq", "head"),
            P("seq", "head"),
            P("seq", "head"),
            P("seq", "head"),
            P("head"),
        ),
        out_specs=(P("seq", "head"), P("seq", "head"), P("seq", "head")),
        check_vma=False,
    )
```

```python
import functools

import jax
import jax.numpy as jnp
from jax import lax
from jax.experimental import pallas as pl
from jax.experimental.pallas import tpu as pltpu
from jax.sharding import PartitionSpec as P

DH = 128
GROUP = 256
CHUNKS = 4
EPS = 1e-05
F32 = jnp.float32
BF16 = jnp.bfloat16


def dot(a, b, ca, cb):
    return lax.dot_general(a, b, (((ca,), (cb,)), ((), ())), preferred_element_type=F32)


def head(ref, j):
    return ref[:, j * DH:(j + 1) * DH]


def causal(turned=False):
    rows = lax.broadcasted_iota(jnp.int32, (GROUP, GROUP), 0)
    cols = lax.broadcasted_iota(jnp.int32, (GROUP, GROUP), 1)
    return cols >= rows if turned else rows >= cols


def masked(scores, mask):
    return jnp.where(mask, scores, 0.0).astype(BF16)


HBM, VMEM = pltpu.HBM, pltpu.VMEM


def call(body, place, ins, outs, grid=(1,), aliases=None, grant=8):
    ins = [(*item, None)[:4] for item in ins]
    outs = [(*item, None)[:5] for item in outs]
    arrays = [pltpu.with_memory_space_constraint(a, m) if m else a for a, _, _, m in ins]
    return pl.pallas_call(
        body,
        grid_spec=pltpu.PrefetchScalarGridSpec(
            num_scalar_prefetch=1,
            grid=grid,
            in_specs=[pl.BlockSpec(b, m) if b else pl.BlockSpec(memory_space=pl.ANY) for _, b, m, _ in ins],
            out_specs=[pl.BlockSpec(b, m) for _, _, b, m, _ in outs],
        ),
        out_shape=[(m or jax.ShapeDtypeStruct)(s, d) for s, d, _, _, m in outs],
        input_output_aliases=aliases or {},
        compiler_params=pltpu.CompilerParams(vmem_limit_bytes=grant * 1024 * 1024),
        cost_estimate=pl.CostEstimate(flops=1024, bytes_accessed=1024, transcendentals=0),
    )(place, *arrays)


def states_body(per, place, a, b, *outs):
    for c, out in enumerate(outs):
        for j in range(per):
            h = c * per + j
            out[j] = dot(head(a, h), head(b, h), 0, 0)


def local_body(per, chunks, heads, place, q, k, v, *refs):
    outs, attn = refs[:chunks], refs[chunks]
    for turn in range(2):
        @pl.when(pl.program_id(0) == turn)
        def _():
            for j in range(heads):
                h = turn * heads + j
                outs[h // per][h % per] = dot(head(k, j), head(v, j), 0, 0)
    mask = causal()
    scores = [dot(head(q, j), head(k, j), 1, 1) for j in range(heads)]
    scores = [masked(s, mask) for s in scores]
    for j, s in enumerate(scores):
        attn[:, j * DH:(j + 1) * DH] = dot(s, head(v, j), 1, 0)


def attn_body(per, first, last, place, al_k, al_o, q_k, q_o, g_k, g_o, n_k, n_o, e, r, other, *refs):
    one, two, *refs = refs
    if not first:
        sq_in, cr_in = one, two
    at_k, at_o, sb_k, sb_o, *stats = refs
    square = jnp.zeros((GROUP, DH), F32) if first else sq_in[...]
    cross = jnp.zeros((GROUP, DH), F32) if first else cr_in[...]
    for j in range(per):
        kept = (e[j] + r[j]).astype(BF16)
        sb_k[j] = kept
        sb_o[j] = other[j].astype(BF16)
        for al, q, g, n, sb, at in (
            (al_k, q_k, g_k, n_k, sb_k, at_k),
            (al_o, q_o, g_o, n_o, sb_o, at_o),
        ):
            x = head(al, j) + dot(head(q, j), sb[j], 1, 0)
            at[:, j * DH:(j + 1) * DH] = x
            scaled = head(n, j).astype(F32) * head(g, j).astype(F32)
            square = square + x * x
            cross = cross + scaled * x
    if last:
        stats[0][0:1] = jnp.sum(square.T, axis=0, keepdims=True)
        stats[0][1:2] = jnp.sum(cross.T, axis=0, keepdims=True)
    else:
        stats[0][...] = square
        stats[1][...] = cross


def delta_body(per, chunks, parts, features, place, *refs):
    stats = refs[:parts]
    attn = refs[parts:parts + chunks]
    q, g, n = refs[parts + chunks:parts + chunks + 3]
    outs = refs[parts + chunks + 3:]
    total = stats[0][...]
    for s in stats[1:]:
        total = total + s[...]
    inverse = lax.rsqrt(total[0:1] / features + EPS)
    slope = inverse * inverse * inverse * (total[1:2] / features)
    inverse = jnp.broadcast_to(inverse, (DH, GROUP)).T
    slope = jnp.broadcast_to(slope, (DH, GROUP)).T
    for c in range(chunks):
        for j in range(per):
            h = c * per + j
            scaled = head(n, h).astype(F32) * head(g, h).astype(F32)
            x = (inverse * scaled - head(attn[c], j) * slope).astype(BF16)
            outs[c][:, j * DH:(j + 1) * DH] = x
            outs[chunks + c][j] = dot(head(q, h), x, 0, 0)


def query_body(per, chunks, place, k, v, *refs):
    qg = refs[-1]
    mask = causal()
    for turn in range(2 * chunks):
        d, sb = refs[turn], refs[2 * chunks + turn]

        @pl.when(pl.program_id(0) == turn)
        def _():
            first = [dot(head(d, j), head(v, j), 1, 1) for j in range(per)]
            prior = [dot(head(d, j), sb[j], 1, 1) for j in range(per)]
            first = [masked(s, mask) for s in first]
            for j, s in enumerate(first):
                qg[:, j * DH:(j + 1) * DH] = (dot(s, head(k, j), 1, 0) + prior[j]).astype(BF16)


def final_body(per, chunks, terms, place, q, k, v, *refs):
    ds, later_in, kg, vg = refs[:chunks], refs[chunks:chunks + chunks * terms], refs[-2], refs[-1]
    mask = causal(turned=True)
    heads = range(chunks * per)

    def later(h):
        state = later_in[h // per * terms][h % per]
        for n in range(1, terms):
            state = state + later_in[h // per * terms + n][h % per]
        return state.astype(BF16)

    outer = [head(ds[h // per], h % per) for h in heads]
    grad = [dot(head(v, h), outer[h], 1, 1) for h in heads]
    score = [dot(head(k, h), head(q, h), 1, 1) for h in heads]
    states = [later(h) for h in heads]
    kg_part = [dot(head(v, h), states[h], 1, 1) for h in heads]
    vg_part = [dot(head(k, h), states[h], 1, 0) for h in heads]
    grad = [masked(x, mask) for x in grad]
    score = [masked(x, mask) for x in score]
    for h in heads:
        at = slice(h * DH, (h + 1) * DH)
        kg[:, at] = (dot(grad[h], head(q, h), 1, 0) + kg_part[h]).astype(BF16)
        vg[:, at] = (dot(score[h], outer[h], 1, 0) + vg_part[h]).astype(BF16)


def solution(mesh):
    count = mesh.shape["seq"]
    parts = mesh.shape["head"]
    long = count // 2
    swap = [(i, i ^ 1) for i in range(count)]

    def hop(array, near, far, reverse):
        pairs = []
        for z in range(long):
            to = z + far
            if to < long and near(z):
                for y in range(2):
                    pairs.append((2 * z + y, 2 * to + y))
        if reverse:
            pairs = [(count - 1 - a, count - 1 - b) for a, b in pairs]
        return lax.ppermute(array, "seq", pairs)

    def shift(array, far, reverse):
        return hop(array, lambda at: True, far, reverse)

    def doubling(parts, reverse):
        out = []
        for part in parts:
            carry = shift(part, 1, reverse)
            far = 1
            while far < long:
                carry = carry + shift(carry, far, reverse)
                far *= 2
            out.append(carry)
        return out

    def scan(kept, sent, leads, reverse, ready, beside):
        own = [None] * len(kept)
        if long > 4 or long < 2:
            swapped = [lax.ppermute(b, "seq", swap) for b in sent]
            own = [jnp.where(leads, 0.0, r) for r in swapped]
            sums = [a + r for a, r in zip(kept, swapped)]
            sums = doubling(sums, reverse) if long > 1 else [jnp.zeros_like(a) for a in sums]
            others = [
                lax.ppermute(jnp.where(leads, e + a, e), "seq", swap) for a, e in zip(kept, sums)
            ]
            return list(zip(sums, own, others))
        chunks = len(kept)
        order = sorted((2 * stage + c, -stage, c, stage) for stage in range(long) for c in range(chunks))
        part, flight, carry, out = {}, {}, {}, {}
        last = ready

        def swap_after(c, *things):
            if c < chunks:
                part_sent, *_ = lax.optimization_barrier((sent[c], *things))
                flight[c] = lax.ppermute(part_sent, "seq", swap)

        swap_after(0)
        swap_after(1)
        swap_after(2, *ready)
        for _, _, c, stage in order:
            if (stage, c) in beside:
                last = last + [beside[stage, c](out)]
            got, *_ = lax.optimization_barrier((flight[c], *last))
            if stage == 0:
                own[c] = jnp.where(leads, 0.0, got)
                part[c] = send = kept[c] + got
                swap_after(c + 3, send)
            else:
                carry[c] = got if stage == 1 else carry[c] + got
                send = carry[c] + part[c]
            if stage < long - 1:
                flight[c] = hop(send, lambda at: at == stage, 1, reverse)
            else:
                send = jnp.where(leads, carry[c] + kept[c], carry[c])
                out[c] = (carry[c], own[c], lax.ppermute(send, "seq", swap))
            last = [send]
        return [out[c] for c in range(chunks)]

    def shards(queries, keys, values, out_grad, norm_gain):
        tokens, width = queries.shape
        heads = width // DH
        half = heads // 2
        per = half // CHUNKS
        wide = half * DH
        narrow = per * DH
        at_seq = lax.axis_index("seq")
        y = at_seq % 2
        place, leads, ends = lax.optimization_barrier((y.astype(jnp.int32).reshape(1), y == 0, y == 1))
        gain = norm_gain.reshape(1, width)

        kept_half = lambda i, s: (0, s[0])
        sent_half = lambda i, s: (0, 1 - s[0])
        whole2 = lambda i, s: (0, 0)
        whole3 = lambda i, s: (0, 0, 0)

        def at_k(c):
            return lambda i, s: (0, s[0] * CHUNKS + c)

        def at_o(c):
            return lambda i, s: (0, (1 - s[0]) * CHUNKS + c)

        sent = call(
            functools.partial(states_body, per), place,
            [(a, (tokens, wide), sent_half, HBM) for a in (keys, values)],
            [((per, DH, DH), F32, (per, DH, DH), whole3, VMEM)] * CHUNKS,
        )

        group = half // 2
        strip = lambda i, s: (0, (2 * s[0] + i) % 4)
        *kept, attn_local = call(
            functools.partial(local_body, per, CHUNKS, group), place,
            [(a, (tokens, group * DH), strip, HBM) for a in (queries, keys, values)],
            [((per, DH, DH), F32, (per, DH, DH), whole3, VMEM)] * CHUNKS + [
                ((tokens, width), F32, (tokens, group * DH), strip, VMEM),
            ],
            grid=(4,),
        )
        tail = long - 1
        spread = 2 < long <= 4
        before = scan(kept, sent, leads, False, [attn_local], {})

        block = (tokens, narrow)
        square = cross = None
        attns, priors = [], []
        for c in range(CHUNKS):
            e, r, other = before[c]
            first, last = c == 0, c == CHUNKS - 1
            ins = []
            for a in (attn_local, queries, out_grad):
                ins += [(a, block, at_k(c)), (a, block, at_o(c))]
            ins += [(gain, (1, narrow), at_k(c)), (gain, (1, narrow), at_o(c))]
            ins += [(a, (per, DH, DH), whole3) for a in (e, r, other)]
            if first:
                ins += [(a, None, None, VMEM) for a in (keys, values)]
            else:
                ins += [(a, (GROUP, DH), whole2) for a in (square, cross)]
            outs = [(block, F32, block, whole2, VMEM)] * 2 + [((per, DH, DH), BF16, (per, DH, DH), whole3, VMEM)] * 2
            if last:
                outs += [((2, GROUP), F32, (2, GROUP), whole2)]
            else:
                outs += [((GROUP, DH), F32, (GROUP, DH), whole2)] * 2
            a_k, a_o, s_k, s_o, *stats = call(
                functools.partial(attn_body, per, first, last), place, ins, outs)
            attns.append((a_k, a_o))
            priors.append((s_k, s_o))
            if last:
                mine = stats[0]
            else:
                square, cross = stats

        sums = [mine]
        paired = parts & (parts - 1) == 0
        for step in range(1, parts):
            sums.append(lax.ppermute(
                mine, "head", [(i, i ^ step if paired else (i + step) % parts) for i in range(parts)]))

        def delta(which, index):
            ins = [(a, (2, GROUP), whole2) for a in sums]
            ins += [(attns[c][which], block, whole2) for c in range(CHUNKS)]
            ins += [(queries, (tokens, wide), index), (out_grad, (tokens, wide), index), (gain, (1, wide), index)]
            outs = [(block, BF16, block, whole2, VMEM)] * CHUNKS
            outs += [((per, DH, DH), F32, (per, DH, DH), whole3, VMEM)] * CHUNKS
            result = call(
                functools.partial(delta_body, per, CHUNKS, parts, float(parts * heads * DH)), place, ins, outs)
            return result[:CHUNKS], result[CHUNKS:]

        d_o, sent = delta(1, sent_half)
        d_k, kept = delta(0, kept_half)

        def mine(c):
            return lambda i, s: (0, jnp.where(i % 2 == 0, s[0], 1 - s[0]) * CHUNKS + c + i // 2)

        state3 = (per, DH, DH)
        made = {"query": [], "rest": []}

        def query(c, count):
            ins = [(a, block, mine(c)) for a in (keys, values)]
            some = range(c, c + count)
            ins += [(a, block, whole2) for i in some for a in (d_k[i], d_o[i])]
            ins += [(a, state3, whole3) for i in some for a in priors[i]]
            aliases = {}
            if made["query"]:
                aliases[len(ins) + 1] = 0
                ins += [(a, None, None, HBM) for a in made["query"]]
            made["query"] = call(
                functools.partial(query_body, per, count), place, ins,
                [((tokens, width), BF16, block, mine(c), HBM)], grid=(2 * count,), aliases=aliases)
            return made["query"][0]

        def rest(c, which, after, count=1):
            steps = CHUNKS // count
            index = lambda i, s: (0, (1 - s[0] if which else s[0]) * steps + c // count)
            wider = (tokens, narrow * count)
            some = range(c, c + count)
            states = [a for i in some for a in (after[i][2:] if which else after[i][:2])]
            ins = [(a, wider, index) for a in (queries, keys, values)]
            ins += [((d_o if which else d_k)[i], block, whole2) for i in some]
            ins += [(a, state3, whole3) for a in states]
            aliases = {}
            if made["rest"]:
                aliases = {len(ins) + 1: 0, len(ins) + 2: 1}
                ins += [(a, None, None, HBM) for a in made["rest"]]
            made["rest"] = call(
                functools.partial(final_body, per, count, len(states) // count), place, ins,
                [((tokens, width), BF16, wider, index, HBM)] * 2, aliases=aliases)
            return made["rest"][0]

        beside = {
            (tail, 0): lambda out: query(1, 1),
            (tail, 1): lambda out: query(2, 1),
            (tail, CHUNKS - 2): lambda out: query(3, 1),
            (tail, CHUNKS - 1): lambda out: rest(0, 0, out, 2),
        } if spread else {}
        after = scan(kept, sent, ends, True, [query(0, 1)], beside)
        if not spread:
            query(1, 3)
            rest(0, 0, after, 2)
        rest(2, 0, after, 2)
        for c in range(CHUNKS):
            rest(c, 1, after)
        return made["query"][0], made["rest"][0], made["rest"][1]

    return jax.shard_map(
        shards,
        mesh=mesh,
        in_specs=(
            P("seq", "head"),
            P("seq", "head"),
            P("seq", "head"),
            P("seq", "head"),
            P("head"),
        ),
        out_specs=(P("seq", "head"), P("seq", "head"), P("seq", "head")),
        check_vma=False,
    )
```

```python
import functools

import jax
import jax.numpy as jnp
from jax import lax
from jax.experimental import pallas as pl
from jax.experimental.pallas import tpu as pltpu
from jax.sharding import PartitionSpec as P

DH = 128
GROUP = 256
CHUNKS = 4
EPS = 1e-05
F32 = jnp.float32
BF16 = jnp.bfloat16


def dot(a, b, ca, cb):
    return lax.dot_general(a, b, (((ca,), (cb,)), ((), ())), preferred_element_type=F32)


def head(ref, j):
    return ref[:, j * DH:(j + 1) * DH]


def causal(turned=False):
    rows = lax.broadcasted_iota(jnp.int32, (GROUP, GROUP), 0)
    cols = lax.broadcasted_iota(jnp.int32, (GROUP, GROUP), 1)
    return cols >= rows if turned else rows >= cols


def masked(scores, mask):
    return jnp.where(mask, scores, 0.0).astype(BF16)


HBM, VMEM = pltpu.HBM, pltpu.VMEM


def call(body, place, ins, outs, grid=(1,), aliases=None, grant=8):
    ins = [(*item, None)[:4] for item in ins]
    outs = [(*item, None)[:5] for item in outs]
    arrays = [pltpu.with_memory_space_constraint(a, m) if m else a for a, _, _, m in ins]
    return pl.pallas_call(
        body,
        grid_spec=pltpu.PrefetchScalarGridSpec(
            num_scalar_prefetch=1,
            grid=grid,
            in_specs=[pl.BlockSpec(b, m) if b else pl.BlockSpec(memory_space=pl.ANY) for _, b, m, _ in ins],
            out_specs=[pl.BlockSpec(b, m) for _, _, b, m, _ in outs],
        ),
        out_shape=[(m or jax.ShapeDtypeStruct)(s, d) for s, d, _, _, m in outs],
        input_output_aliases=aliases or {},
        compiler_params=pltpu.CompilerParams(vmem_limit_bytes=grant * 1024 * 1024),
        cost_estimate=pl.CostEstimate(flops=1024, bytes_accessed=1024, transcendentals=0),
    )(place, *arrays)


def states_body(per, place, a, b, *outs):
    for c, out in enumerate(outs):
        for j in range(per):
            h = c * per + j
            out[j] = dot(head(a, h), head(b, h), 0, 0)


def local_body(per, chunks, heads, place, q, k, v, *refs):
    outs, attn = refs[:chunks], refs[chunks]
    for turn in range(2):
        @pl.when(pl.program_id(0) == turn)
        def _():
            for j in range(heads):
                h = turn * heads + j
                outs[h // per][h % per] = dot(head(k, j), head(v, j), 0, 0)
    mask = causal()
    scores = [dot(head(q, j), head(k, j), 1, 1) for j in range(heads)]
    scores = [masked(s, mask) for s in scores]
    for j, s in enumerate(scores):
        attn[:, j * DH:(j + 1) * DH] = dot(s, head(v, j), 1, 0)


def attn_body(per, first, last, place, al_k, al_o, q_k, q_o, g_k, g_o, n_k, n_o, e, r, other, *refs):
    one, two, *refs = refs
    if not first:
        sq_in, cr_in = one, two
    at_k, at_o, sb_k, sb_o, *stats = refs
    square = jnp.zeros((GROUP, DH), F32) if first else sq_in[...]
    cross = jnp.zeros((GROUP, DH), F32) if first else cr_in[...]
    for j in range(per):
        kept = (e[j] + r[j]).astype(BF16)
        sb_k[j] = kept
        sb_o[j] = other[j].astype(BF16)
        for al, q, g, n, sb, at in (
            (al_k, q_k, g_k, n_k, sb_k, at_k),
            (al_o, q_o, g_o, n_o, sb_o, at_o),
        ):
            x = head(al, j) + dot(head(q, j), sb[j], 1, 0)
            at[:, j * DH:(j + 1) * DH] = x
            scaled = head(n, j).astype(F32) * head(g, j).astype(F32)
            square = square + x * x
            cross = cross + scaled * x
    if last:
        stats[0][0:1] = jnp.sum(square.T, axis=0, keepdims=True)
        stats[0][1:2] = jnp.sum(cross.T, axis=0, keepdims=True)
    else:
        stats[0][...] = square
        stats[1][...] = cross


def delta_body(per, chunks, parts, features, place, *refs):
    stats = refs[:parts]
    attn = refs[parts:parts + chunks]
    q, g, n = refs[parts + chunks:parts + chunks + 3]
    outs = refs[parts + chunks + 3:]
    total = stats[0][...]
    for s in stats[1:]:
        total = total + s[...]
    inverse = lax.rsqrt(total[0:1] / features + EPS)
    slope = inverse * inverse * inverse * (total[1:2] / features)
    inverse = jnp.broadcast_to(inverse, (DH, GROUP)).T
    slope = jnp.broadcast_to(slope, (DH, GROUP)).T
    for c in range(chunks):
        for j in range(per):
            h = c * per + j
            scaled = head(n, h).astype(F32) * head(g, h).astype(F32)
            x = (inverse * scaled - head(attn[c], j) * slope).astype(BF16)
            outs[c][:, j * DH:(j + 1) * DH] = x
            outs[chunks + c][j] = dot(head(q, h), x, 0, 0)


def query_body(per, chunks, place, k, v, *refs):
    qg = refs[-1]
    mask = causal()
    for turn in range(2 * chunks):
        d, sb = refs[turn], refs[2 * chunks + turn]

        @pl.when(pl.program_id(0) == turn)
        def _():
            first = [dot(head(d, j), head(v, j), 1, 1) for j in range(per)]
            prior = [dot(head(d, j), sb[j], 1, 1) for j in range(per)]
            first = [masked(s, mask) for s in first]
            for j, s in enumerate(first):
                qg[:, j * DH:(j + 1) * DH] = (dot(s, head(k, j), 1, 0) + prior[j]).astype(BF16)


def final_body(per, chunks, terms, place, q, k, v, *refs):
    ds, later_in, kg, vg = refs[:chunks], refs[chunks:chunks + chunks * terms], refs[-2], refs[-1]
    mask = causal(turned=True)
    heads = range(chunks * per)

    def later(h):
        state = later_in[h // per * terms][h % per]
        for n in range(1, terms):
            state = state + later_in[h // per * terms + n][h % per]
        return state.astype(BF16)

    outer = [head(ds[h // per], h % per) for h in heads]
    grad = [dot(head(v, h), outer[h], 1, 1) for h in heads]
    score = [dot(head(k, h), head(q, h), 1, 1) for h in heads]
    states = [later(h) for h in heads]
    kg_part = [dot(head(v, h), states[h], 1, 1) for h in heads]
    vg_part = [dot(head(k, h), states[h], 1, 0) for h in heads]
    grad = [masked(x, mask) for x in grad]
    score = [masked(x, mask) for x in score]
    for h in heads:
        at = slice(h * DH, (h + 1) * DH)
        kg[:, at] = (dot(grad[h], head(q, h), 1, 0) + kg_part[h]).astype(BF16)
        vg[:, at] = (dot(score[h], outer[h], 1, 0) + vg_part[h]).astype(BF16)


def solution(mesh):
    count = mesh.shape["seq"]
    parts = mesh.shape["head"]
    long = count // 2
    swap = [(i, i ^ 1) for i in range(count)]

    def hop(array, near, far, reverse):
        pairs = []
        for z in range(long):
            to = z + far
            if to < long and near(z):
                for y in range(2):
                    pairs.append((2 * z + y, 2 * to + y))
        if reverse:
            pairs = [(count - 1 - a, count - 1 - b) for a, b in pairs]
        return lax.ppermute(array, "seq", pairs)

    def shift(array, far, reverse):
        return hop(array, lambda at: True, far, reverse)

    def doubling(parts, reverse):
        out = []
        for part in parts:
            carry = shift(part, 1, reverse)
            far = 1
            while far < long:
                carry = carry + shift(carry, far, reverse)
                far *= 2
            out.append(carry)
        return out

    def scan(kept, sent, leads, reverse, ready, beside):
        own = [None] * len(kept)
        if long > 4 or long < 2:
            swapped = [lax.ppermute(b, "seq", swap) for b in sent]
            own = [jnp.where(leads, 0.0, r) for r in swapped]
            sums = [a + r for a, r in zip(kept, swapped)]
            sums = doubling(sums, reverse) if long > 1 else [jnp.zeros_like(a) for a in sums]
            others = [
                lax.ppermute(jnp.where(leads, e + a, e), "seq", swap) for a, e in zip(kept, sums)
            ]
            return list(zip(sums, own, others))
        chunks = len(kept)
        order = sorted((2 * stage + c, stage, c) for stage in range(long) for c in range(chunks))
        part, flight, carry, out = {}, {}, {}, {}
        last = ready

        def swap_after(c, *things):
            if c < chunks:
                part_sent, *_ = lax.optimization_barrier((sent[c], *things))
                flight[c] = lax.ppermute(part_sent, "seq", swap)

        swap_after(0)
        swap_after(1)
        swap_after(2)
        for _, stage, c in order:
            if (stage, c) in beside:
                last = last + [beside[stage, c](out)]
            got, *_ = lax.optimization_barrier((flight[c], *last))
            if stage == 0:
                own[c] = jnp.where(leads, 0.0, got)
                part[c] = send = kept[c] + got
                swap_after(c + 3, send)
            else:
                carry[c] = got if stage == 1 else carry[c] + got
                send = carry[c] + part[c]
            if stage < long - 1:
                flight[c] = hop(send, lambda at: at == stage, 1, reverse)
            else:
                send = jnp.where(leads, carry[c] + kept[c], carry[c])
                out[c] = (carry[c], own[c], lax.ppermute(send, "seq", swap))
            last = [send]
        return [out[c] for c in range(chunks)]

    def shards(queries, keys, values, out_grad, norm_gain):
        tokens, width = queries.shape
        heads = width // DH
        half = heads // 2
        per = half // CHUNKS
        wide = half * DH
        narrow = per * DH
        at_seq = lax.axis_index("seq")
        y = at_seq % 2
        place, leads, ends = lax.optimization_barrier((y.astype(jnp.int32).reshape(1), y == 0, y == 1))
        gain = norm_gain.reshape(1, width)

        whole2 = lambda i, s: (0, 0)
        whole3 = lambda i, s: (0, 0, 0)

        def at_k(c):
            return lambda i, s: (0, s[0] * CHUNKS + c)

        def at_o(c):
            return lambda i, s: (0, (1 - s[0]) * CHUNKS + c)

        some = CHUNKS // 2
        sent = []
        for n in range(2):
            sent += call(
                functools.partial(states_body, per), place,
                [(a, (tokens, wide // 2), lambda i, s: (0, 2 * (1 - s[0]) + n), HBM) for a in (keys, values)],
                [((per, DH, DH), F32, (per, DH, DH), whole3, VMEM)] * some,
            )

        group = half // 2
        strip = lambda i, s: (0, (2 * s[0] + i) % 4)
        *kept, attn_local = call(
            functools.partial(local_body, per, CHUNKS, group), place,
            [(a, (tokens, group * DH), strip, HBM) for a in (queries, keys, values)],
            [((per, DH, DH), F32, (per, DH, DH), whole3, VMEM)] * CHUNKS + [
                ((tokens, width), F32, (tokens, group * DH), strip, VMEM),
            ],
            grid=(4,),
        )
        tail = long - 1
        spread = 2 < long <= 4
        before = scan(kept, sent, leads, False, [attn_local], {})

        block = (tokens, narrow)
        square = cross = None
        attns, priors = [], []
        for c in range(CHUNKS):
            e, r, other = before[c]
            first, last = c == 0, c == CHUNKS - 1
            ins = []
            for a in (attn_local, queries, out_grad):
                ins += [(a, block, at_k(c)), (a, block, at_o(c))]
            ins += [(gain, (1, narrow), at_k(c)), (gain, (1, narrow), at_o(c))]
            ins += [(a, (per, DH, DH), whole3) for a in (e, r, other)]
            if first:
                ins += [(a, None, None, VMEM) for a in (keys, values)]
            else:
                ins += [(a, (GROUP, DH), whole2) for a in (square, cross)]
            outs = [(block, F32, block, whole2, VMEM)] * 2 + [((per, DH, DH), BF16, (per, DH, DH), whole3, VMEM)] * 2
            if last:
                outs += [((2, GROUP), F32, (2, GROUP), whole2)]
            else:
                outs += [((GROUP, DH), F32, (GROUP, DH), whole2)] * 2
            a_k, a_o, s_k, s_o, *stats = call(
                functools.partial(attn_body, per, first, last), place, ins, outs)
            attns.append((a_k, a_o))
            priors.append((s_k, s_o))
            if last:
                mine = stats[0]
            else:
                square, cross = stats

        sums = [mine]
        paired = parts & (parts - 1) == 0
        for step in range(1, parts):
            sums.append(lax.ppermute(
                mine, "head", [(i, i ^ step if paired else (i + step) % parts) for i in range(parts)]))

        def delta(which, first, count):
            span = count * narrow
            index = lambda i, s: (0, (1 - s[0] if which else s[0]) * (CHUNKS // count) + first // count)
            ins = [(a, (2, GROUP), whole2) for a in sums]
            ins += [(attns[c][which], block, whole2) for c in range(first, first + count)]
            ins += [(queries, (tokens, span), index), (out_grad, (tokens, span), index), (gain, (1, span), index)]
            outs = [(block, BF16, block, whole2, VMEM)] * count
            outs += [((per, DH, DH), F32, (per, DH, DH), whole3, VMEM)] * count
            result = call(
                functools.partial(delta_body, per, count, parts, float(parts * heads * DH)), place, ins, outs)
            return result[:count], result[count:]

        d_one, sent_one = delta(1, 0, some)
        d_two, sent_two = delta(1, some, some)
        d_o, sent = d_one + d_two, sent_one + sent_two
        d_k, kept = delta(0, 0, CHUNKS)

        def mine(c):
            return lambda i, s: (0, jnp.where(i % 2 == 0, s[0], 1 - s[0]) * CHUNKS + c + i // 2)

        state3 = (per, DH, DH)
        made = {"query": [], "rest": []}

        def query(c, count):
            ins = [(a, block, mine(c)) for a in (keys, values)]
            some = range(c, c + count)
            ins += [(a, block, whole2) for i in some for a in (d_k[i], d_o[i])]
            ins += [(a, state3, whole3) for i in some for a in priors[i]]
            aliases = {}
            if made["query"]:
                aliases[len(ins) + 1] = 0
                ins += [(a, None, None, HBM) for a in made["query"]]
            made["query"] = call(
                functools.partial(query_body, per, count), place, ins,
                [((tokens, width), BF16, block, mine(c), HBM)], grid=(2 * count,), aliases=aliases)
            return made["query"][0]

        def rest(c, which, after, count=1):
            steps = CHUNKS // count
            index = lambda i, s: (0, (1 - s[0] if which else s[0]) * steps + c // count)
            wider = (tokens, narrow * count)
            some = range(c, c + count)
            states = [a for i in some for a in (after[i][2:] if which else after[i][:2])]
            ins = [(a, wider, index) for a in (queries, keys, values)]
            ins += [((d_o if which else d_k)[i], block, whole2) for i in some]
            ins += [(a, state3, whole3) for a in states]
            aliases = {}
            if made["rest"]:
                aliases = {len(ins) + 1: 0, len(ins) + 2: 1}
                ins += [(a, None, None, HBM) for a in made["rest"]]
            made["rest"] = call(
                functools.partial(final_body, per, count, len(states) // count), place, ins,
                [((tokens, width), BF16, wider, index, HBM)] * 2, aliases=aliases)
            return made["rest"][0]

        beside = {
            (2, 0): lambda out: query(1, 1),
            (tail, 0): lambda out: query(2, 1),
            (tail, 1): lambda out: query(3, 1),
            (tail, CHUNKS - 1): lambda out: rest(0, 0, out, 2),
        } if spread else {}
        after = scan(kept, sent, ends, True, [query(0, 1)], beside)
        if not spread:
            query(1, 3)
            rest(0, 0, after, 2)
        rest(2, 0, after, 2)
        for c in range(CHUNKS):
            rest(c, 1, after)
        return made["query"][0], made["rest"][0], made["rest"][1]

    return jax.shard_map(
        shards,
        mesh=mesh,
        in_specs=(
            P("seq", "head"),
            P("seq", "head"),
            P("seq", "head"),
            P("seq", "head"),
            P("head"),
        ),
        out_specs=(P("seq", "head"), P("seq", "head"), P("seq", "head")),
        check_vma=False,
    )
```

```python
import functools

import jax
import jax.numpy as jnp
from jax import lax
from jax.experimental import pallas as pl
from jax.experimental.pallas import tpu as pltpu
from jax.sharding import PartitionSpec as P

DH = 128
GROUP = 256
CHUNKS = 4
EPS = 1e-05
F32 = jnp.float32
BF16 = jnp.bfloat16


def dot(a, b, ca, cb):
    return lax.dot_general(a, b, (((ca,), (cb,)), ((), ())), preferred_element_type=F32)


def head(ref, j):
    return ref[:, j * DH:(j + 1) * DH]


def causal(turned=False):
    rows = lax.broadcasted_iota(jnp.int32, (GROUP, GROUP), 0)
    cols = lax.broadcasted_iota(jnp.int32, (GROUP, GROUP), 1)
    return cols >= rows if turned else rows >= cols


def masked(scores, mask):
    return jnp.where(mask, scores, 0.0).astype(BF16)


HBM, VMEM = pltpu.HBM, pltpu.VMEM


def call(body, place, ins, outs, grid=(1,), aliases=None, grant=8):
    ins = [(*item, None)[:4] for item in ins]
    outs = [(*item, None)[:5] for item in outs]
    arrays = [pltpu.with_memory_space_constraint(a, m) if m else a for a, _, _, m in ins]
    return pl.pallas_call(
        body,
        grid_spec=pltpu.PrefetchScalarGridSpec(
            num_scalar_prefetch=1,
            grid=grid,
            in_specs=[pl.BlockSpec(b, m) if b else pl.BlockSpec(memory_space=pl.ANY) for _, b, m, _ in ins],
            out_specs=[pl.BlockSpec(b, m) for _, _, b, m, _ in outs],
        ),
        out_shape=[(m or jax.ShapeDtypeStruct)(s, d) for s, d, _, _, m in outs],
        input_output_aliases=aliases or {},
        compiler_params=pltpu.CompilerParams(vmem_limit_bytes=grant * 1024 * 1024),
        cost_estimate=pl.CostEstimate(flops=1024, bytes_accessed=1024, transcendentals=0),
    )(place, *arrays)


def states_body(per, place, a, b, *outs):
    for c, out in enumerate(outs):
        for j in range(per):
            h = c * per + j
            out[j] = dot(head(a, h), head(b, h), 0, 0)


def local_body(per, chunks, heads, place, q, k, v, *refs):
    outs, attn = refs[:chunks], refs[chunks]
    for turn in range(2):
        @pl.when(pl.program_id(0) == turn)
        def _():
            for j in range(heads):
                h = turn * heads + j
                outs[h // per][h % per] = dot(head(k, j), head(v, j), 0, 0)
    mask = causal()
    scores = [dot(head(q, j), head(k, j), 1, 1) for j in range(heads)]
    scores = [masked(s, mask) for s in scores]
    for j, s in enumerate(scores):
        attn[:, j * DH:(j + 1) * DH] = dot(s, head(v, j), 1, 0)


def attn_body(per, first, last, place, al_k, al_o, q_k, q_o, g_k, g_o, n_k, n_o, e, r, other, *refs):
    one, two, *refs = refs
    if not first:
        sq_in, cr_in = one, two
    at_k, at_o, sb_k, sb_o, *stats = refs
    square = jnp.zeros((GROUP, DH), F32) if first else sq_in[...]
    cross = jnp.zeros((GROUP, DH), F32) if first else cr_in[...]
    for j in range(per):
        kept = (e[j] + r[j]).astype(BF16)
        sb_k[j] = kept
        sb_o[j] = other[j].astype(BF16)
        for al, q, g, n, sb, at in (
            (al_k, q_k, g_k, n_k, sb_k, at_k),
            (al_o, q_o, g_o, n_o, sb_o, at_o),
        ):
            x = head(al, j) + dot(head(q, j), sb[j], 1, 0)
            at[:, j * DH:(j + 1) * DH] = x
            scaled = head(n, j).astype(F32) * head(g, j).astype(F32)
            square = square + x * x
            cross = cross + scaled * x
    if last:
        stats[0][0:1] = jnp.sum(square.T, axis=0, keepdims=True)
        stats[0][1:2] = jnp.sum(cross.T, axis=0, keepdims=True)
    else:
        stats[0][...] = square
        stats[1][...] = cross


def delta_body(per, chunks, parts, features, place, *refs):
    stats = refs[:parts]
    attn = refs[parts:parts + chunks]
    q, g, n = refs[parts + chunks:parts + chunks + 3]
    outs = refs[parts + chunks + 3:]
    total = stats[0][...]
    for s in stats[1:]:
        total = total + s[...]
    inverse = lax.rsqrt(total[0:1] / features + EPS)
    slope = inverse * inverse * inverse * (total[1:2] / features)
    inverse = jnp.broadcast_to(inverse, (DH, GROUP)).T
    slope = jnp.broadcast_to(slope, (DH, GROUP)).T
    for c in range(chunks):
        for j in range(per):
            h = c * per + j
            scaled = head(n, h).astype(F32) * head(g, h).astype(F32)
            x = (inverse * scaled - head(attn[c], j) * slope).astype(BF16)
            outs[c][:, j * DH:(j + 1) * DH] = x
            outs[chunks + c][j] = dot(head(q, h), x, 0, 0)


def query_body(per, chunks, place, k, v, *refs):
    qg = refs[-1]
    mask = causal()
    for turn in range(2 * chunks):
        d, sb = refs[turn], refs[2 * chunks + turn]

        @pl.when(pl.program_id(0) == turn)
        def _():
            first = [dot(head(d, j), head(v, j), 1, 1) for j in range(per)]
            prior = [dot(head(d, j), sb[j], 1, 1) for j in range(per)]
            first = [masked(s, mask) for s in first]
            for j, s in enumerate(first):
                qg[:, j * DH:(j + 1) * DH] = (dot(s, head(k, j), 1, 0) + prior[j]).astype(BF16)


def final_body(per, chunks, terms, place, q, k, v, *refs):
    ds, later_in, kg, vg = refs[:chunks], refs[chunks:chunks + chunks * terms], refs[-2], refs[-1]
    mask = causal(turned=True)
    heads = range(chunks * per)

    def later(h):
        state = later_in[h // per * terms][h % per]
        for n in range(1, terms):
            state = state + later_in[h // per * terms + n][h % per]
        return state.astype(BF16)

    outer = [head(ds[h // per], h % per) for h in heads]
    grad = [dot(head(v, h), outer[h], 1, 1) for h in heads]
    score = [dot(head(k, h), head(q, h), 1, 1) for h in heads]
    states = [later(h) for h in heads]
    kg_part = [dot(head(v, h), states[h], 1, 1) for h in heads]
    vg_part = [dot(head(k, h), states[h], 1, 0) for h in heads]
    grad = [masked(x, mask) for x in grad]
    score = [masked(x, mask) for x in score]
    for h in heads:
        at = slice(h * DH, (h + 1) * DH)
        kg[:, at] = (dot(grad[h], head(q, h), 1, 0) + kg_part[h]).astype(BF16)
        vg[:, at] = (dot(score[h], outer[h], 1, 0) + vg_part[h]).astype(BF16)


def solution(mesh):
    count = mesh.shape["seq"]
    parts = mesh.shape["head"]
    long = count // 2
    swap = [(i, i ^ 1) for i in range(count)]

    def hop(array, near, far, reverse):
        pairs = []
        for z in range(long):
            to = z + far
            if to < long and near(z):
                for y in range(2):
                    pairs.append((2 * z + y, 2 * to + y))
        if reverse:
            pairs = [(count - 1 - a, count - 1 - b) for a, b in pairs]
        return lax.ppermute(array, "seq", pairs)

    def shift(array, far, reverse):
        return hop(array, lambda at: True, far, reverse)

    def doubling(parts, reverse):
        out = []
        for part in parts:
            carry = shift(part, 1, reverse)
            far = 1
            while far < long:
                carry = carry + shift(carry, far, reverse)
                far *= 2
            out.append(carry)
        return out

    def scan(kept, sent, leads, reverse, ready, beside):
        own = [None] * len(kept)
        if long > 4 or long < 2:
            swapped = [lax.ppermute(b, "seq", swap) for b in sent]
            own = [jnp.where(leads, 0.0, r) for r in swapped]
            sums = [a + r for a, r in zip(kept, swapped)]
            sums = doubling(sums, reverse) if long > 1 else [jnp.zeros_like(a) for a in sums]
            others = [
                lax.ppermute(jnp.where(leads, e + a, e), "seq", swap) for a, e in zip(kept, sums)
            ]
            return list(zip(sums, own, others))
        chunks = len(kept)
        order = sorted((2 * stage + c, stage, c) for stage in range(long) for c in range(chunks))
        part, flight, carry, out, sends = {}, {}, {}, {}, {}
        last = ready

        def swap_after(c, *things):
            if c < chunks:
                part_sent, *_ = lax.optimization_barrier((sent[c], *things))
                flight[c] = lax.ppermute(part_sent, "seq", swap)

        swap_after(0)
        swap_after(1)
        swap_after(2)
        for _, stage, c in order:
            if (stage, c) in beside:
                last = last + [beside[stage, c](out, sends)]
            got, *_ = lax.optimization_barrier((flight[c], *last))
            if stage == 0:
                own[c] = jnp.where(leads, 0.0, got)
                part[c] = send = kept[c] + got
                swap_after(c + 3, send)
            else:
                carry[c] = got if stage == 1 else carry[c] + got
                send = carry[c] + part[c]
            if stage < long - 1:
                flight[c] = hop(send, lambda at: at == stage, 1, reverse)
            else:
                send = jnp.where(leads, carry[c] + kept[c], carry[c])
                out[c] = (carry[c], own[c], lax.ppermute(send, "seq", swap))
            last = [send]
            sends[stage, c] = send
        return [out[c] for c in range(chunks)]

    def shards(queries, keys, values, out_grad, norm_gain):
        tokens, width = queries.shape
        heads = width // DH
        half = heads // 2
        per = half // CHUNKS
        wide = half * DH
        narrow = per * DH
        at_seq = lax.axis_index("seq")
        y = at_seq % 2
        place, leads, ends = lax.optimization_barrier((y.astype(jnp.int32).reshape(1), y == 0, y == 1))
        gain = norm_gain.reshape(1, width)

        whole2 = lambda i, s: (0, 0)
        whole3 = lambda i, s: (0, 0, 0)

        def at_k(c):
            return lambda i, s: (0, s[0] * CHUNKS + c)

        def at_o(c):
            return lambda i, s: (0, (1 - s[0]) * CHUNKS + c)

        some = CHUNKS // 2
        sent = []
        for n in range(2):
            sent += call(
                functools.partial(states_body, per), place,
                [(a, (tokens, wide // 2), lambda i, s: (0, 2 * (1 - s[0]) + n), HBM) for a in (keys, values)],
                [((per, DH, DH), F32, (per, DH, DH), whole3, VMEM)] * some,
            )

        group = half // 2
        strip = lambda i, s: (0, (2 * s[0] + i) % 4)
        *kept, attn_local = call(
            functools.partial(local_body, per, CHUNKS, group), place,
            [(a, (tokens, group * DH), strip, HBM) for a in (queries, keys, values)],
            [((per, DH, DH), F32, (per, DH, DH), whole3, VMEM)] * CHUNKS + [
                ((tokens, width), F32, (tokens, group * DH), strip, VMEM),
            ],
            grid=(4,),
        )
        tail = long - 1
        spread = 2 < long <= 4
        before = scan(kept, sent, leads, False, [attn_local], {})

        block = (tokens, narrow)
        square = cross = None
        attns, priors = [], []
        for c in range(CHUNKS):
            e, r, other = before[c]
            first, last = c == 0, c == CHUNKS - 1
            ins = []
            for a in (attn_local, queries, out_grad):
                ins += [(a, block, at_k(c)), (a, block, at_o(c))]
            ins += [(gain, (1, narrow), at_k(c)), (gain, (1, narrow), at_o(c))]
            ins += [(a, (per, DH, DH), whole3) for a in (e, r, other)]
            if first:
                ins += [(a, None, None, VMEM) for a in (keys, values)]
            else:
                ins += [(a, (GROUP, DH), whole2) for a in (square, cross)]
            outs = [(block, F32, block, whole2, VMEM)] * 2 + [((per, DH, DH), BF16, (per, DH, DH), whole3, VMEM)] * 2
            if last:
                outs += [((2, GROUP), F32, (2, GROUP), whole2)]
            else:
                outs += [((GROUP, DH), F32, (GROUP, DH), whole2)] * 2
            a_k, a_o, s_k, s_o, *stats = call(
                functools.partial(attn_body, per, first, last), place, ins, outs)
            attns.append((a_k, a_o))
            priors.append((s_k, s_o))
            if last:
                mine = stats[0]
            else:
                square, cross = stats

        sums = [mine]
        paired = parts & (parts - 1) == 0
        for step in range(1, parts):
            sums.append(lax.ppermute(
                mine, "head", [(i, i ^ step if paired else (i + step) % parts) for i in range(parts)]))

        def delta(which, first, count):
            span = count * narrow
            index = lambda i, s: (0, (1 - s[0] if which else s[0]) * (CHUNKS // count) + first // count)
            ins = [(a, (2, GROUP), whole2) for a in sums]
            ins += [(attns[c][which], block, whole2) for c in range(first, first + count)]
            ins += [(queries, (tokens, span), index), (out_grad, (tokens, span), index), (gain, (1, span), index)]
            outs = [(block, BF16, block, whole2, VMEM)] * count
            outs += [((per, DH, DH), F32, (per, DH, DH), whole3, VMEM)] * count
            result = call(
                functools.partial(delta_body, per, count, parts, float(parts * heads * DH)), place, ins, outs)
            return result[:count], result[count:]

        d_one, sent_one = delta(1, 0, some)
        d_two, sent_two = delta(1, some, some)
        d_o, sent = d_one + d_two, sent_one + sent_two
        d_k, kept = delta(0, 0, CHUNKS)

        def mine(c):
            return lambda i, s: (0, jnp.where(i % 2 == 0, s[0], 1 - s[0]) * CHUNKS + c + i // 2)

        state3 = (per, DH, DH)
        made = {"query": [], "rest": []}

        def query(c, count, tie=None):
            ins = [(a, block, mine(c)) for a in (keys, values)]
            some = range(c, c + count)
            grads = [a for i in some for a in (d_k[i], d_o[i])]
            if tie is not None:
                grads[0], _ = lax.optimization_barrier((grads[0], tie))
            ins += [(a, block, whole2) for a in grads]
            ins += [(a, state3, whole3) for i in some for a in priors[i]]
            aliases = {}
            if made["query"]:
                aliases[len(ins) + 1] = 0
                ins += [(a, None, None, HBM) for a in made["query"]]
            made["query"] = call(
                functools.partial(query_body, per, count), place, ins,
                [((tokens, width), BF16, block, mine(c), HBM)], grid=(2 * count,), aliases=aliases)
            return made["query"][0]

        def rest(c, which, after, count=1):
            steps = CHUNKS // count
            index = lambda i, s: (0, (1 - s[0] if which else s[0]) * steps + c // count)
            wider = (tokens, narrow * count)
            some = range(c, c + count)
            states = [a for i in some for a in (after[i][2:] if which else after[i][:2])]
            ins = [(a, wider, index) for a in (queries, keys, values)]
            ins += [((d_o if which else d_k)[i], block, whole2) for i in some]
            ins += [(a, state3, whole3) for a in states]
            aliases = {}
            if made["rest"]:
                aliases = {len(ins) + 1: 0, len(ins) + 2: 1}
                ins += [(a, None, None, HBM) for a in made["rest"]]
            made["rest"] = call(
                functools.partial(final_body, per, count, len(states) // count), place, ins,
                [((tokens, width), BF16, wider, index, HBM)] * 2, aliases=aliases)
            return made["rest"][0]

        beside = {
            (2, 0): lambda out, sends: query(0, 2, sends[1, 1]),
            (tail, 0): lambda out, sends: query(2, 1, sends[2, 1]),
            (tail, 1): lambda out, sends: query(3, 1),
            (tail, 2): lambda out, sends: rest(0, 0, out, 2),
            (tail, 3): lambda out, sends: rest(2, 0, out),
        } if spread else {}
        after = scan(kept, sent, ends, True, [], beside)
        if not spread:
            query(0, CHUNKS)
            rest(0, 0, after, 2)
            rest(2, 0, after)
        rest(3, 0, after)
        rest(0, 1, after, 2)
        rest(2, 1, after)
        rest(3, 1, after)
        return made["query"][0], made["rest"][0], made["rest"][1]

    return jax.shard_map(
        shards,
        mesh=mesh,
        in_specs=(
            P("seq", "head"),
            P("seq", "head"),
            P("seq", "head"),
            P("seq", "head"),
            P("head"),
        ),
        out_specs=(P("seq", "head"), P("seq", "head"), P("seq", "head")),
        check_vma=False,
    )
```

```python
import functools

import jax
import jax.numpy as jnp
from jax import lax
from jax.experimental import pallas as pl
from jax.experimental.pallas import tpu as pltpu
from jax.sharding import PartitionSpec as P

DH = 128
GROUP = 256
CHUNKS = 4
EPS = 1e-05
F32 = jnp.float32
BF16 = jnp.bfloat16


def dot(a, b, ca, cb):
    return lax.dot_general(a, b, (((ca,), (cb,)), ((), ())), preferred_element_type=F32)


def head(ref, j):
    return ref[:, j * DH:(j + 1) * DH]


def causal(turned=False):
    rows = lax.broadcasted_iota(jnp.int32, (GROUP, GROUP), 0)
    cols = lax.broadcasted_iota(jnp.int32, (GROUP, GROUP), 1)
    return cols >= rows if turned else rows >= cols


def masked(scores, mask):
    return jnp.where(mask, scores, 0.0).astype(BF16)


HBM, VMEM = pltpu.HBM, pltpu.VMEM


def call(body, place, ins, outs, grid=(1,), aliases=None, grant=8):
    ins = [(*item, None)[:4] for item in ins]
    outs = [(*item, None)[:5] for item in outs]
    arrays = [pltpu.with_memory_space_constraint(a, m) if m else a for a, _, _, m in ins]
    return pl.pallas_call(
        body,
        grid_spec=pltpu.PrefetchScalarGridSpec(
            num_scalar_prefetch=1,
            grid=grid,
            in_specs=[pl.BlockSpec(b, m) if b else pl.BlockSpec(memory_space=pl.ANY) for _, b, m, _ in ins],
            out_specs=[pl.BlockSpec(b, m) for _, _, b, m, _ in outs],
        ),
        out_shape=[(m or jax.ShapeDtypeStruct)(s, d) for s, d, _, _, m in outs],
        input_output_aliases=aliases or {},
        compiler_params=pltpu.CompilerParams(vmem_limit_bytes=grant * 1024 * 1024),
        cost_estimate=pl.CostEstimate(flops=1024, bytes_accessed=1024, transcendentals=0),
    )(place, *arrays)


def states_body(per, place, a, b, *outs):
    for c, out in enumerate(outs):
        for j in range(per):
            h = c * per + j
            out[j] = dot(head(a, h), head(b, h), 0, 0)


def local_body(per, chunks, heads, place, q, k, v, *refs):
    outs, attn = refs[-1 - chunks:-1], refs[-1]
    for turn in range(chunks * per // heads):
        @pl.when(pl.program_id(0) == turn)
        def _():
            for j in range(heads):
                h = turn * heads + j
                outs[h // per][h % per] = dot(head(k, j), head(v, j), 0, 0)
    mask = causal()
    scores = [dot(head(q, j), head(k, j), 1, 1) for j in range(heads)]
    scores = [masked(s, mask) for s in scores]
    for j, s in enumerate(scores):
        attn[:, j * DH:(j + 1) * DH] = dot(s, head(v, j), 1, 0)


def attn_body(per, first, last, place, al_k, al_o, q_k, q_o, g_k, g_o, n_k, n_o, e, r, other, *refs):
    one, two, *refs = refs
    if not first:
        sq_in, cr_in = one, two
    at_k, at_o, sb_k, sb_o, *stats = refs
    square = jnp.zeros((GROUP, DH), F32) if first else sq_in[...]
    cross = jnp.zeros((GROUP, DH), F32) if first else cr_in[...]
    for j in range(per):
        kept = (e[j] + r[j]).astype(BF16)
        sb_k[j] = kept
        sb_o[j] = other[j].astype(BF16)
        for al, q, g, n, sb, at in (
            (al_k, q_k, g_k, n_k, sb_k, at_k),
            (al_o, q_o, g_o, n_o, sb_o, at_o),
        ):
            x = head(al, j) + dot(head(q, j), sb[j], 1, 0)
            at[:, j * DH:(j + 1) * DH] = x
            scaled = head(n, j).astype(F32) * head(g, j).astype(F32)
            square = square + x * x
            cross = cross + scaled * x
    if last:
        stats[0][0:1] = jnp.sum(square.T, axis=0, keepdims=True)
        stats[0][1:2] = jnp.sum(cross.T, axis=0, keepdims=True)
    else:
        stats[0][...] = square
        stats[1][...] = cross


def delta_body(per, chunks, parts, features, place, *refs):
    stats = refs[:parts]
    attn = refs[parts:parts + chunks]
    q, g, n = refs[parts + chunks:parts + chunks + 3]
    outs = refs[parts + chunks + 3:]
    total = stats[0][...]
    for s in stats[1:]:
        total = total + s[...]
    inverse = lax.rsqrt(total[0:1] / features + EPS)
    slope = inverse * inverse * inverse * (total[1:2] / features)
    inverse = jnp.broadcast_to(inverse, (DH, GROUP)).T
    slope = jnp.broadcast_to(slope, (DH, GROUP)).T
    for c in range(chunks):
        for j in range(per):
            h = c * per + j
            scaled = head(n, h).astype(F32) * head(g, h).astype(F32)
            x = (inverse * scaled - head(attn[c], j) * slope).astype(BF16)
            outs[c][:, j * DH:(j + 1) * DH] = x
            outs[chunks + c][j] = dot(head(q, h), x, 0, 0)


def column(ref, base, h):
    return ref[:, pl.ds(pl.multiple_of(base + h * DH, DH), DH)]


def query_body(per, half, first, chunks, place, k, v, *refs):
    qg = refs[-1]
    mask = causal()
    for turn in range(2 * chunks):
        d, sb = refs[turn], refs[2 * chunks + turn]
        base = (1 - place[0] if turn % 2 else place[0]) * half * DH + (first + turn // 2) * per * DH

        @pl.when(pl.program_id(0) == turn)
        def _():
            scores = [dot(head(d, j), column(v, base, j), 1, 1) for j in range(per)]
            prior = [dot(head(d, j), sb[j], 1, 1) for j in range(per)]
            scores = [masked(s, mask) for s in scores]
            for j, s in enumerate(scores):
                qg[:, j * DH:(j + 1) * DH] = (dot(s, column(k, base, j), 1, 0) + prior[j]).astype(BF16)


def final_body(per, half, first, other, chunks, terms, place, q, k, v, *refs):
    ds, later_in, kg, vg = refs[:chunks], refs[chunks:chunks + chunks * terms], refs[-2], refs[-1]
    mask = causal(turned=True)
    heads = range(chunks * per)
    base = (1 - place[0] if other else place[0]) * half * DH + first * per * DH

    def later(h):
        state = later_in[h // per * terms][h % per]
        for n in range(1, terms):
            state = state + later_in[h // per * terms + n][h % per]
        return state.astype(BF16)

    outer = [head(ds[h // per], h % per) for h in heads]
    qs, ks, vs = ([column(a, base, h) for h in heads] for a in (q, k, v))
    grad = [dot(vs[h], outer[h], 1, 1) for h in heads]
    score = [dot(ks[h], qs[h], 1, 1) for h in heads]
    states = [later(h) for h in heads]
    kg_part = [dot(vs[h], states[h], 1, 1) for h in heads]
    vg_part = [dot(ks[h], states[h], 1, 0) for h in heads]
    grad = [masked(x, mask) for x in grad]
    score = [masked(x, mask) for x in score]
    for h in heads:
        at = slice(h * DH, (h + 1) * DH)
        kg[:, at] = (dot(grad[h], qs[h], 1, 0) + kg_part[h]).astype(BF16)
        vg[:, at] = (dot(score[h], outer[h], 1, 0) + vg_part[h]).astype(BF16)


def solution(mesh):
    count = mesh.shape["seq"]
    parts = mesh.shape["head"]
    long = count // 2
    swap = [(i, i ^ 1) for i in range(count)]

    def hop(array, near, far, reverse):
        pairs = []
        for z in range(long):
            to = z + far
            if to < long and near(z):
                for y in range(2):
                    pairs.append((2 * z + y, 2 * to + y))
        if reverse:
            pairs = [(count - 1 - a, count - 1 - b) for a, b in pairs]
        return lax.ppermute(array, "seq", pairs)

    def shift(array, far, reverse):
        return hop(array, lambda at: True, far, reverse)

    def doubling(parts, reverse):
        out = []
        for part in parts:
            carry = shift(part, 1, reverse)
            far = 1
            while far < long:
                carry = carry + shift(carry, far, reverse)
                far *= 2
            out.append(carry)
        return out

    def scan(kept, sent, leads, reverse, ready, beside):
        own = [None] * len(kept)
        if long > 4 or long < 2:
            swapped = [lax.ppermute(b, "seq", swap) for b in sent]
            own = [jnp.where(leads, 0.0, r) for r in swapped]
            sums = [a + r for a, r in zip(kept, swapped)]
            sums = doubling(sums, reverse) if long > 1 else [jnp.zeros_like(a) for a in sums]
            others = [
                lax.ppermute(jnp.where(leads, e + a, e), "seq", swap) for a, e in zip(kept, sums)
            ]
            return list(zip(sums, own, others))
        chunks = len(kept)
        order = sorted((2 * stage + c, stage, c) for stage in range(long) for c in range(chunks))
        part, flight, carry, out, sends = {}, {}, {}, {}, {}
        last = ready

        def swap_after(c, *things):
            if c < chunks:
                part_sent, *_ = lax.optimization_barrier((sent[c], *things))
                flight[c] = lax.ppermute(part_sent, "seq", swap)

        swap_after(0)
        swap_after(1)
        swap_after(2)
        for _, stage, c in order:
            if (stage, c) in beside:
                last = last + [beside[stage, c](out, sends)]
            got, *_ = lax.optimization_barrier((flight[c], *last))
            if stage == 0:
                own[c] = jnp.where(leads, 0.0, got)
                part[c] = send = kept[c] + got
                swap_after(c + 3, send)
            else:
                carry[c] = got if stage == 1 else carry[c] + got
                send = carry[c] + part[c]
            if stage < long - 1:
                flight[c] = hop(send, lambda at: at == stage, 1, reverse)
            else:
                send = jnp.where(leads, carry[c] + kept[c], carry[c])
                out[c] = (carry[c], own[c], lax.ppermute(send, "seq", swap))
            last = [send]
            sends[stage, c] = send
        return [out[c] for c in range(chunks)]

    def shards(queries, keys, values, out_grad, norm_gain):
        tokens, width = queries.shape
        heads = width // DH
        half = heads // 2
        per = half // CHUNKS
        wide = half * DH
        narrow = per * DH
        at_seq = lax.axis_index("seq")
        y = at_seq % 2
        place, leads, ends = lax.optimization_barrier((y.astype(jnp.int32).reshape(1), y == 0, y == 1))
        gain = norm_gain.reshape(1, width)

        whole2 = lambda i, s: (0, 0)
        whole3 = lambda i, s: (0, 0, 0)

        def at_k(c):
            return lambda i, s: (0, s[0] * CHUNKS + c)

        def at_o(c):
            return lambda i, s: (0, (1 - s[0]) * CHUNKS + c)

        some = CHUNKS // 2
        sent = []
        for n in range(2):
            sent += call(
                functools.partial(states_body, per), place,
                [(a, (tokens, wide // 2), lambda i, s: (0, 2 * (1 - s[0]) + n), HBM) for a in (keys, values)],
                [((per, DH, DH), F32, (per, DH, DH), whole3, VMEM)] * some,
            )

        group = half // 2

        def local(which, chunks, memory, ties):
            strip = lambda i, s: (0, 2 * (1 - s[0] if which else s[0]) + i)
            return call(
                functools.partial(local_body, per, chunks, group), place,
                [(a, (tokens, group * DH), strip, memory) for a in (queries, keys, values)]
                + [(a, None, None) for a in ties],
                [((per, DH, DH), F32, (per, DH, DH), whole3, VMEM)] * chunks + [
                    ((tokens, wide), F32, (tokens, group * DH), lambda i, s: (0, i), VMEM),
                ],
                grid=(2,),
            )

        *kept, local_kept = local(0, CHUNKS, HBM, [])
        tail = long - 1
        spread = 2 < long <= 4
        before = scan(kept, sent, leads, False, [local_kept], {})
        local_other, = local(1, 0, VMEM, [before[CHUNKS - 1][0]])

        block = (tokens, narrow)
        square = cross = None
        attns, priors = [], []
        for c in range(CHUNKS):
            e, r, other = before[c]
            first, last = c == 0, c == CHUNKS - 1
            ins = []
            here = lambda i, s: (0, c)
            ins += [(local_kept, block, here), (local_other, block, here)]
            for a in (queries, out_grad):
                ins += [(a, block, at_k(c)), (a, block, at_o(c))]
            ins += [(gain, (1, narrow), at_k(c)), (gain, (1, narrow), at_o(c))]
            ins += [(a, (per, DH, DH), whole3) for a in (e, r, other)]
            if first:
                ins += [(a, None, None, VMEM) for a in (keys, values)]
            else:
                ins += [(a, (GROUP, DH), whole2) for a in (square, cross)]
            outs = [(block, F32, block, whole2, VMEM)] * 2 + [((per, DH, DH), BF16, (per, DH, DH), whole3, VMEM)] * 2
            if last:
                outs += [((2, GROUP), F32, (2, GROUP), whole2)]
            else:
                outs += [((GROUP, DH), F32, (GROUP, DH), whole2)] * 2
            a_k, a_o, s_k, s_o, *stats = call(
                functools.partial(attn_body, per, first, last), place, ins, outs)
            attns.append((a_k, a_o))
            priors.append((s_k, s_o))
            if last:
                mine = stats[0]
            else:
                square, cross = stats

        sums = [mine]
        paired = parts & (parts - 1) == 0
        for step in range(1, parts):
            sums.append(lax.ppermute(
                mine, "head", [(i, i ^ step if paired else (i + step) % parts) for i in range(parts)]))

        def delta(which, first, count):
            span = count * narrow
            index = lambda i, s: (0, (1 - s[0] if which else s[0]) * (CHUNKS // count) + first // count)
            ins = [(a, (2, GROUP), whole2) for a in sums]
            ins += [(attns[c][which], block, whole2) for c in range(first, first + count)]
            ins += [(queries, (tokens, span), index), (out_grad, (tokens, span), index), (gain, (1, span), index)]
            outs = [(block, BF16, block, whole2, VMEM)] * count
            outs += [((per, DH, DH), F32, (per, DH, DH), whole3, VMEM)] * count
            result = call(
                functools.partial(delta_body, per, count, parts, float(parts * heads * DH)), place, ins, outs)
            return result[:count], result[count:]

        d_one, sent_one = delta(1, 0, some)
        d_two, sent_two = delta(1, some, some)
        d_o, sent = d_one + d_two, sent_one + sent_two
        d_k, kept = delta(0, 0, CHUNKS)

        def mine(c):
            return lambda i, s: (0, jnp.where(i % 2 == 0, s[0], 1 - s[0]) * CHUNKS + c + i // 2)

        state3 = (per, DH, DH)
        made = {"query": [], "rest": []}

        def query(c, count, tie=None):
            ins = [(a, (tokens, width), whole2) for a in (keys, values)]
            some = range(c, c + count)
            grads = [a for i in some for a in (d_k[i], d_o[i])]
            if tie is not None:
                grads[0], _ = lax.optimization_barrier((grads[0], tie))
            ins += [(a, block, whole2) for a in grads]
            ins += [(a, state3, whole3) for i in some for a in priors[i]]
            aliases = {}
            if made["query"]:
                aliases[len(ins) + 1] = 0
                ins += [(a, None, None, HBM) for a in made["query"]]
            made["query"] = call(
                functools.partial(query_body, per, half, c, count), place, ins,
                [((tokens, width), BF16, block, mine(c), HBM)], grid=(2 * count,), aliases=aliases)
            return made["query"][0]

        def rest(c, which, after, count=1):
            steps = CHUNKS // count
            index = lambda i, s: (0, (1 - s[0] if which else s[0]) * steps + c // count)
            wider = (tokens, narrow * count)
            some = range(c, c + count)
            states = [a for i in some for a in (after[i][2:] if which else after[i][:2])]
            ins = [(a, (tokens, width), whole2) for a in (queries, keys, values)]
            ins += [((d_o if which else d_k)[i], block, whole2) for i in some]
            ins += [(a, state3, whole3) for a in states]
            aliases = {}
            if made["rest"]:
                aliases = {len(ins) + 1: 0, len(ins) + 2: 1}
                ins += [(a, None, None, HBM) for a in made["rest"]]
            made["rest"] = call(
                functools.partial(final_body, per, half, c, which, count, len(states) // count), place, ins,
                [((tokens, width), BF16, wider, index, HBM)] * 2, aliases=aliases)
            return made["rest"][0]

        beside = {
            (2, 0): lambda out, sends: query(0, 2, sends[1, 1]),
            (tail, 0): lambda out, sends: query(2, 1, sends[2, 1]),
            (tail, 1): lambda out, sends: query(3, 1),
            (tail, 2): lambda out, sends: rest(0, 0, out, 2),
            (tail, 3): lambda out, sends: rest(2, 0, out),
        } if spread else {}
        after = scan(kept, sent, ends, True, [], beside)
        if not spread:
            query(0, CHUNKS)
            rest(0, 0, after, 2)
            rest(2, 0, after)
        rest(3, 0, after)
        rest(0, 1, after, 2)
        rest(2, 1, after)
        rest(3, 1, after)
        return made["query"][0], made["rest"][0], made["rest"][1]

    return jax.shard_map(
        shards,
        mesh=mesh,
        in_specs=(
            P("seq", "head"),
            P("seq", "head"),
            P("seq", "head"),
            P("seq", "head"),
            P("head"),
        ),
        out_specs=(P("seq", "head"), P("seq", "head"), P("seq", "head")),
        check_vma=False,
    )
```

```python
import functools

import jax
import jax.numpy as jnp
from jax import lax
from jax.experimental import pallas as pl
from jax.experimental.pallas import tpu as pltpu
from jax.sharding import PartitionSpec as P

DH = 128
GROUP = 256
CHUNKS = 4
EPS = 1e-05
F32 = jnp.float32
BF16 = jnp.bfloat16


def dot(a, b, ca, cb):
    return lax.dot_general(a, b, (((ca,), (cb,)), ((), ())), preferred_element_type=F32)


def head(ref, j):
    return ref[:, j * DH:(j + 1) * DH]


def causal(turned=False):
    rows = lax.broadcasted_iota(jnp.int32, (GROUP, GROUP), 0)
    cols = lax.broadcasted_iota(jnp.int32, (GROUP, GROUP), 1)
    return cols >= rows if turned else rows >= cols


def masked(scores, mask):
    return jnp.where(mask, scores, 0.0).astype(BF16)


HBM, VMEM = pltpu.HBM, pltpu.VMEM


def call(body, place, ins, outs, grid=(1,), aliases=None, grant=8):
    ins = [(*item, None)[:4] for item in ins]
    outs = [(*item, None)[:5] for item in outs]
    arrays = [pltpu.with_memory_space_constraint(a, m) if m else a for a, _, _, m in ins]
    return pl.pallas_call(
        body,
        grid_spec=pltpu.PrefetchScalarGridSpec(
            num_scalar_prefetch=1,
            grid=grid,
            in_specs=[pl.BlockSpec(b, m) if b else pl.BlockSpec(memory_space=pl.ANY) for _, b, m, _ in ins],
            out_specs=[pl.BlockSpec(b, m) for _, _, b, m, _ in outs],
        ),
        out_shape=[(m or jax.ShapeDtypeStruct)(s, d) for s, d, _, _, m in outs],
        input_output_aliases=aliases or {},
        compiler_params=pltpu.CompilerParams(vmem_limit_bytes=grant * 1024 * 1024),
        cost_estimate=pl.CostEstimate(flops=1024, bytes_accessed=1024, transcendentals=0),
    )(place, *arrays)


def states_body(per, place, a, b, *outs):
    for c, out in enumerate(outs):
        for j in range(per):
            h = c * per + j
            out[j] = dot(head(a, h), head(b, h), 0, 0)


def local_body(per, chunks, heads, place, q, k, v, *refs):
    outs, attn = refs[-1 - chunks:-1], refs[-1]
    for turn in range(chunks * per // heads):
        @pl.when(pl.program_id(0) == turn)
        def _():
            for j in range(heads):
                h = turn * heads + j
                outs[h // per][h % per] = dot(head(k, j), head(v, j), 0, 0)
    mask = causal()
    scores = [dot(head(q, j), head(k, j), 1, 1) for j in range(heads)]
    scores = [masked(s, mask) for s in scores]
    for j, s in enumerate(scores):
        attn[:, j * DH:(j + 1) * DH] = dot(s, head(v, j), 1, 0)


def attn_body(per, first, last, place, al_k, al_o, q_k, q_o, g_k, g_o, n_k, n_o, e, r, other, *refs):
    one, two, *refs = refs
    if not first:
        sq_in, cr_in = one, two
    at_k, at_o, sb_k, sb_o, *stats = refs
    square = jnp.zeros((GROUP, DH), F32) if first else sq_in[...]
    cross = jnp.zeros((GROUP, DH), F32) if first else cr_in[...]
    for j in range(per):
        kept = (e[j] + r[j]).astype(BF16)
        sb_k[j] = kept
        sb_o[j] = other[j].astype(BF16)
        for al, q, g, n, sb, at in (
            (al_k, q_k, g_k, n_k, sb_k, at_k),
            (al_o, q_o, g_o, n_o, sb_o, at_o),
        ):
            x = head(al, j) + dot(head(q, j), sb[j], 1, 0)
            at[:, j * DH:(j + 1) * DH] = x
            scaled = head(n, j).astype(F32) * head(g, j).astype(F32)
            square = square + x * x
            cross = cross + scaled * x
    if last:
        stats[0][0:1] = jnp.sum(square.T, axis=0, keepdims=True)
        stats[0][1:2] = jnp.sum(cross.T, axis=0, keepdims=True)
    else:
        stats[0][...] = square
        stats[1][...] = cross


def delta_body(per, chunks, parts, features, place, *refs):
    stats = refs[:parts]
    attn = refs[parts:parts + chunks]
    q, g, n = refs[parts + chunks:parts + chunks + 3]
    outs = refs[parts + chunks + 3:]
    total = stats[0][...]
    for s in stats[1:]:
        total = total + s[...]
    inverse = lax.rsqrt(total[0:1] / features + EPS)
    slope = inverse * inverse * inverse * (total[1:2] / features)
    inverse = jnp.broadcast_to(inverse, (DH, GROUP)).T
    slope = jnp.broadcast_to(slope, (DH, GROUP)).T
    for c in range(chunks):
        for j in range(per):
            h = c * per + j
            scaled = head(n, h).astype(F32) * head(g, h).astype(F32)
            x = (inverse * scaled - head(attn[c], j) * slope).astype(BF16)
            outs[c][:, j * DH:(j + 1) * DH] = x
            outs[chunks + c][j] = dot(head(q, h), x, 0, 0)


def column(ref, base, h):
    return ref[:, pl.ds(pl.multiple_of(base + h * DH, DH), DH)]


def query_body(per, half, chunks, place, k, v, *refs):
    qg = refs[-1]
    mask = causal()
    for turn in range(2 * chunks):
        d, sb = refs[turn], refs[2 * chunks + turn]
        base = (1 - place[0] if turn % 2 else place[0]) * half * DH + turn // 2 * per * DH
        scores = [dot(head(d, j), column(v, base, j), 1, 1) for j in range(per)]
        prior = [dot(head(d, j), sb[j], 1, 1) for j in range(per)]
        scores = [masked(s, mask) for s in scores]
        for j, s in enumerate(scores):
            qg[:, pl.ds(pl.multiple_of(base + j * DH, DH), DH)] = (
                dot(s, column(k, base, j), 1, 0) + prior[j]).astype(BF16)


def final_body(per, half, units, place, q, k, v, *refs):
    count = len(units)
    kg, vg = refs[-2], refs[-1]
    mask = causal(turned=True)
    used = count
    for turn, (c, other, terms) in enumerate(units):
        d, later_in = refs[turn], refs[used:used + terms]
        used += terms
        base = (1 - place[0] if other else place[0]) * half * DH + c * per * DH

        @pl.when(pl.program_id(0) == turn)
        def _():
            heads = range(per)
            states = [sum((t[h] for t in later_in[1:]), later_in[0][h]).astype(BF16) for h in heads]
            outer = [head(d, h) for h in heads]
            qs, ks, vs = ([column(a, base, h) for h in heads] for a in (q, k, v))
            grad = [dot(vs[h], outer[h], 1, 1) for h in heads]
            score = [dot(ks[h], qs[h], 1, 1) for h in heads]
            kg_part = [dot(vs[h], states[h], 1, 1) for h in heads]
            vg_part = [dot(ks[h], states[h], 1, 0) for h in heads]
            grad = [masked(x, mask) for x in grad]
            score = [masked(x, mask) for x in score]
            for h in heads:
                at = slice(h * DH, (h + 1) * DH)
                kg[:, at] = (dot(grad[h], qs[h], 1, 0) + kg_part[h]).astype(BF16)
                vg[:, at] = (dot(score[h], outer[h], 1, 0) + vg_part[h]).astype(BF16)


def solution(mesh):
    count = mesh.shape["seq"]
    parts = mesh.shape["head"]
    long = count // 2
    swap = [(i, i ^ 1) for i in range(count)]

    def hop(array, near, far, reverse):
        pairs = []
        for z in range(long):
            to = z + far
            if to < long and near(z):
                for y in range(2):
                    pairs.append((2 * z + y, 2 * to + y))
        if reverse:
            pairs = [(count - 1 - a, count - 1 - b) for a, b in pairs]
        return lax.ppermute(array, "seq", pairs)

    def shift(array, far, reverse):
        return hop(array, lambda at: True, far, reverse)

    def doubling(parts, reverse):
        out = []
        for part in parts:
            carry = shift(part, 1, reverse)
            far = 1
            while far < long:
                carry = carry + shift(carry, far, reverse)
                far *= 2
            out.append(carry)
        return out

    def scan(kept, sent, leads, reverse, ready, beside):
        own = [None] * len(kept)
        if long > 4 or long < 2:
            swapped = [lax.ppermute(b, "seq", swap) for b in sent]
            own = [jnp.where(leads, 0.0, r) for r in swapped]
            sums = [a + r for a, r in zip(kept, swapped)]
            sums = doubling(sums, reverse) if long > 1 else [jnp.zeros_like(a) for a in sums]
            others = [
                lax.ppermute(jnp.where(leads, e + a, e), "seq", swap) for a, e in zip(kept, sums)
            ]
            return list(zip(sums, own, others))
        chunks = len(kept)
        order = sorted((2 * stage + c, stage, c) for stage in range(long) for c in range(chunks))
        part, flight, carry, out, sends = {}, {}, {}, {}, {}
        last = ready

        def swap_after(c, *things):
            if c < chunks:
                part_sent, *_ = lax.optimization_barrier((sent[c], *things))
                flight[c] = lax.ppermute(part_sent, "seq", swap)

        swap_after(0)
        swap_after(1)
        swap_after(2)
        for _, stage, c in order:
            if (stage, c) in beside:
                last = last + [beside[stage, c](out, sends)]
            got, *_ = lax.optimization_barrier((flight[c], *last))
            if stage == 0:
                own[c] = jnp.where(leads, 0.0, got)
                part[c] = send = kept[c] + got
                swap_after(c + 3, send)
            else:
                carry[c] = got if stage == 1 else carry[c] + got
                send = carry[c] + part[c]
            if stage < long - 1:
                flight[c] = hop(send, lambda at: at == stage, 1, reverse)
            else:
                send = jnp.where(leads, carry[c] + kept[c], carry[c])
                out[c] = (carry[c], own[c], lax.ppermute(send, "seq", swap))
            last = [send]
            sends[stage, c] = send
        return [out[c] for c in range(chunks)]

    def shards(queries, keys, values, out_grad, norm_gain):
        tokens, width = queries.shape
        heads = width // DH
        half = heads // 2
        per = half // CHUNKS
        wide = half * DH
        narrow = per * DH
        at_seq = lax.axis_index("seq")
        y = at_seq % 2
        place, leads, ends = lax.optimization_barrier((y.astype(jnp.int32).reshape(1), y == 0, y == 1))
        gain = norm_gain.reshape(1, width)

        whole2 = lambda i, s: (0, 0)
        whole3 = lambda i, s: (0, 0, 0)

        def at_k(c):
            return lambda i, s: (0, s[0] * CHUNKS + c)

        def at_o(c):
            return lambda i, s: (0, (1 - s[0]) * CHUNKS + c)

        some = CHUNKS // 2
        sent = []
        for n in range(2):
            sent += call(
                functools.partial(states_body, per), place,
                [(a, (tokens, wide // 2), lambda i, s: (0, 2 * (1 - s[0]) + n), HBM) for a in (keys, values)],
                [((per, DH, DH), F32, (per, DH, DH), whole3, VMEM)] * some,
            )

        group = half // 2

        def local(which, chunks, memory, ties):
            strip = lambda i, s: (0, 2 * (1 - s[0] if which else s[0]) + i)
            return call(
                functools.partial(local_body, per, chunks, group), place,
                [(a, (tokens, group * DH), strip, memory) for a in (queries, keys, values)]
                + [(a, None, None) for a in ties],
                [((per, DH, DH), F32, (per, DH, DH), whole3, VMEM)] * chunks + [
                    ((tokens, wide), F32, (tokens, group * DH), lambda i, s: (0, i), VMEM),
                ],
                grid=(2,),
            )

        *kept, local_kept = local(0, CHUNKS, HBM, [])
        spread = 2 < long <= 4
        before = scan(kept, sent, leads, False, [local_kept], {})
        local_other, = local(1, 0, VMEM, [before[CHUNKS - 1][0]])

        block = (tokens, narrow)
        square = cross = None
        attns, priors = [], []
        for c in range(CHUNKS):
            e, r, other = before[c]
            first, last = c == 0, c == CHUNKS - 1
            ins = []
            here = lambda i, s: (0, c)
            ins += [(local_kept, block, here), (local_other, block, here)]
            for a in (queries, out_grad):
                ins += [(a, block, at_k(c)), (a, block, at_o(c))]
            ins += [(gain, (1, narrow), at_k(c)), (gain, (1, narrow), at_o(c))]
            ins += [(a, (per, DH, DH), whole3) for a in (e, r, other)]
            if first:
                ins += [(a, None, None, VMEM) for a in (keys, values)]
            else:
                ins += [(a, (GROUP, DH), whole2) for a in (square, cross)]
            outs = [(block, F32, block, whole2, VMEM)] * 2 + [((per, DH, DH), BF16, (per, DH, DH), whole3, VMEM)] * 2
            if last:
                outs += [((2, GROUP), F32, (2, GROUP), whole2)]
            else:
                outs += [((GROUP, DH), F32, (GROUP, DH), whole2)] * 2
            a_k, a_o, s_k, s_o, *stats = call(
                functools.partial(attn_body, per, first, last), place, ins, outs)
            attns.append((a_k, a_o))
            priors.append((s_k, s_o))
            if last:
                mine = stats[0]
            else:
                square, cross = stats

        sums = [mine]
        paired = parts & (parts - 1) == 0
        for step in range(1, parts):
            sums.append(lax.ppermute(
                mine, "head", [(i, i ^ step if paired else (i + step) % parts) for i in range(parts)]))

        def delta(which, first, count):
            span = count * narrow
            index = lambda i, s: (0, (1 - s[0] if which else s[0]) * (CHUNKS // count) + first // count)
            ins = [(a, (2, GROUP), whole2) for a in sums]
            ins += [(attns[c][which], block, whole2) for c in range(first, first + count)]
            ins += [(queries, (tokens, span), index), (out_grad, (tokens, span), index), (gain, (1, span), index)]
            outs = [(block, BF16, block, whole2, VMEM)] * count
            outs += [((per, DH, DH), F32, (per, DH, DH), whole3, VMEM)] * count
            result = call(
                functools.partial(delta_body, per, count, parts, float(parts * heads * DH)), place, ins, outs)
            return result[:count], result[count:]

        d_one, sent_one = delta(1, 0, some)
        d_two, sent_two = delta(1, some, some)
        d_o, sent = d_one + d_two, sent_one + sent_two
        d_k, kept = delta(0, 0, CHUNKS)

        state3 = (per, DH, DH)

        def query(tie=None):
            ins = [(a, (tokens, width), whole2) for a in (keys, values)]
            grads = [a for i in range(CHUNKS) for a in (d_k[i], d_o[i])]
            if tie is not None:
                grads[0], _ = lax.optimization_barrier((grads[0], tie))
            ins += [(a, block, whole2) for a in grads]
            ins += [(a, state3, whole3) for i in range(CHUNKS) for a in priors[i]]
            made = call(
                functools.partial(query_body, per, half, CHUNKS), place, ins,
                [((tokens, width), BF16, (tokens, width), whole2, VMEM)])
            query_made.extend(made)
            return made[0]

        def rest(units, after, made):
            states = [after[c][2:] if other else after[c][:2] for c, other in units]

            def index(i, s):
                at = 0
                for n, (c, other) in enumerate(units):
                    at = jnp.where(i == n, (1 - s[0] if other else s[0]) * CHUNKS + c, at)
                return (0, at)

            ins = [(a, (tokens, width), whole2) for a in (queries, keys, values)]
            ins += [((d_o if other else d_k)[c], block, whole2) for c, other in units]
            ins += [(a, state3, whole3) for some in states for a in some]
            aliases = {}
            if made:
                aliases = {len(ins) + 1: 0, len(ins) + 2: 1}
                ins += [(a, None, None, HBM) for a in made]
            kinds = [(c, other, len(some)) for (c, other), some in zip(units, states)]
            return call(
                functools.partial(final_body, per, half, kinds), place, ins,
                [((tokens, width), BF16, block, index, HBM)] * 2, grid=(len(units),), aliases=aliases)

        query_made = []
        beside = {(2, 0): lambda out, sends: query(sends[1, 1])} if spread else {}
        after = scan(kept, sent, ends, True, [], beside)
        if not spread:
            query()
        made = rest([(c, 0) for c in range(CHUNKS)] + [(c, 1) for c in range(CHUNKS - 2)], after, [])
        for c in range(CHUNKS - 2, CHUNKS):
            made = rest([(c, 1)], after, made)
        return query_made[0], made[0], made[1]

    return jax.shard_map(
        shards,
        mesh=mesh,
        in_specs=(
            P("seq", "head"),
            P("seq", "head"),
            P("seq", "head"),
            P("seq", "head"),
            P("head"),
        ),
        out_specs=(P("seq", "head"), P("seq", "head"), P("seq", "head")),
        check_vma=False,
    )
```

```python
import functools

import jax
import jax.numpy as jnp
from jax import lax
from jax.experimental import pallas as pl
from jax.experimental.pallas import tpu as pltpu
from jax.sharding import PartitionSpec as P

DH = 128
GROUP = 256
CHUNKS = 4
EPS = 1e-05
F32 = jnp.float32
BF16 = jnp.bfloat16


def dot(a, b, ca, cb):
    return lax.dot_general(a, b, (((ca,), (cb,)), ((), ())), preferred_element_type=F32)


def head(ref, j):
    return ref[:, j * DH:(j + 1) * DH]


def causal(turned=False):
    rows = lax.broadcasted_iota(jnp.int32, (GROUP, GROUP), 0)
    cols = lax.broadcasted_iota(jnp.int32, (GROUP, GROUP), 1)
    return cols >= rows if turned else rows >= cols


def masked(scores, mask):
    return jnp.where(mask, scores, 0.0).astype(BF16)


HBM, VMEM = pltpu.HBM, pltpu.VMEM


def call(body, place, ins, outs, grid=(1,), aliases=None, grant=8):
    ins = [(*item, None)[:4] for item in ins]
    outs = [(*item, None)[:5] for item in outs]
    arrays = [pltpu.with_memory_space_constraint(a, m) if m else a for a, _, _, m in ins]
    return pl.pallas_call(
        body,
        grid_spec=pltpu.PrefetchScalarGridSpec(
            num_scalar_prefetch=1,
            grid=grid,
            in_specs=[pl.BlockSpec(b, m) if b else pl.BlockSpec(memory_space=pl.ANY) for _, b, m, _ in ins],
            out_specs=[pl.BlockSpec(b, m) for _, _, b, m, _ in outs],
        ),
        out_shape=[(m or jax.ShapeDtypeStruct)(s, d) for s, d, _, _, m in outs],
        input_output_aliases=aliases or {},
        compiler_params=pltpu.CompilerParams(vmem_limit_bytes=grant * 1024 * 1024),
        cost_estimate=pl.CostEstimate(flops=1024, bytes_accessed=1024, transcendentals=0),
    )(place, *arrays)


def states_body(per, place, a, b, *outs):
    for c, out in enumerate(outs):
        for j in range(per):
            h = c * per + j
            out[j] = dot(head(a, h), head(b, h), 0, 0)


def local_body(per, chunks, heads, place, q, k, v, *refs):
    outs, attn = refs[-1 - chunks:-1], refs[-1]
    for turn in range(chunks * per // heads):
        @pl.when(pl.program_id(0) == turn)
        def _():
            for j in range(heads):
                h = turn * heads + j
                outs[h // per][h % per] = dot(head(k, j), head(v, j), 0, 0)
    mask = causal()
    scores = [dot(head(q, j), head(k, j), 1, 1) for j in range(heads)]
    scores = [masked(s, mask) for s in scores]
    for j, s in enumerate(scores):
        attn[:, j * DH:(j + 1) * DH] = dot(s, head(v, j), 1, 0)


def attn_body(per, first, last, place, al_k, al_o, q_k, q_o, g_k, g_o, n_k, n_o, e, r, other, *refs):
    one, two, *refs = refs
    if not first:
        sq_in, cr_in = one, two
    at_k, at_o, sb_k, sb_o, *stats = refs
    square = jnp.zeros((GROUP, DH), F32) if first else sq_in[...]
    cross = jnp.zeros((GROUP, DH), F32) if first else cr_in[...]
    for j in range(per):
        kept = (e[j] + r[j]).astype(BF16)
        sb_k[j] = kept
        sb_o[j] = other[j].astype(BF16)
        for al, q, g, n, sb, at in (
            (al_k, q_k, g_k, n_k, sb_k, at_k),
            (al_o, q_o, g_o, n_o, sb_o, at_o),
        ):
            x = head(al, j) + dot(head(q, j), sb[j], 1, 0)
            at[:, j * DH:(j + 1) * DH] = x
            scaled = head(n, j).astype(F32) * head(g, j).astype(F32)
            square = square + x * x
            cross = cross + scaled * x
    if last:
        stats[0][0:1] = jnp.sum(square.T, axis=0, keepdims=True)
        stats[0][1:2] = jnp.sum(cross.T, axis=0, keepdims=True)
    else:
        stats[0][...] = square
        stats[1][...] = cross


def delta_body(per, chunks, parts, features, place, *refs):
    stats = refs[:parts]
    attn = refs[parts:parts + chunks]
    q, g, n = refs[parts + chunks:parts + chunks + 3]
    outs = refs[parts + chunks + 3:]
    total = stats[0][...]
    for s in stats[1:]:
        total = total + s[...]
    inverse = lax.rsqrt(total[0:1] / features + EPS)
    slope = inverse * inverse * inverse * (total[1:2] / features)
    inverse = jnp.broadcast_to(inverse, (DH, GROUP)).T
    slope = jnp.broadcast_to(slope, (DH, GROUP)).T
    for c in range(chunks):
        for j in range(per):
            h = c * per + j
            scaled = head(n, h).astype(F32) * head(g, h).astype(F32)
            x = (inverse * scaled - head(attn[c], j) * slope).astype(BF16)
            outs[c][:, j * DH:(j + 1) * DH] = x
            outs[chunks + c][j] = dot(head(q, h), x, 0, 0)


def column(ref, base, h):
    return ref[:, pl.ds(pl.multiple_of(base + h * DH, DH), DH)]


def query_body(per, half, chunks, place, k, v, *refs):
    qg = refs[-1]
    mask = causal()
    for turn in range(2 * chunks):
        d, sb = refs[turn], refs[2 * chunks + turn]
        base = (1 - place[0] if turn % 2 else place[0]) * half * DH + turn // 2 * per * DH
        scores = [dot(head(d, j), column(v, base, j), 1, 1) for j in range(per)]
        prior = [dot(head(d, j), sb[j], 1, 1) for j in range(per)]
        scores = [masked(s, mask) for s in scores]
        for j, s in enumerate(scores):
            qg[:, pl.ds(pl.multiple_of(base + j * DH, DH), DH)] = (
                dot(s, column(k, base, j), 1, 0) + prior[j]).astype(BF16)


def final_body(per, half, units, place, q, k, v, *refs):
    count = len(units)
    kg, vg = refs[-2], refs[-1]
    mask = causal(turned=True)
    used = count
    for turn, (c, other, terms) in enumerate(units):
        d, later_in = refs[turn], refs[used:used + terms]
        used += terms
        base = (1 - place[0] if other else place[0]) * half * DH + c * per * DH

        @pl.when(pl.program_id(0) == turn)
        def _():
            heads = range(per)
            states = [sum((t[h] for t in later_in[1:]), later_in[0][h]).astype(BF16) for h in heads]
            outer = [head(d, h) for h in heads]
            qs, ks, vs = ([column(a, base, h) for h in heads] for a in (q, k, v))
            grad = [dot(vs[h], outer[h], 1, 1) for h in heads]
            score = [dot(ks[h], qs[h], 1, 1) for h in heads]
            kg_part = [dot(vs[h], states[h], 1, 1) for h in heads]
            vg_part = [dot(ks[h], states[h], 1, 0) for h in heads]
            grad = [masked(x, mask) for x in grad]
            score = [masked(x, mask) for x in score]
            for h in heads:
                at = slice(h * DH, (h + 1) * DH)
                kg[:, at] = (dot(grad[h], qs[h], 1, 0) + kg_part[h]).astype(BF16)
                vg[:, at] = (dot(score[h], outer[h], 1, 0) + vg_part[h]).astype(BF16)


def solution(mesh):
    count = mesh.shape["seq"]
    parts = mesh.shape["head"]
    long = count // 2
    swap = [(i, i ^ 1) for i in range(count)]

    def hop(array, near, far, reverse):
        pairs = []
        for z in range(long):
            to = z + far
            if to < long and near(z):
                for y in range(2):
                    pairs.append((2 * z + y, 2 * to + y))
        if reverse:
            pairs = [(count - 1 - a, count - 1 - b) for a, b in pairs]
        return lax.ppermute(array, "seq", pairs)

    def shift(array, far, reverse):
        return hop(array, lambda at: True, far, reverse)

    def doubling(parts, reverse):
        out = []
        for part in parts:
            carry = shift(part, 1, reverse)
            far = 1
            while far < long:
                carry = carry + shift(carry, far, reverse)
                far *= 2
            out.append(carry)
        return out

    def scan(kept, sent, leads, reverse, ready, beside):
        own = [None] * len(kept)
        if long > 4 or long < 2:
            swapped = [lax.ppermute(b, "seq", swap) for b in sent]
            own = [jnp.where(leads, 0.0, r) for r in swapped]
            sums = [a + r for a, r in zip(kept, swapped)]
            sums = doubling(sums, reverse) if long > 1 else [jnp.zeros_like(a) for a in sums]
            others = [
                lax.ppermute(jnp.where(leads, e + a, e), "seq", swap) for a, e in zip(kept, sums)
            ]
            return list(zip(sums, own, others))
        chunks = len(kept)
        order = sorted((2 * stage + c, stage, c) for stage in range(long) for c in range(chunks))
        part, flight, carry, out, sends = {}, {}, {}, {}, {}
        last = ready

        def swap_after(c, *things):
            if c < chunks:
                part_sent, *_ = lax.optimization_barrier((sent[c], *things))
                flight[c] = lax.ppermute(part_sent, "seq", swap)

        swap_after(0)
        swap_after(1)
        swap_after(2)
        for _, stage, c in order:
            if (stage, c) in beside:
                last = last + [beside[stage, c](out, sends)]
            got, *_ = lax.optimization_barrier((flight[c], *last))
            if stage == 0:
                own[c] = jnp.where(leads, 0.0, got)
                part[c] = send = kept[c] + got
                swap_after(c + 3, send)
            else:
                carry[c] = got if stage == 1 else carry[c] + got
                send = carry[c] + part[c]
            if stage < long - 1:
                flight[c] = hop(send, lambda at: at == stage, 1, reverse)
            else:
                send = jnp.where(leads, carry[c] + kept[c], carry[c])
                out[c] = (carry[c], own[c], lax.ppermute(send, "seq", swap))
            last = [send]
            sends[stage, c] = send
        return [out[c] for c in range(chunks)]

    def shards(queries, keys, values, out_grad, norm_gain):
        tokens, width = queries.shape
        heads = width // DH
        half = heads // 2
        per = half // CHUNKS
        wide = half * DH
        narrow = per * DH
        at_seq = lax.axis_index("seq")
        y = at_seq % 2
        place, leads, ends = lax.optimization_barrier((y.astype(jnp.int32).reshape(1), y == 0, y == 1))
        gain = norm_gain.reshape(1, width)

        whole2 = lambda i, s: (0, 0)
        whole3 = lambda i, s: (0, 0, 0)

        def at_k(c):
            return lambda i, s: (0, s[0] * CHUNKS + c)

        def at_o(c):
            return lambda i, s: (0, (1 - s[0]) * CHUNKS + c)

        some = CHUNKS // 2
        sent = []
        for n in range(2):
            sent += call(
                functools.partial(states_body, per), place,
                [(a, (tokens, wide // 2), lambda i, s: (0, 2 * (1 - s[0]) + n), HBM) for a in (keys, values)],
                [((per, DH, DH), F32, (per, DH, DH), whole3, VMEM)] * some,
            )

        group = half // 2

        def local(which, chunks, memory, ties):
            strip = lambda i, s: (0, 2 * (1 - s[0] if which else s[0]) + i)
            return call(
                functools.partial(local_body, per, chunks, group), place,
                [(a, (tokens, group * DH), strip, memory) for a in (queries, keys, values)]
                + [(a, None, None) for a in ties],
                [((per, DH, DH), F32, (per, DH, DH), whole3, VMEM)] * chunks + [
                    ((tokens, wide), F32, (tokens, group * DH), lambda i, s: (0, i), VMEM),
                ],
                grid=(2,),
            )

        *kept, local_kept = local(0, CHUNKS, HBM, [])
        spread = 2 < long <= 4
        before = scan(kept, sent, leads, False, [local_kept], {})
        local_other, = local(1, 0, VMEM, [before[CHUNKS - 1][0]])

        block = (tokens, narrow)
        square = cross = None
        attns, priors = [], []
        for c in range(CHUNKS):
            e, r, other = before[c]
            first, last = c == 0, c == CHUNKS - 1
            ins = []
            here = lambda i, s: (0, c)
            ins += [(local_kept, block, here), (local_other, block, here)]
            for a in (queries, out_grad):
                ins += [(a, block, at_k(c)), (a, block, at_o(c))]
            ins += [(gain, (1, narrow), at_k(c)), (gain, (1, narrow), at_o(c))]
            ins += [(a, (per, DH, DH), whole3) for a in (e, r, other)]
            if first:
                ins += [(a, None, None, VMEM) for a in (keys, values)]
            else:
                ins += [(a, (GROUP, DH), whole2) for a in (square, cross)]
            outs = [(block, F32, block, whole2, VMEM)] * 2 + [((per, DH, DH), BF16, (per, DH, DH), whole3, VMEM)] * 2
            if last:
                outs += [((2, GROUP), F32, (2, GROUP), whole2)]
            else:
                outs += [((GROUP, DH), F32, (GROUP, DH), whole2)] * 2
            a_k, a_o, s_k, s_o, *stats = call(
                functools.partial(attn_body, per, first, last), place, ins, outs)
            attns.append((a_k, a_o))
            priors.append((s_k, s_o))
            if last:
                mine = stats[0]
            else:
                square, cross = stats

        sums = [mine]
        paired = parts & (parts - 1) == 0
        for step in range(1, parts):
            sums.append(lax.ppermute(
                mine, "head", [(i, i ^ step if paired else (i + step) % parts) for i in range(parts)]))

        def delta(which, first, count):
            span = count * narrow
            index = lambda i, s: (0, (1 - s[0] if which else s[0]) * (CHUNKS // count) + first // count)
            ins = [(a, (2, GROUP), whole2) for a in sums]
            ins += [(attns[c][which], block, whole2) for c in range(first, first + count)]
            ins += [(queries, (tokens, span), index), (out_grad, (tokens, span), index), (gain, (1, span), index)]
            outs = [(block, BF16, block, whole2, VMEM)] * count
            outs += [((per, DH, DH), F32, (per, DH, DH), whole3, VMEM)] * count
            result = call(
                functools.partial(delta_body, per, count, parts, float(parts * heads * DH)), place, ins, outs)
            return result[:count], result[count:]

        d_one, sent_one = delta(1, 0, some)
        d_two, sent_two = delta(1, some, some)
        d_o, sent = d_one + d_two, sent_one + sent_two
        d_k, kept = delta(0, 0, CHUNKS)

        state3 = (per, DH, DH)

        def query(tie=None):
            ins = [(a, (tokens, width), whole2) for a in (keys, values)]
            grads = [a for i in range(CHUNKS) for a in (d_k[i], d_o[i])]
            if tie is not None:
                grads[0], _ = lax.optimization_barrier((grads[0], tie))
            ins += [(a, block, whole2) for a in grads]
            ins += [(a, state3, whole3) for i in range(CHUNKS) for a in priors[i]]
            made = call(
                functools.partial(query_body, per, half, CHUNKS), place, ins,
                [((tokens, width), BF16, (tokens, width), whole2, VMEM)])
            query_made.extend(made)
            return made[0]

        def rest(units, after, made):
            states = [after[c][2:] if other else after[c][:2] for c, other in units]

            def index(i, s):
                at = 0
                for n, (c, other) in enumerate(units):
                    at = jnp.where(i == n, (1 - s[0] if other else s[0]) * CHUNKS + c, at)
                return (0, at)

            ins = [(a, (tokens, width), whole2) for a in (queries, keys, values)]
            ins += [((d_o if other else d_k)[c], block, whole2) for c, other in units]
            ins += [(a, state3, whole3) for some in states for a in some]
            aliases = {}
            if made:
                aliases = {len(ins) + 1: 0, len(ins) + 2: 1}
                ins += [(a, None, None, HBM) for a in made]
            kinds = [(c, other, len(some)) for (c, other), some in zip(units, states)]
            return call(
                functools.partial(final_body, per, half, kinds), place, ins,
                [((tokens, width), BF16, block, index, HBM)] * 2, grid=(len(units),), aliases=aliases)

        query_made = []
        made = []

        def one(c):
            def work(out, sends):
                made[:] = rest([(c, 0)], out, made)
                return made[0]
            return work

        beside = {
            (2, 0): lambda out, sends: query(sends[1, 2]),
            (long - 1, 1): one(0),
            (long - 1, 2): one(1),
            (long - 1, 3): one(2),
        } if spread else {}
        after = scan(kept, sent, ends, True, [], beside)
        if not spread:
            query()
        for c in range(3 if spread else 0, CHUNKS):
            one(c)(after, None)
        made = rest([(0, 1), (1, 1)], after, made)
        for c in range(2, CHUNKS):
            made = rest([(c, 1)], after, made)
        return query_made[0], made[0], made[1]

    return jax.shard_map(
        shards,
        mesh=mesh,
        in_specs=(
            P("seq", "head"),
            P("seq", "head"),
            P("seq", "head"),
            P("seq", "head"),
            P("head"),
        ),
        out_specs=(P("seq", "head"), P("seq", "head"), P("seq", "head")),
        check_vma=False,
    )
```

```python
import functools

import jax
import jax.numpy as jnp
from jax import lax
from jax.experimental import pallas as pl
from jax.experimental.pallas import tpu as pltpu
from jax.sharding import PartitionSpec as P

DH = 128
GROUP = 256
CHUNKS = 4
EPS = 1e-05
F32 = jnp.float32
BF16 = jnp.bfloat16


def dot(a, b, ca, cb):
    return lax.dot_general(a, b, (((ca,), (cb,)), ((), ())), preferred_element_type=F32)


def head(ref, j):
    return ref[:, j * DH:(j + 1) * DH]


def causal(turned=False):
    rows = lax.broadcasted_iota(jnp.int32, (GROUP, GROUP), 0)
    cols = lax.broadcasted_iota(jnp.int32, (GROUP, GROUP), 1)
    return cols >= rows if turned else rows >= cols


def masked(scores, mask):
    return jnp.where(mask, scores, 0.0).astype(BF16)


HBM, VMEM = pltpu.HBM, pltpu.VMEM


def call(body, place, ins, outs, grid=(1,), aliases=None, grant=8):
    ins = [(*item, None)[:4] for item in ins]
    outs = [(*item, None)[:5] for item in outs]
    arrays = [pltpu.with_memory_space_constraint(a, m) if m else a for a, _, _, m in ins]
    return pl.pallas_call(
        body,
        grid_spec=pltpu.PrefetchScalarGridSpec(
            num_scalar_prefetch=1,
            grid=grid,
            in_specs=[pl.BlockSpec(b, m) if b else pl.BlockSpec(memory_space=pl.ANY) for _, b, m, _ in ins],
            out_specs=[pl.BlockSpec(b, m) for _, _, b, m, _ in outs],
        ),
        out_shape=[(m or jax.ShapeDtypeStruct)(s, d) for s, d, _, _, m in outs],
        input_output_aliases=aliases or {},
        compiler_params=pltpu.CompilerParams(vmem_limit_bytes=grant * 1024 * 1024),
        cost_estimate=pl.CostEstimate(flops=1024, bytes_accessed=1024, transcendentals=0),
    )(place, *arrays)


def states_body(per, place, a, b, *outs):
    for c, out in enumerate(outs):
        for j in range(per):
            h = c * per + j
            out[j] = dot(head(a, h), head(b, h), 0, 0)


def local_body(per, chunks, heads, place, q, k, v, *refs):
    outs, attn = refs[-1 - chunks:-1], refs[-1]
    for turn in range(chunks * per // heads):
        @pl.when(pl.program_id(0) == turn)
        def _():
            for j in range(heads):
                h = turn * heads + j
                outs[h // per][h % per] = dot(head(k, j), head(v, j), 0, 0)
    mask = causal()
    scores = [dot(head(q, j), head(k, j), 1, 1) for j in range(heads)]
    scores = [masked(s, mask) for s in scores]
    for j, s in enumerate(scores):
        attn[:, j * DH:(j + 1) * DH] = dot(s, head(v, j), 1, 0)


def attn_body(per, first, last, place, al_k, al_o, q_k, q_o, g_k, g_o, n_k, n_o, e, r, other, *refs):
    one, two, *refs = refs
    if not first:
        sq_in, cr_in = one, two
    at_k, at_o, sb_k, sb_o, *stats = refs
    square = jnp.zeros((GROUP, DH), F32) if first else sq_in[...]
    cross = jnp.zeros((GROUP, DH), F32) if first else cr_in[...]
    for j in range(per):
        kept = (e[j] + r[j]).astype(BF16)
        sb_k[j] = kept
        sb_o[j] = other[j].astype(BF16)
        for al, q, g, n, sb, at in (
            (al_k, q_k, g_k, n_k, sb_k, at_k),
            (al_o, q_o, g_o, n_o, sb_o, at_o),
        ):
            x = head(al, j) + dot(head(q, j), sb[j], 1, 0)
            at[:, j * DH:(j + 1) * DH] = x
            scaled = head(n, j).astype(F32) * head(g, j).astype(F32)
            square = square + x * x
            cross = cross + scaled * x
    if last:
        stats[0][0:1] = jnp.sum(square.T, axis=0, keepdims=True)
        stats[0][1:2] = jnp.sum(cross.T, axis=0, keepdims=True)
    else:
        stats[0][...] = square
        stats[1][...] = cross


def delta_body(per, chunks, parts, features, place, *refs):
    stats = refs[:parts]
    attn = refs[parts:parts + chunks]
    q, g, n = refs[parts + chunks:parts + chunks + 3]
    outs = refs[parts + chunks + 3:]
    total = stats[0][...]
    for s in stats[1:]:
        total = total + s[...]
    inverse = lax.rsqrt(total[0:1] / features + EPS)
    slope = inverse * inverse * inverse * (total[1:2] / features)
    inverse = jnp.broadcast_to(inverse, (DH, GROUP)).T
    slope = jnp.broadcast_to(slope, (DH, GROUP)).T
    for c in range(chunks):
        for j in range(per):
            h = c * per + j
            scaled = head(n, h).astype(F32) * head(g, h).astype(F32)
            x = (inverse * scaled - head(attn[c], j) * slope).astype(BF16)
            outs[c][:, j * DH:(j + 1) * DH] = x
            outs[chunks + c][j] = dot(head(q, h), x, 0, 0)


def column(ref, base, h):
    return ref[:, pl.ds(pl.multiple_of(base + h * DH, DH), DH)]


def query_body(per, half, chunks, place, k, v, *refs):
    qg = refs[-1]
    mask = causal()
    for turn in range(2 * chunks):
        d, sb = refs[turn], refs[2 * chunks + turn]
        base = (1 - place[0] if turn % 2 else place[0]) * half * DH + turn // 2 * per * DH
        scores = [dot(head(d, j), column(v, base, j), 1, 1) for j in range(per)]
        prior = [dot(head(d, j), sb[j], 1, 1) for j in range(per)]
        scores = [masked(s, mask) for s in scores]
        for j, s in enumerate(scores):
            qg[:, pl.ds(pl.multiple_of(base + j * DH, DH), DH)] = (
                dot(s, column(k, base, j), 1, 0) + prior[j]).astype(BF16)


def final_body(per, half, units, place, q, k, v, *refs):
    count = len(units)
    kg, vg = refs[-2], refs[-1]
    mask = causal(turned=True)
    used = count
    for turn, (c, other, terms) in enumerate(units):
        d, later_in = refs[turn], refs[used:used + terms]
        used += terms
        base = (1 - place[0] if other else place[0]) * half * DH + c * per * DH

        @pl.when(pl.program_id(0) == turn)
        def _():
            heads = range(per)
            states = [sum((t[h] for t in later_in[1:]), later_in[0][h]).astype(BF16) for h in heads]
            outer = [head(d, h) for h in heads]
            qs, ks, vs = ([column(a, base, h) for h in heads] for a in (q, k, v))
            grad = [dot(vs[h], outer[h], 1, 1) for h in heads]
            score = [dot(ks[h], qs[h], 1, 1) for h in heads]
            kg_part = [dot(vs[h], states[h], 1, 1) for h in heads]
            vg_part = [dot(ks[h], states[h], 1, 0) for h in heads]
            grad = [masked(x, mask) for x in grad]
            score = [masked(x, mask) for x in score]
            for h in heads:
                at = slice(h * DH, (h + 1) * DH)
                kg[:, at] = (dot(grad[h], qs[h], 1, 0) + kg_part[h]).astype(BF16)
                vg[:, at] = (dot(score[h], outer[h], 1, 0) + vg_part[h]).astype(BF16)


def solution(mesh):
    count = mesh.shape["seq"]
    parts = mesh.shape["head"]
    long = count // 2
    swap = [(i, i ^ 1) for i in range(count)]

    def hop(array, near, far, reverse):
        pairs = []
        for z in range(long):
            to = z + far
            if to < long and near(z):
                for y in range(2):
                    pairs.append((2 * z + y, 2 * to + y))
        if reverse:
            pairs = [(count - 1 - a, count - 1 - b) for a, b in pairs]
        return lax.ppermute(array, "seq", pairs)

    def shift(array, far, reverse):
        return hop(array, lambda at: True, far, reverse)

    def doubling(parts, reverse):
        out = []
        for part in parts:
            carry = shift(part, 1, reverse)
            far = 1
            while far < long:
                carry = carry + shift(carry, far, reverse)
                far *= 2
            out.append(carry)
        return out

    def scan(kept, sent, leads, reverse, ready, beside):
        own = [None] * len(kept)
        if long > 4 or long < 2:
            swapped = [lax.ppermute(b, "seq", swap) for b in sent]
            own = [jnp.where(leads, 0.0, r) for r in swapped]
            sums = [a + r for a, r in zip(kept, swapped)]
            sums = doubling(sums, reverse) if long > 1 else [jnp.zeros_like(a) for a in sums]
            others = [
                lax.ppermute(jnp.where(leads, e + a, e), "seq", swap) for a, e in zip(kept, sums)
            ]
            return list(zip(sums, own, others))
        chunks = len(kept)
        order = sorted((2 * stage + c, stage, c) for stage in range(long) for c in range(chunks))
        part, flight, carry, out, sends = {}, {}, {}, {}, {}
        last = ready

        def swap_after(c, *things):
            if c < chunks:
                part_sent, *_ = lax.optimization_barrier((sent[c], *things))
                flight[c] = lax.ppermute(part_sent, "seq", swap)

        swap_after(0)
        swap_after(1)
        swap_after(2)
        for _, stage, c in order:
            if (stage, c) in beside:
                last = last + [beside[stage, c](out, sends)]
            got, *_ = lax.optimization_barrier((flight[c], *last))
            if stage == 0:
                own[c] = jnp.where(leads, 0.0, got)
                part[c] = send = kept[c] + got
                swap_after(c + 3, send)
            else:
                carry[c] = got if stage == 1 else carry[c] + got
                send = carry[c] + part[c]
            if stage < long - 1:
                flight[c] = hop(send, lambda at: at == stage, 1, reverse)
            else:
                send = jnp.where(leads, carry[c] + kept[c], carry[c])
                out[c] = (carry[c], own[c], lax.ppermute(send, "seq", swap))
            last = [send]
            sends[stage, c] = send
        return [out[c] for c in range(chunks)]

    def shards(queries, keys, values, out_grad, norm_gain):
        tokens, width = queries.shape
        heads = width // DH
        half = heads // 2
        per = half // CHUNKS
        wide = half * DH
        narrow = per * DH
        at_seq = lax.axis_index("seq")
        y = at_seq % 2
        place, leads, ends = lax.optimization_barrier((y.astype(jnp.int32).reshape(1), y == 0, y == 1))
        gain = norm_gain.reshape(1, width)

        whole2 = lambda i, s: (0, 0)
        whole3 = lambda i, s: (0, 0, 0)

        def at_k(c):
            return lambda i, s: (0, s[0] * CHUNKS + c)

        def at_o(c):
            return lambda i, s: (0, (1 - s[0]) * CHUNKS + c)

        some = CHUNKS // 2
        sent = []
        for n in range(2):
            sent += call(
                functools.partial(states_body, per), place,
                [(a, (tokens, wide // 2), lambda i, s: (0, 2 * (1 - s[0]) + n), HBM) for a in (keys, values)],
                [((per, DH, DH), F32, (per, DH, DH), whole3, VMEM)] * some,
            )

        group = half // 2

        def local(which, chunks, memory, ties):
            strip = lambda i, s: (0, 2 * (1 - s[0] if which else s[0]) + i)
            return call(
                functools.partial(local_body, per, chunks, group), place,
                [(a, (tokens, group * DH), strip, memory) for a in (queries, keys, values)]
                + [(a, None, None) for a in ties],
                [((per, DH, DH), F32, (per, DH, DH), whole3, VMEM)] * chunks + [
                    ((tokens, wide), F32, (tokens, group * DH), lambda i, s: (0, i), VMEM),
                ],
                grid=(2,),
            )

        *kept, local_kept = local(0, CHUNKS, HBM, [])
        spread = 2 < long <= 4
        before = scan(kept, sent, leads, False, [local_kept], {})
        local_other, = local(1, 0, VMEM, [before[CHUNKS - 1][0]])

        block = (tokens, narrow)
        square = cross = None
        attns, priors = [], []
        for c in range(CHUNKS):
            e, r, other = before[c]
            first, last = c == 0, c == CHUNKS - 1
            ins = []
            here = lambda i, s: (0, c)
            ins += [(local_kept, block, here), (local_other, block, here)]
            for a in (queries, out_grad):
                ins += [(a, block, at_k(c)), (a, block, at_o(c))]
            ins += [(gain, (1, narrow), at_k(c)), (gain, (1, narrow), at_o(c))]
            ins += [(a, (per, DH, DH), whole3) for a in (e, r, other)]
            if first:
                ins += [(a, None, None, VMEM) for a in (keys, values)]
            else:
                ins += [(a, (GROUP, DH), whole2) for a in (square, cross)]
            outs = [(block, F32, block, whole2, VMEM)] * 2 + [((per, DH, DH), BF16, (per, DH, DH), whole3, VMEM)] * 2
            if last:
                outs += [((2, GROUP), F32, (2, GROUP), whole2)]
            else:
                outs += [((GROUP, DH), F32, (GROUP, DH), whole2)] * 2
            a_k, a_o, s_k, s_o, *stats = call(
                functools.partial(attn_body, per, first, last), place, ins, outs)
            attns.append((a_k, a_o))
            priors.append((s_k, s_o))
            if last:
                mine = stats[0]
            else:
                square, cross = stats

        sums = [mine]
        paired = parts & (parts - 1) == 0
        for step in range(1, parts):
            sums.append(lax.ppermute(
                mine, "head", [(i, i ^ step if paired else (i + step) % parts) for i in range(parts)]))

        def delta(which, first, count):
            span = count * narrow
            index = lambda i, s: (0, (1 - s[0] if which else s[0]) * (CHUNKS // count) + first // count)
            ins = [(a, (2, GROUP), whole2) for a in sums]
            ins += [(attns[c][which], block, whole2) for c in range(first, first + count)]
            ins += [(queries, (tokens, span), index), (out_grad, (tokens, span), index), (gain, (1, span), index)]
            outs = [(block, BF16, block, whole2, VMEM)] * count
            outs += [((per, DH, DH), F32, (per, DH, DH), whole3, VMEM)] * count
            result = call(
                functools.partial(delta_body, per, count, parts, float(parts * heads * DH)), place, ins, outs)
            return result[:count], result[count:]

        d_one, sent_one = delta(1, 0, some)
        d_two, sent_two = delta(1, some, some)
        d_o, sent = d_one + d_two, sent_one + sent_two
        d_k, kept = delta(0, 0, CHUNKS)

        state3 = (per, DH, DH)

        def query(tie=None):
            ins = [(a, (tokens, width), whole2) for a in (keys, values)]
            grads = [a for i in range(CHUNKS) for a in (d_k[i], d_o[i])]
            if tie is not None:
                grads[0], _ = lax.optimization_barrier((grads[0], tie))
            ins += [(a, block, whole2) for a in grads]
            ins += [(a, state3, whole3) for i in range(CHUNKS) for a in priors[i]]
            made = call(
                functools.partial(query_body, per, half, CHUNKS), place, ins,
                [((tokens, width), BF16, (tokens, width), whole2, VMEM)])
            query_made.extend(made)
            return made[0]

        def rest(units, after, made):
            states = [after[c][2:] if other else after[c][:2] for c, other in units]

            def index(i, s):
                at = 0
                for n, (c, other) in enumerate(units):
                    at = jnp.where(i == n, (1 - s[0] if other else s[0]) * CHUNKS + c, at)
                return (0, at)

            ins = [(a, (tokens, width), whole2) for a in (queries, keys, values)]
            ins += [((d_o if other else d_k)[c], block, whole2) for c, other in units]
            ins += [(a, state3, whole3) for some in states for a in some]
            aliases = {}
            if made:
                aliases = {len(ins) + 1: 0, len(ins) + 2: 1}
                ins += [(a, None, None, HBM) for a in made]
            kinds = [(c, other, len(some)) for (c, other), some in zip(units, states)]
            return call(
                functools.partial(final_body, per, half, kinds), place, ins,
                [((tokens, width), BF16, block, index, HBM)] * 2, grid=(len(units),), aliases=aliases)

        query_made = []
        made = []

        def pair(c):
            def work(out, sends):
                made[:] = rest([(c, 0), (c + 1, 0)], out, made)
                return made[0]
            return work

        beside = {
            (2, 0): lambda out, sends: query(sends[1, 1]),
            (long - 1, 2): pair(0),
        } if spread else {}
        after = scan(kept, sent, ends, True, [], beside)
        if not spread:
            query()
        for c in range(2 if spread else 0, CHUNKS, 2):
            pair(c)(after, None)
        made = rest([(0, 1), (1, 1)], after, made)
        for c in range(2, CHUNKS):
            made = rest([(c, 1)], after, made)
        return query_made[0], made[0], made[1]

    return jax.shard_map(
        shards,
        mesh=mesh,
        in_specs=(
            P("seq", "head"),
            P("seq", "head"),
            P("seq", "head"),
            P("seq", "head"),
            P("head"),
        ),
        out_specs=(P("seq", "head"), P("seq", "head"), P("seq", "head")),
        check_vma=False,
    )
```

```python
import functools

import jax
import jax.numpy as jnp
from jax import lax
from jax.experimental import pallas as pl
from jax.experimental.pallas import tpu as pltpu
from jax.sharding import PartitionSpec as P

DH = 128
GROUP = 256
CHUNKS = 4
EPS = 1e-05
F32 = jnp.float32
BF16 = jnp.bfloat16


def dot(a, b, ca, cb):
    return lax.dot_general(a, b, (((ca,), (cb,)), ((), ())), preferred_element_type=F32)


def head(ref, j):
    return ref[:, j * DH:(j + 1) * DH]


def causal(turned=False):
    rows = lax.broadcasted_iota(jnp.int32, (GROUP, GROUP), 0)
    cols = lax.broadcasted_iota(jnp.int32, (GROUP, GROUP), 1)
    return cols >= rows if turned else rows >= cols


def masked(scores, mask):
    return jnp.where(mask, scores, 0.0).astype(BF16)


HBM, VMEM = pltpu.HBM, pltpu.VMEM


def call(body, place, ins, outs, grid=(1,), aliases=None, grant=8):
    ins = [(*item, None)[:4] for item in ins]
    outs = [(*item, None)[:5] for item in outs]
    arrays = [pltpu.with_memory_space_constraint(a, m) if m else a for a, _, _, m in ins]
    return pl.pallas_call(
        body,
        grid_spec=pltpu.PrefetchScalarGridSpec(
            num_scalar_prefetch=1,
            grid=grid,
            in_specs=[pl.BlockSpec(b, m) if b else pl.BlockSpec(memory_space=pl.ANY) for _, b, m, _ in ins],
            out_specs=[pl.BlockSpec(b, m) for _, _, b, m, _ in outs],
        ),
        out_shape=[(m or jax.ShapeDtypeStruct)(s, d) for s, d, _, _, m in outs],
        input_output_aliases=aliases or {},
        compiler_params=pltpu.CompilerParams(vmem_limit_bytes=grant * 1024 * 1024),
        cost_estimate=pl.CostEstimate(flops=1024, bytes_accessed=1024, transcendentals=0),
    )(place, *arrays)


def states_body(per, place, a, b, *outs):
    for c, out in enumerate(outs):
        for j in range(per):
            h = c * per + j
            out[j] = dot(head(a, h), head(b, h), 0, 0)


def local_body(per, chunks, heads, place, q, k, v, *refs):
    outs, attn = refs[-1 - chunks:-1], refs[-1]
    for turn in range(chunks * per // heads):
        @pl.when(pl.program_id(0) == turn)
        def _():
            for j in range(heads):
                h = turn * heads + j
                outs[h // per][h % per] = dot(head(k, j), head(v, j), 0, 0)
    mask = causal()
    scores = [dot(head(q, j), head(k, j), 1, 1) for j in range(heads)]
    scores = [masked(s, mask) for s in scores]
    for j, s in enumerate(scores):
        attn[:, j * DH:(j + 1) * DH] = dot(s, head(v, j), 1, 0)


def attn_body(per, first, last, place, al_k, al_o, q_k, q_o, g_k, g_o, n_k, n_o, e, r, other, *refs):
    one, two, *refs = refs
    if not first:
        sq_in, cr_in = one, two
    at_k, at_o, sb_k, sb_o, *stats = refs
    square = jnp.zeros((GROUP, DH), F32) if first else sq_in[...]
    cross = jnp.zeros((GROUP, DH), F32) if first else cr_in[...]
    for j in range(per):
        kept = (e[j] + r[j]).astype(BF16)
        sb_k[j] = kept
        sb_o[j] = other[j].astype(BF16)
        for al, q, g, n, sb, at in (
            (al_k, q_k, g_k, n_k, sb_k, at_k),
            (al_o, q_o, g_o, n_o, sb_o, at_o),
        ):
            x = head(al, j) + dot(head(q, j), sb[j], 1, 0)
            at[:, j * DH:(j + 1) * DH] = x
            scaled = head(n, j).astype(F32) * head(g, j).astype(F32)
            square = square + x * x
            cross = cross + scaled * x
    if last:
        stats[0][0:1] = jnp.sum(square.T, axis=0, keepdims=True)
        stats[0][1:2] = jnp.sum(cross.T, axis=0, keepdims=True)
    else:
        stats[0][...] = square
        stats[1][...] = cross


def delta_body(per, chunks, parts, features, place, *refs):
    stats = refs[:parts]
    attn = refs[parts:parts + chunks]
    q, g, n = refs[parts + chunks:parts + chunks + 3]
    outs = refs[parts + chunks + 3:]
    total = stats[0][...]
    for s in stats[1:]:
        total = total + s[...]
    inverse = lax.rsqrt(total[0:1] / features + EPS)
    slope = inverse * inverse * inverse * (total[1:2] / features)
    inverse = jnp.broadcast_to(inverse, (DH, GROUP)).T
    slope = jnp.broadcast_to(slope, (DH, GROUP)).T
    for c in range(chunks):
        for j in range(per):
            h = c * per + j
            scaled = head(n, h).astype(F32) * head(g, h).astype(F32)
            x = (inverse * scaled - head(attn[c], j) * slope).astype(BF16)
            outs[c][:, j * DH:(j + 1) * DH] = x
            outs[chunks + c][j] = dot(head(q, h), x, 0, 0)


def column(ref, base, h):
    return ref[:, pl.ds(pl.multiple_of(base + h * DH, DH), DH)]


def query_body(per, half, chunks, place, k, v, *refs):
    qg = refs[-1]
    mask = causal()
    for turn in range(2 * chunks):
        d, sb = refs[turn], refs[2 * chunks + turn]
        base = (1 - place[0] if turn % 2 else place[0]) * half * DH + turn // 2 * per * DH
        scores = [dot(head(d, j), column(v, base, j), 1, 1) for j in range(per)]
        prior = [dot(head(d, j), sb[j], 1, 1) for j in range(per)]
        scores = [masked(s, mask) for s in scores]
        for j, s in enumerate(scores):
            qg[:, pl.ds(pl.multiple_of(base + j * DH, DH), DH)] = (
                dot(s, column(k, base, j), 1, 0) + prior[j]).astype(BF16)


def final_body(per, half, units, place, q, k, v, *refs):
    count = len(units)
    kg, vg = refs[-2], refs[-1]
    mask = causal(turned=True)
    used = count
    for turn, (c, other, terms) in enumerate(units):
        d, later_in = refs[turn], refs[used:used + terms]
        used += terms
        base = (1 - place[0] if other else place[0]) * half * DH + c * per * DH

        @pl.when(pl.program_id(0) == turn)
        def _():
            heads = range(per)
            states = [sum((t[h] for t in later_in[1:]), later_in[0][h]).astype(BF16) for h in heads]
            outer = [head(d, h) for h in heads]
            qs, ks, vs = ([column(a, base, h) for h in heads] for a in (q, k, v))
            grad = [dot(vs[h], outer[h], 1, 1) for h in heads]
            score = [dot(ks[h], qs[h], 1, 1) for h in heads]
            kg_part = [dot(vs[h], states[h], 1, 1) for h in heads]
            vg_part = [dot(ks[h], states[h], 1, 0) for h in heads]
            grad = [masked(x, mask) for x in grad]
            score = [masked(x, mask) for x in score]
            for h in heads:
                at = slice(h * DH, (h + 1) * DH)
                kg[:, at] = (dot(grad[h], qs[h], 1, 0) + kg_part[h]).astype(BF16)
                vg[:, at] = (dot(score[h], outer[h], 1, 0) + vg_part[h]).astype(BF16)


def solution(mesh):
    count = mesh.shape["seq"]
    parts = mesh.shape["head"]
    long = count // 2
    swap = [(i, i ^ 1) for i in range(count)]

    def hop(array, near, far, reverse):
        pairs = []
        for z in range(long):
            to = z + far
            if to < long and near(z):
                for y in range(2):
                    pairs.append((2 * z + y, 2 * to + y))
        if reverse:
            pairs = [(count - 1 - a, count - 1 - b) for a, b in pairs]
        return lax.ppermute(array, "seq", pairs)

    def shift(array, far, reverse):
        return hop(array, lambda at: True, far, reverse)

    def doubling(parts, reverse):
        out = []
        for part in parts:
            carry = shift(part, 1, reverse)
            far = 1
            while far < long:
                carry = carry + shift(carry, far, reverse)
                far *= 2
            out.append(carry)
        return out

    def scan(kept, sent, leads, reverse, ready, beside):
        own = [None] * len(kept)
        if long > 4 or long < 2:
            swapped = [lax.ppermute(b, "seq", swap) for b in sent]
            own = [jnp.where(leads, 0.0, r) for r in swapped]
            sums = [a + r for a, r in zip(kept, swapped)]
            sums = doubling(sums, reverse) if long > 1 else [jnp.zeros_like(a) for a in sums]
            others = [
                lax.ppermute(jnp.where(leads, e + a, e), "seq", swap) for a, e in zip(kept, sums)
            ]
            return list(zip(sums, own, others))
        chunks = len(kept)
        order = sorted((2 * stage + c, stage, c) for stage in range(long) for c in range(chunks))
        part, flight, carry, out, sends = {}, {}, {}, {}, {}
        last = ready

        def swap_after(c, *things):
            if c < chunks:
                part_sent, *_ = lax.optimization_barrier((sent[c], *things))
                flight[c] = lax.ppermute(part_sent, "seq", swap)

        swap_after(0)
        swap_after(1)
        swap_after(2)
        for _, stage, c in order:
            if (stage, c) in beside:
                last = last + [beside[stage, c](out, sends)]
            got, *_ = lax.optimization_barrier((flight[c], *last))
            if stage == 0:
                own[c] = jnp.where(leads, 0.0, got)
                part[c] = send = kept[c] + got
                swap_after(c + 3, send)
            else:
                carry[c] = got if stage == 1 else carry[c] + got
                send = carry[c] + part[c]
            if stage < long - 1:
                flight[c] = hop(send, lambda at: at == stage, 1, reverse)
            else:
                send = jnp.where(leads, carry[c] + kept[c], carry[c])
                out[c] = (carry[c], own[c], lax.ppermute(send, "seq", swap))
            last = [send]
            sends[stage, c] = send
        return [out[c] for c in range(chunks)]

    def shards(queries, keys, values, out_grad, norm_gain):
        tokens, width = queries.shape
        heads = width // DH
        half = heads // 2
        per = half // CHUNKS
        wide = half * DH
        narrow = per * DH
        at_seq = lax.axis_index("seq")
        y = at_seq % 2
        place, leads, ends = lax.optimization_barrier((y.astype(jnp.int32).reshape(1), y == 0, y == 1))
        gain = norm_gain.reshape(1, width)

        whole2 = lambda i, s: (0, 0)
        whole3 = lambda i, s: (0, 0, 0)

        def at_k(c):
            return lambda i, s: (0, s[0] * CHUNKS + c)

        def at_o(c):
            return lambda i, s: (0, (1 - s[0]) * CHUNKS + c)

        some = CHUNKS // 2
        sent = []
        for n in range(2):
            sent += call(
                functools.partial(states_body, per), place,
                [(a, (tokens, wide // 2), lambda i, s: (0, 2 * (1 - s[0]) + n), HBM) for a in (keys, values)],
                [((per, DH, DH), F32, (per, DH, DH), whole3, VMEM)] * some,
            )

        group = half // 2

        def local(which, chunks, memory, ties):
            strip = lambda i, s: (0, 2 * (1 - s[0] if which else s[0]) + i)
            return call(
                functools.partial(local_body, per, chunks, group), place,
                [(a, (tokens, group * DH), strip, memory) for a in (queries, keys, values)]
                + [(a, None, None) for a in ties],
                [((per, DH, DH), F32, (per, DH, DH), whole3, VMEM)] * chunks + [
                    ((tokens, wide), F32, (tokens, group * DH), lambda i, s: (0, i), VMEM),
                ],
                grid=(2,),
            )

        *kept, local_kept = local(0, CHUNKS, HBM, [])
        spread = 2 < long <= 4
        before = scan(kept, sent, leads, False, [local_kept], {})
        local_other, = local(1, 0, VMEM, [before[CHUNKS - 1][0]])

        block = (tokens, narrow)
        square = cross = None
        attns, priors = [], []
        for c in range(CHUNKS):
            e, r, other = before[c]
            first, last = c == 0, c == CHUNKS - 1
            ins = []
            here = lambda i, s: (0, c)
            ins += [(local_kept, block, here), (local_other, block, here)]
            for a in (queries, out_grad):
                ins += [(a, block, at_k(c)), (a, block, at_o(c))]
            ins += [(gain, (1, narrow), at_k(c)), (gain, (1, narrow), at_o(c))]
            ins += [(a, (per, DH, DH), whole3) for a in (e, r, other)]
            if first:
                ins += [(a, None, None, VMEM) for a in (keys, values)]
            else:
                ins += [(a, (GROUP, DH), whole2) for a in (square, cross)]
            outs = [(block, F32, block, whole2, VMEM)] * 2 + [((per, DH, DH), BF16, (per, DH, DH), whole3, VMEM)] * 2
            if last:
                outs += [((2, GROUP), F32, (2, GROUP), whole2)]
            else:
                outs += [((GROUP, DH), F32, (GROUP, DH), whole2)] * 2
            a_k, a_o, s_k, s_o, *stats = call(
                functools.partial(attn_body, per, first, last), place, ins, outs)
            attns.append((a_k, a_o))
            priors.append((s_k, s_o))
            if last:
                mine = stats[0]
            else:
                square, cross = stats

        sums = [mine]
        paired = parts & (parts - 1) == 0
        for step in range(1, parts):
            sums.append(lax.ppermute(
                mine, "head", [(i, i ^ step if paired else (i + step) % parts) for i in range(parts)]))

        def delta(which, first, count):
            span = count * narrow
            index = lambda i, s: (0, (1 - s[0] if which else s[0]) * (CHUNKS // count) + first // count)
            ins = [(a, (2, GROUP), whole2) for a in sums]
            ins += [(attns[c][which], block, whole2) for c in range(first, first + count)]
            ins += [(queries, (tokens, span), index), (out_grad, (tokens, span), index), (gain, (1, span), index)]
            outs = [(block, BF16, block, whole2, VMEM)] * count
            outs += [((per, DH, DH), F32, (per, DH, DH), whole3, VMEM)] * count
            result = call(
                functools.partial(delta_body, per, count, parts, float(parts * heads * DH)), place, ins, outs)
            return result[:count], result[count:]

        d_one, sent_one = delta(1, 0, some)
        d_two, sent_two = delta(1, some, some)
        d_o, sent = d_one + d_two, sent_one + sent_two
        d_k, kept = delta(0, 0, CHUNKS)

        state3 = (per, DH, DH)

        def query(tie=None):
            ins = [(a, (tokens, width), whole2) for a in (keys, values)]
            grads = [a for i in range(CHUNKS) for a in (d_k[i], d_o[i])]
            if tie is not None:
                grads[0], _ = lax.optimization_barrier((grads[0], tie))
            ins += [(a, block, whole2) for a in grads]
            ins += [(a, state3, whole3) for i in range(CHUNKS) for a in priors[i]]
            made = call(
                functools.partial(query_body, per, half, CHUNKS), place, ins,
                [((tokens, width), BF16, (tokens, width), whole2, VMEM)])
            query_made.extend(made)
            return made[0]

        def rest(units, after, made):
            states = [after[c][2:] if other else after[c][:2] for c, other in units]

            def index(i, s):
                at = 0
                for n, (c, other) in enumerate(units):
                    at = jnp.where(i == n, (1 - s[0] if other else s[0]) * CHUNKS + c, at)
                return (0, at)

            ins = [(a, (tokens, width), whole2) for a in (queries, keys, values)]
            ins += [((d_o if other else d_k)[c], block, whole2) for c, other in units]
            ins += [(a, state3, whole3) for some in states for a in some]
            aliases = {}
            if made:
                aliases = {len(ins) + 1: 0, len(ins) + 2: 1}
                ins += [(a, None, None, HBM) for a in made]
            kinds = [(c, other, len(some)) for (c, other), some in zip(units, states)]
            return call(
                functools.partial(final_body, per, half, kinds), place, ins,
                [((tokens, width), BF16, block, index, HBM)] * 2, grid=(len(units),), aliases=aliases)

        query_made = []
        made = []

        def kept_units(first, count=1):
            def work(out, sends):
                made[:] = rest([(c, 0) for c in range(first, first + count)], out, made)
                return made[0]
            return work

        beside = {
            (2, 0): lambda out, sends: query(sends[1, 2]),
            (long - 1, 2): kept_units(0, 2),
            (long - 1, 3): kept_units(2, 1),
        } if spread else {}
        after = scan(kept, sent, ends, True, [], beside)
        if not spread:
            query()
        if not spread:
            kept_units(0, 3)(after, None)
        kept_units(3, 1)(after, None)
        made = rest([(0, 1), (1, 1)], after, made)
        for c in range(2, CHUNKS):
            made = rest([(c, 1)], after, made)
        return query_made[0], made[0], made[1]

    return jax.shard_map(
        shards,
        mesh=mesh,
        in_specs=(
            P("seq", "head"),
            P("seq", "head"),
            P("seq", "head"),
            P("seq", "head"),
            P("head"),
        ),
        out_specs=(P("seq", "head"), P("seq", "head"), P("seq", "head")),
        check_vma=False,
    )
```

```python
import functools

import jax
import jax.numpy as jnp
from jax import lax
from jax.experimental import pallas as pl
from jax.experimental.pallas import tpu as pltpu
from jax.sharding import PartitionSpec as P

DH = 128
GROUP = 256
CHUNKS = 4
EPS = 1e-05
F32 = jnp.float32
BF16 = jnp.bfloat16


def dot(a, b, ca, cb):
    return lax.dot_general(a, b, (((ca,), (cb,)), ((), ())), preferred_element_type=F32)


def head(ref, j):
    return ref[:, j * DH:(j + 1) * DH]


def causal(turned=False):
    rows = lax.broadcasted_iota(jnp.int32, (GROUP, GROUP), 0)
    cols = lax.broadcasted_iota(jnp.int32, (GROUP, GROUP), 1)
    return cols >= rows if turned else rows >= cols


def masked(scores, mask):
    return jnp.where(mask, scores, 0.0).astype(BF16)


HBM, VMEM = pltpu.HBM, pltpu.VMEM


def call(body, place, ins, outs, grid=(1,), aliases=None, grant=8):
    ins = [(*item, None)[:4] for item in ins]
    outs = [(*item, None)[:5] for item in outs]
    arrays = [pltpu.with_memory_space_constraint(a, m) if m else a for a, _, _, m in ins]
    return pl.pallas_call(
        body,
        grid_spec=pltpu.PrefetchScalarGridSpec(
            num_scalar_prefetch=1,
            grid=grid,
            in_specs=[pl.BlockSpec(b, m) if b else pl.BlockSpec(memory_space=pl.ANY) for _, b, m, _ in ins],
            out_specs=[pl.BlockSpec(b, m) for _, _, b, m, _ in outs],
        ),
        out_shape=[(m or jax.ShapeDtypeStruct)(s, d) for s, d, _, _, m in outs],
        input_output_aliases=aliases or {},
        compiler_params=pltpu.CompilerParams(vmem_limit_bytes=grant * 1024 * 1024),
        cost_estimate=pl.CostEstimate(flops=1024, bytes_accessed=1024, transcendentals=0),
    )(place, *arrays)


def states_body(per, place, a, b, *outs):
    for c, out in enumerate(outs):
        for j in range(per):
            h = c * per + j
            out[j] = dot(head(a, h), head(b, h), 0, 0)


def local_body(per, chunks, heads, place, q, k, v, *refs):
    outs, attn = refs[-1 - chunks:-1], refs[-1]
    for turn in range(chunks * per // heads):
        @pl.when(pl.program_id(0) == turn)
        def _():
            for j in range(heads):
                h = turn * heads + j
                outs[h // per][h % per] = dot(head(k, j), head(v, j), 0, 0)
    mask = causal()
    scores = [dot(head(q, j), head(k, j), 1, 1) for j in range(heads)]
    scores = [masked(s, mask) for s in scores]
    for j, s in enumerate(scores):
        attn[:, j * DH:(j + 1) * DH] = dot(s, head(v, j), 1, 0)


def attn_body(per, first, last, place, al_k, al_o, q_k, q_o, g_k, g_o, n_k, n_o, e, r, other, *refs):
    one, two, *refs = refs
    if not first:
        sq_in, cr_in = one, two
    at_k, at_o, sb_k, sb_o, *stats = refs
    square = jnp.zeros((GROUP, DH), F32) if first else sq_in[...]
    cross = jnp.zeros((GROUP, DH), F32) if first else cr_in[...]
    for j in range(per):
        kept = (e[j] + r[j]).astype(BF16)
        sb_k[j] = kept
        sb_o[j] = other[j].astype(BF16)
        for al, q, g, n, sb, at in (
            (al_k, q_k, g_k, n_k, sb_k, at_k),
            (al_o, q_o, g_o, n_o, sb_o, at_o),
        ):
            x = head(al, j) + dot(head(q, j), sb[j], 1, 0)
            at[:, j * DH:(j + 1) * DH] = x
            scaled = head(n, j).astype(F32) * head(g, j).astype(F32)
            square = square + x * x
            cross = cross + scaled * x
    if last:
        stats[0][0:1] = jnp.sum(square.T, axis=0, keepdims=True)
        stats[0][1:2] = jnp.sum(cross.T, axis=0, keepdims=True)
    else:
        stats[0][...] = square
        stats[1][...] = cross


def delta_body(per, chunks, parts, features, place, *refs):
    stats = refs[:parts]
    attn = refs[parts:parts + chunks]
    q, g, n = refs[parts + chunks:parts + chunks + 3]
    outs = refs[parts + chunks + 3:]
    total = stats[0][...]
    for s in stats[1:]:
        total = total + s[...]
    inverse = lax.rsqrt(total[0:1] / features + EPS)
    slope = inverse * inverse * inverse * (total[1:2] / features)
    inverse = jnp.broadcast_to(inverse, (DH, GROUP)).T
    slope = jnp.broadcast_to(slope, (DH, GROUP)).T
    for c in range(chunks):
        for j in range(per):
            h = c * per + j
            scaled = head(n, h).astype(F32) * head(g, h).astype(F32)
            x = (inverse * scaled - head(attn[c], j) * slope).astype(BF16)
            outs[c][:, j * DH:(j + 1) * DH] = x
            outs[chunks + c][j] = dot(head(q, h), x, 0, 0)


def column(ref, base, h):
    return ref[:, pl.ds(pl.multiple_of(base + h * DH, DH), DH)]


def query_body(per, half, chunks, place, k, v, *refs):
    qg = refs[-1]
    mask = causal()
    for turn in range(2 * chunks):
        d, sb = refs[turn], refs[2 * chunks + turn]
        base = (1 - place[0] if turn % 2 else place[0]) * half * DH + turn // 2 * per * DH
        scores = [dot(head(d, j), column(v, base, j), 1, 1) for j in range(per)]
        prior = [dot(head(d, j), sb[j], 1, 1) for j in range(per)]
        scores = [masked(s, mask) for s in scores]
        for j, s in enumerate(scores):
            qg[:, pl.ds(pl.multiple_of(base + j * DH, DH), DH)] = (
                dot(s, column(k, base, j), 1, 0) + prior[j]).astype(BF16)


def final_body(per, half, units, place, q, k, v, *refs):
    count = len(units)
    kg, vg = refs[-2], refs[-1]
    mask = causal(turned=True)
    used = count
    for turn, (c, other, terms) in enumerate(units):
        d, later_in = refs[turn], refs[used:used + terms]
        used += terms
        base = (1 - place[0] if other else place[0]) * half * DH + c * per * DH

        @pl.when(pl.program_id(0) == turn)
        def _():
            heads = range(per)
            states = [sum((t[h] for t in later_in[1:]), later_in[0][h]).astype(BF16) for h in heads]
            outer = [head(d, h) for h in heads]
            qs, ks, vs = ([column(a, base, h) for h in heads] for a in (q, k, v))
            grad = [dot(vs[h], outer[h], 1, 1) for h in heads]
            score = [dot(ks[h], qs[h], 1, 1) for h in heads]
            kg_part = [dot(vs[h], states[h], 1, 1) for h in heads]
            vg_part = [dot(ks[h], states[h], 1, 0) for h in heads]
            grad = [masked(x, mask) for x in grad]
            score = [masked(x, mask) for x in score]
            for h in heads:
                at = slice(h * DH, (h + 1) * DH)
                kg[:, at] = (dot(grad[h], qs[h], 1, 0) + kg_part[h]).astype(BF16)
                vg[:, at] = (dot(score[h], outer[h], 1, 0) + vg_part[h]).astype(BF16)


def solution(mesh):
    count = mesh.shape["seq"]
    parts = mesh.shape["head"]
    long = count // 2
    swap = [(i, i ^ 1) for i in range(count)]

    def hop(array, near, far, reverse):
        pairs = []
        for z in range(long):
            to = z + far
            if to < long and near(z):
                for y in range(2):
                    pairs.append((2 * z + y, 2 * to + y))
        if reverse:
            pairs = [(count - 1 - a, count - 1 - b) for a, b in pairs]
        return lax.ppermute(array, "seq", pairs)

    def shift(array, far, reverse):
        return hop(array, lambda at: True, far, reverse)

    def doubling(parts, reverse):
        out = []
        for part in parts:
            carry = shift(part, 1, reverse)
            far = 1
            while far < long:
                carry = carry + shift(carry, far, reverse)
                far *= 2
            out.append(carry)
        return out

    def scan(kept, sent, leads, reverse, ready, beside):
        own = [None] * len(kept)
        if long > 4 or long < 2:
            swapped = [lax.ppermute(b, "seq", swap) for b in sent]
            own = [jnp.where(leads, 0.0, r) for r in swapped]
            sums = [a + r for a, r in zip(kept, swapped)]
            sums = doubling(sums, reverse) if long > 1 else [jnp.zeros_like(a) for a in sums]
            others = [
                lax.ppermute(jnp.where(leads, e + a, e), "seq", swap) for a, e in zip(kept, sums)
            ]
            return list(zip(sums, own, others))
        chunks = len(kept)
        order = sorted((2 * stage + c, stage, c) for stage in range(long) for c in range(chunks))
        part, flight, carry, out, sends = {}, {}, {}, {}, {}
        last = ready

        def swap_after(c, *things):
            if c < chunks:
                part_sent, *_ = lax.optimization_barrier((sent[c], *things))
                flight[c] = lax.ppermute(part_sent, "seq", swap)

        swap_after(0)
        swap_after(1)
        swap_after(2)
        for _, stage, c in order:
            if (stage, c) in beside:
                last = last + [beside[stage, c](out, sends)]
            got, *_ = lax.optimization_barrier((flight[c], *last))
            if stage == 0:
                own[c] = jnp.where(leads, 0.0, got)
                part[c] = send = kept[c] + got
                swap_after(c + 3, send)
            else:
                carry[c] = got if stage == 1 else carry[c] + got
                send = carry[c] + part[c]
            if stage < long - 1:
                flight[c] = hop(send, lambda at: at == stage, 1, reverse)
            else:
                send = jnp.where(leads, carry[c] + kept[c], carry[c])
                out[c] = (carry[c], own[c], lax.ppermute(send, "seq", swap))
            last = [send]
            sends[stage, c] = send
        return [out[c] for c in range(chunks)]

    def shards(queries, keys, values, out_grad, norm_gain):
        tokens, width = queries.shape
        heads = width // DH
        half = heads // 2
        per = half // CHUNKS
        wide = half * DH
        narrow = per * DH
        at_seq = lax.axis_index("seq")
        y = at_seq % 2
        place, leads, ends = lax.optimization_barrier((y.astype(jnp.int32).reshape(1), y == 0, y == 1))
        gain = norm_gain.reshape(1, width)

        whole2 = lambda i, s: (0, 0)
        whole3 = lambda i, s: (0, 0, 0)

        def at_k(c):
            return lambda i, s: (0, s[0] * CHUNKS + c)

        def at_o(c):
            return lambda i, s: (0, (1 - s[0]) * CHUNKS + c)

        some = CHUNKS // 2
        sent = []
        for n in range(2):
            sent += call(
                functools.partial(states_body, per), place,
                [(a, (tokens, wide // 2), lambda i, s: (0, 2 * (1 - s[0]) + n), HBM) for a in (keys, values)],
                [((per, DH, DH), F32, (per, DH, DH), whole3, VMEM)] * some,
            )

        group = half // 2

        def local(which, chunks, memory, ties):
            strip = lambda i, s: (0, 2 * (1 - s[0] if which else s[0]) + i)
            return call(
                functools.partial(local_body, per, chunks, group), place,
                [(a, (tokens, group * DH), strip, memory) for a in (queries, keys, values)]
                + [(a, None, None) for a in ties],
                [((per, DH, DH), F32, (per, DH, DH), whole3, VMEM)] * chunks + [
                    ((tokens, wide), F32, (tokens, group * DH), lambda i, s: (0, i), VMEM),
                ],
                grid=(2,),
            )

        *kept, local_kept = local(0, CHUNKS, HBM, [])
        spread = 2 < long <= 4
        before = scan(kept, sent, leads, False, [local_kept], {})
        local_other, = local(1, 0, VMEM, [before[CHUNKS - 1][0]])

        block = (tokens, narrow)
        square = cross = None
        attns, priors = [], []
        for c in range(CHUNKS):
            e, r, other = before[c]
            first, last = c == 0, c == CHUNKS - 1
            ins = []
            here = lambda i, s: (0, c)
            ins += [(local_kept, block, here), (local_other, block, here)]
            for a in (queries, out_grad):
                ins += [(a, block, at_k(c)), (a, block, at_o(c))]
            ins += [(gain, (1, narrow), at_k(c)), (gain, (1, narrow), at_o(c))]
            ins += [(a, (per, DH, DH), whole3) for a in (e, r, other)]
            if first:
                ins += [(a, None, None, VMEM) for a in (keys, values)]
            else:
                ins += [(a, (GROUP, DH), whole2) for a in (square, cross)]
            outs = [(block, F32, block, whole2, VMEM)] * 2 + [((per, DH, DH), BF16, (per, DH, DH), whole3, VMEM)] * 2
            if last:
                outs += [((2, GROUP), F32, (2, GROUP), whole2)]
            else:
                outs += [((GROUP, DH), F32, (GROUP, DH), whole2)] * 2
            a_k, a_o, s_k, s_o, *stats = call(
                functools.partial(attn_body, per, first, last), place, ins, outs)
            attns.append((a_k, a_o))
            priors.append((s_k, s_o))
            if last:
                mine = stats[0]
            else:
                square, cross = stats

        sums = [mine]
        paired = parts & (parts - 1) == 0
        for step in range(1, parts):
            sums.append(lax.ppermute(
                mine, "head", [(i, i ^ step if paired else (i + step) % parts) for i in range(parts)]))

        def delta(which, first, count):
            span = count * narrow
            index = lambda i, s: (0, (1 - s[0] if which else s[0]) * (CHUNKS // count) + first // count)
            ins = [(a, (2, GROUP), whole2) for a in sums]
            ins += [(attns[c][which], block, whole2) for c in range(first, first + count)]
            ins += [(queries, (tokens, span), index), (out_grad, (tokens, span), index), (gain, (1, span), index)]
            outs = [(block, BF16, block, whole2, VMEM)] * count
            outs += [((per, DH, DH), F32, (per, DH, DH), whole3, VMEM)] * count
            result = call(
                functools.partial(delta_body, per, count, parts, float(parts * heads * DH)), place, ins, outs)
            return result[:count], result[count:]

        d_one, sent_one = delta(1, 0, some)
        d_two, sent_two = delta(1, some, some)
        d_o, sent = d_one + d_two, sent_one + sent_two
        d_k, kept = delta(0, 0, CHUNKS)

        state3 = (per, DH, DH)

        def query(tie=None):
            ins = [(a, (tokens, width), whole2) for a in (keys, values)]
            grads = [a for i in range(CHUNKS) for a in (d_k[i], d_o[i])]
            if tie is not None:
                grads[0], _ = lax.optimization_barrier((grads[0], tie))
            ins += [(a, block, whole2) for a in grads]
            ins += [(a, state3, whole3) for i in range(CHUNKS) for a in priors[i]]
            made = call(
                functools.partial(query_body, per, half, CHUNKS), place, ins,
                [((tokens, width), BF16, (tokens, width), whole2, VMEM)])
            query_made.extend(made)
            return made[0]

        def rest(units, after, made):
            states = [after[c][2:] if other else after[c][:2] for c, other in units]

            def index(i, s):
                at = 0
                for n, (c, other) in enumerate(units):
                    at = jnp.where(i == n, (1 - s[0] if other else s[0]) * CHUNKS + c, at)
                return (0, at)

            ins = [(a, (tokens, width), whole2) for a in (queries, keys, values)]
            ins += [((d_o if other else d_k)[c], block, whole2) for c, other in units]
            ins += [(a, state3, whole3) for some in states for a in some]
            aliases = {}
            if made:
                aliases = {len(ins) + 1: 0, len(ins) + 2: 1}
                ins += [(a, None, None, HBM) for a in made]
            kinds = [(c, other, len(some)) for (c, other), some in zip(units, states)]
            return call(
                functools.partial(final_body, per, half, kinds), place, ins,
                [((tokens, width), BF16, block, index, HBM)] * 2, grid=(len(units),), aliases=aliases)

        query_made = []
        made = []

        def kept_units(first, count=1):
            def work(out, sends):
                made[:] = rest([(c, 0) for c in range(first, first + count)], out, made)
                return made[0]
            return work

        beside = {
            (2, 0): lambda out, sends: query(sends[1, 2]),
            (long - 1, 1): kept_units(0, 1),
            (long - 1, 2): kept_units(1, 1),
        } if spread else {}
        after = scan(kept, sent, ends, True, [], beside)
        if not spread:
            query()
        if not spread:
            kept_units(0, CHUNKS - 2)(after, None)
        kept_units(2, 2)(after, None)
        made = rest([(0, 1), (1, 1)], after, made)
        for c in range(2, CHUNKS):
            made = rest([(c, 1)], after, made)
        return query_made[0], made[0], made[1]

    return jax.shard_map(
        shards,
        mesh=mesh,
        in_specs=(
            P("seq", "head"),
            P("seq", "head"),
            P("seq", "head"),
            P("seq", "head"),
            P("head"),
        ),
        out_specs=(P("seq", "head"), P("seq", "head"), P("seq", "head")),
        check_vma=False,
    )
```
